32 devices in a mesh: dp: 8 (over z, x), section: 4 (over y, core).
Axes of the slice: x: 2, y: 2, z: 4, core: 2. Of those that a mesh axis runs over, the one named last changes fastest.
Arguments:
- feeds: bfloat16 [16384, 768], P(('dp', 'section')), may hold values from -6 to 6
- text_lengths: int32 [32], P('dp'), may hold values from 0 to 59, as said below
- norm_gains: bfloat16 [4, 2, 384], P('section'), may hold values from 0.099609375 to 1.8984375
- qkv_weight: bfloat16 [4, 384, 2304], P('section'), may hold values from -0.21875 to 0.21875
- out_weight: bfloat16 [4, 384, 768], P('section'), may hold values from -0.625 to 0.625
- expert_in: bfloat16 [4, 2, 384, 3072], P('section'), may hold values from -0.21875 to 0.21875
- expert_out: bfloat16 [4, 2, 1536, 768], P('section'), may hold values from -0.109375 to 0.109375
Outputs:
- ends: float32 [16384, 768], P(('dp', 'section'))
- gain_grads: float32 [4, 2, 384], P('section', None, 'dp')
- qkv_grads: float32 [4, 384, 2304], P('section', None, 'dp')
- out_grads: float32 [4, 384, 768], P('section', None, 'dp')
- expert_in_grads: float32 [4, 2, 384, 3072], P('section', None, None, 'dp')
- expert_out_grads: float32 [4, 2, 1536, 768], P('section', None, None, 'dp')
The draws below stay inside these ranges and needn't reach their ends.
Inputs may be any that keep to these rules, and one draw needn't show every extreme that they name: `text_lengths`: 0 marks an image item of 197 rows; k > 0 a pair of 197 image rows followed by k text rows; the rest of the slot is padding. Some item is an image and some has 59 text rows.
All inputs are finite; a program needn't handle non-finite values.
Results may differ from the reference program's by a relative error of at most 0.03.
Values may be sent and summed in bfloat16 or wider, within the bound.
No kernel may reach another device: no remote copies, remote signals or barrier semaphores. Data moves between devices by JAX's collectives and lax.ppermute only.
A program may use at most 192 MiB of HBM per device.

```python
from functools import partial
import jax
import jax.numpy as jnp
from jax import lax

D = 768
HEADS = 12
FF = 3072
HEAD_DIM = 64
IMAGE_ROWS = 197
ROWS = 256
TEXT_MAX = 59
MB = 2
ITEMS = 32
TOKENS = 16384
N_DP = 8
N_SECTION = 4


def draw_text_lengths(key, part):
    key = jax.random.fold_in(key, 11)
    length_key, kind_key, spot_key = jax.random.split(key, 3)
    lengths = jax.random.randint(length_key, (ITEMS,), 1, TEXT_MAX + 1)
    images = jax.random.randint(kind_key, (ITEMS,), 0, 3) == 0
    values = jnp.where(images, 0, lengths)
    spots = jax.random.permutation(spot_key, ITEMS)
    values = values.at[spots[0]].set(TEXT_MAX)
    values = values.at[spots[1]].set(0)
    return values.astype(jnp.int32)


def steps_of(stream_key, extent, cuts, low, top_value):
    loudness = 1.0
    for dim, shards_of in cuts:
        heights = jax.random.uniform(jax.random.fold_in(jax.random.fold_in(stream_key, 6), dim), (shards_of,), jnp.float32, low / len(cuts), top_value / len(cuts))
        loudness = loudness * jnp.repeat(jnp.exp(heights), extent[dim] // shards_of).reshape((-1,) + (1,) * (len(extent) - 1 - dim))
    return loudness


def bell_draw(key, shape, deviation, most, shards=(), held_as=jnp.bfloat16):
    result = jax.random.normal(key, shape, jnp.float32) * deviation
    if len(shards) > 0:
        result = steps_of(key, shape, shards, -0.22, 0.18) * result
    return jnp.clip(result, min=-most, max=most).astype(held_as)


def setup_inputs(seed: int = 0) -> dict:
    streams_of = jax.random.split(jax.random.key(seed), 8)
    return {
        "feeds": bell_draw(streams_of[0], (TOKENS, D), 1.0, 6.0, ((0, 32),)),
        "text_lengths": draw_text_lengths(jax.random.fold_in(streams_of[7], 71), 0),
        "norm_gains": jnp.clip(1.0 + 0.18 * jax.random.normal(streams_of[2], (N_SECTION, 2, D // 2), jnp.float32), 0.099609375, 1.8984375).astype(jnp.bfloat16),
        "qkv_weight": bell_draw(streams_of[3], (N_SECTION, D // 2, 3 * D), D ** -0.5, 0.21875, ((0, 4),)),
        "out_weight": bell_draw(streams_of[4], (N_SECTION, D // 2, D), (D // 8) ** -0.5, 0.625, ((0, 4),)),
        "expert_in": bell_draw(streams_of[5], (N_SECTION, 2, D // 2, FF), D ** -0.5, 0.21875, ((0, 4),)),
        "expert_out": bell_draw(streams_of[6], (N_SECTION, 2, FF // 2, D), FF ** -0.5, 0.109375, ((0, 4),)),
    }


EPSILON = 1e-05
MASKED = -1e+30
HIGHEST = lax.Precision.HIGHEST

@jax.custom_vjp
def low(v):
    return lax.optimization_barrier(v.astype(jnp.bfloat16)).astype(jnp.float32)

@jax.custom_vjp
def low_back(v):
    return v

def low_keep(v):
    return (low(v), None)

def low_pass(kept, grad):
    return (grad,)

def back_keep(v):
    return (v, None)

def back_low(kept, grad):
    return (low(grad),)
low.defvjp(low_keep, low_pass)
low_back.defvjp(back_keep, back_low)

def norm_apply(hidden, gain_row):
    centred = hidden - lax.optimization_barrier(jnp.mean(hidden, axis=-1, keepdims=True))
    spread = lax.optimization_barrier(jnp.mean(centred * centred, axis=-1, keepdims=True))
    return centred * lax.rsqrt(spread + EPSILON) * gain_row

def gelu_exact(values):
    return jax.nn.gelu(values, approximate=False)

def layer(hidden, live_keys, first_expert, second_expert, params):
    norm_gain, qkv_mat, proj_mat, in_stack, back_stack = params
    row_count = hidden.shape[0]
    normed = low(norm_apply(hidden, norm_gain[0]))
    packed = low_back(low(jnp.dot(normed, qkv_mat, precision=HIGHEST, preferred_element_type=jnp.float32)))
    head_split = packed.reshape(row_count, 3, HEADS, HEAD_DIM)
    scores = jnp.einsum('qhd,khd->hqk', head_split[:, 0], head_split[:, 1], precision=HIGHEST) * HEAD_DIM ** (-0.5)
    scores = low_back(jnp.where(live_keys[None, None, :], scores, MASKED))
    shifted = jnp.exp(scores - lax.optimization_barrier(jnp.max(scores, axis=-1, keepdims=True)))
    attn_probs = low(shifted / lax.optimization_barrier(jnp.sum(shifted, axis=-1, keepdims=True)))
    context = jnp.einsum('hqk,khd->qhd', attn_probs, head_split[:, 2], precision=HIGHEST)
    context = low_back(low(context.reshape(row_count, HEADS * HEAD_DIM)))
    mixed_rows = hidden + low_back(jnp.dot(context, proj_mat, precision=HIGHEST, preferred_element_type=jnp.float32))
    second = low(norm_apply(mixed_rows, norm_gain[1]))
    pieces = []
    for start_row, stop_row, expert in ((0, IMAGE_ROWS, first_expert), (IMAGE_ROWS, row_count, second_expert)):
        inner_act = low_back(jnp.dot(second[start_row:stop_row], in_stack[expert], precision=HIGHEST, preferred_element_type=jnp.float32))
        active = low(gelu_exact(inner_act))
        pieces.append(low_back(jnp.dot(active, back_stack[expert], precision=HIGHEST, preferred_element_type=jnp.float32)))
    return mixed_rows + jnp.concatenate(pieces, axis=0)

def build(gains_all, qkv_all, proj_all, in_all, back_all, layer_num):
    low_block = 2 * layer_num
    high_block = 2 * layer_num + 1
    return (jnp.concatenate([gains_all[low_block], gains_all[high_block]], axis=-1), jnp.concatenate([qkv_all[low_block], qkv_all[high_block]], axis=0), jnp.concatenate([proj_all[low_block], proj_all[high_block]], axis=0), jnp.concatenate([in_all[low_block], in_all[high_block]], axis=1), jnp.concatenate([back_all[low_block], back_all[high_block]], axis=1))

def group_pass(group, lower_set, upper_set):
    group_inputs, group_live, group_kinds = group

    def lower_item(hidden, live_keys):
        return layer(hidden, live_keys, 0, 1, lower_set)

    def upper_item(hidden, live_keys, kind_value):
        return layer(hidden, live_keys, kind_value, kind_value, upper_set)
    first_out = jax.vmap(lower_item)(group_inputs, group_live)
    passed = low_back(low(first_out))
    return jax.vmap(upper_item)(passed, group_live, group_kinds)

def arrange(grads):
    gain_grad, qkv_grad, proj_grad, in_grad, back_grad = grads
    return (gain_grad.reshape(2, 2, D // 2).transpose(1, 0, 2), qkv_grad.reshape(2, D // 2, 3 * D), proj_grad.reshape(2, D // 2, D), in_grad.reshape(2, 2, D // 2, FF).transpose(1, 0, 2, 3), back_grad.reshape(2, 2, FF // 2, D).transpose(1, 0, 2, 3))

def reference(feeds, text_lengths, norm_gains, qkv_weight, out_weight, expert_in, expert_out):
    gains_all = norm_gains.astype(jnp.float32)
    qkv_all = qkv_weight.astype(jnp.float32)
    proj_all = out_weight.astype(jnp.float32)
    in_all = expert_in.astype(jnp.float32)
    back_all = expert_out.astype(jnp.float32)
    blocks = feeds.astype(jnp.float32).reshape(N_DP, N_SECTION, MB, ROWS, D)
    inputs = blocks[:, 0:2].reshape(N_DP, 2 * MB, ROWS, D)
    cotangent = blocks[:, 2:4].reshape(N_DP, 2 * MB, ROWS, D)
    lengths = text_lengths.astype(jnp.int32).reshape(N_DP, 2 * MB)
    positions = jnp.arange(ROWS, dtype=jnp.int32)
    live = positions[None, None, :] < (IMAGE_ROWS + lengths)[:, :, None]
    kinds = (lengths > 0).astype(jnp.int32)
    lower_params = build(gains_all, qkv_all, proj_all, in_all, back_all, 0)
    upper_params = build(gains_all, qkv_all, proj_all, in_all, back_all, 1)

    def forward(inputs_all, lower_set, upper_set):
        stepper = jax.checkpoint(partial(group_pass, lower_set=lower_set, upper_set=upper_set))
        return lax.map(stepper, (inputs_all, live, kinds))
    outputs, back_fn = jax.vjp(forward, inputs, lower_params, upper_params)
    grad_inputs, lower_grads, upper_grads = back_fn(jnp.where(live[..., None], cotangent, 0.0))
    ends = jnp.concatenate([grad_inputs.reshape(N_DP, 2, MB, ROWS, D), outputs.reshape(N_DP, 2, MB, ROWS, D)], axis=1)
    ends = ends.reshape(N_DP * N_SECTION * MB * ROWS, D)
    lower_out = arrange(lower_grads)
    upper_out = arrange(upper_grads)
    merged = [jnp.concatenate([lower_part, upper_part], axis=0) for lower_part, upper_part in zip(lower_out, upper_out)]
    return (ends, merged[0], merged[1], merged[2], merged[3], merged[4])
```

```python
import functools

import jax
import jax.numpy as jnp
from jax import lax
from jax.experimental import pallas as pl
from jax.experimental.pallas import tpu as pltpu
from jax.sharding import PartitionSpec as P

D = 768
HALF = D // 2
HEADS = 12
FF = 3072
FF_HALF = FF // 2
HEAD_DIM = 64
IMAGE_ROWS = 197
ROWS = 256
MB = 2
TAIL = 192
KEPT = FF_HALF + 3 * HALF

EPSILON = 1e-05
MASKED = -1e30
F32 = jnp.float32
BF16 = jnp.bfloat16
VMEM_BYTES = 56 * 1024 * 1024


def dot_nn(left, right):
    return lax.dot_general(left, right, (((1,), (0,)), ((), ())), preferred_element_type=F32)


def dot_nt(left, right):
    return lax.dot_general(left, right, (((1,), (1,)), ((), ())), preferred_element_type=F32)


def dot_tn(left, right):
    return lax.dot_general(left, right, (((0,), (0,)), ((), ())), preferred_element_type=F32)


def norm_parts(hidden):
    centred = hidden - jnp.mean(hidden, axis=-1, keepdims=True)
    spread = jnp.mean(centred * centred, axis=-1, keepdims=True)
    inverse = lax.rsqrt(spread + EPSILON)
    return centred * inverse, inverse


def norm_back(grad, hidden, gain_row):
    unit, inverse = norm_parts(hidden)
    gain_grad = jnp.sum(grad * unit, axis=0, keepdims=True)
    scaled = grad * gain_row
    mean_plain = jnp.mean(scaled, axis=-1, keepdims=True)
    mean_unit = jnp.mean(scaled * unit, axis=-1, keepdims=True)
    return inverse * (scaled - mean_plain - unit * mean_unit), gain_grad


def gelu_pair(values):
    size = jnp.abs(values)
    denom = 1.0 + (0.3275911 * 0.7071067811865476) * size
    rough = pl.reciprocal(denom, approx=True)
    t = rough * (2.0 - denom * rough)
    poly = 0.5 * 1.061405429
    for factor in (-1.453152027, 1.421413741, -0.284496736, 0.254829592):
        poly = poly * t + 0.5 * factor
    bell = jnp.exp(values * values * -0.5)
    upper_tail = poly * t * bell
    cdf = jnp.where(values < 0, upper_tail, 1.0 - upper_tail)
    return values * cdf, cdf + values * bell * 0.3989422804014327


def lane_half(value, which):
    lanes = lax.broadcasted_iota(jnp.int32, value.shape, 1)
    picked = lanes < HEAD_DIM if which == 0 else lanes >= HEAD_DIM
    return jnp.where(picked, value, jnp.zeros_like(value))


def weight_copies(pos, first, second, weights, held, sems):
    qkv_own, qkv_other, proj_own, proj_other, in_own, in_other, back_own, back_other = weights
    qkv_held, proj_held, in_held, back_held = held
    own_at = pl.multiple_of(pos * HALF, HALF)
    other_at = pl.multiple_of((1 - pos) * HALF, HALF)
    own_deep = pl.multiple_of(pos * FF_HALF, FF_HALF)
    other_deep = pl.multiple_of((1 - pos) * FF_HALF, FF_HALF)

    def pair(index, own, other, held_own, held_other):
        return [
            pltpu.make_async_copy(own, held_own, sems.at[index]),
            pltpu.make_async_copy(other, held_other, sems.at[index + 1]),
        ]

    copies = {
        "qkv": pair(
            0,
            qkv_own,
            qkv_other,
            qkv_held.at[pl.ds(own_at, HALF)],
            qkv_held.at[pl.ds(other_at, HALF)],
        ),
        "proj": pair(
            2,
            proj_own,
            proj_other,
            proj_held.at[pl.ds(own_at, HALF)],
            proj_held.at[pl.ds(other_at, HALF)],
        ),
    }
    for slot, expert in ((0, first), (1, second)):
        copies["in", slot] = pair(
            4 + 4 * slot,
            in_own.at[expert],
            in_other.at[expert],
            in_held.at[slot, pl.ds(own_at, HALF)],
            in_held.at[slot, pl.ds(other_at, HALF)],
        )
        copies["back", slot] = pair(
            6 + 4 * slot,
            back_own.at[expert],
            back_other.at[expert],
            back_held.at[slot, pl.ds(own_deep, FF_HALF)],
            back_held.at[slot, pl.ds(other_deep, FF_HALF)],
        )
    return copies


def begin(copies):
    for copy in copies:
        copy.start()


def finish(copies):
    for copy in copies:
        copy.wait()


def forward_kernel(n_alias, info, rows_ref, gain_ref, *rest):
    weights = rest[:8]
    (
        keep_out,
        send_out,
        qkv_out,
        probs_out,
        mixed_out,
        slope_out,
        low_out,
        high_out,
        qkv_held,
        proj_held,
        in_held,
        back_held,
        left_rows,
        qkv_rows,
        probs,
        mixed,
        active,
        slope,
        low,
        high,
        in_sems,
        out_sems,
    ) = rest[8 + n_alias :]
    pos, first, second, live = info[1], info[2], info[3], info[4]

    @pl.when(info[0] == 1)
    def _():
        copies = weight_copies(
            pos, first, second, weights, (qkv_held, proj_held, in_held, back_held), in_sems
        )
        two = first != second
        begin(copies["qkv"])
        begin(copies["proj"])
        begin(copies["in", 0])
        begin(copies["back", 0])

        @pl.when(two)
        def _():
            begin(copies["in", 1])
            begin(copies["back", 1])

        own_at = pl.multiple_of(pos * HALF, HALF)
        other_at = pl.multiple_of((1 - pos) * HALF, HALF)
        sent = []

        def send(source, target):
            copy = pltpu.make_async_copy(source, target, out_sems.at[len(sent)])
            copy.start()
            sent.append(copy)

        def send_halves(place):
            to = FF_HALF + place * HALF
            send(left_rows.at[place, :, pl.ds(own_at, HALF)], keep_out.at[:, pl.ds(to, HALF)])
            send(left_rows.at[place, :, pl.ds(other_at, HALF)], send_out.at[:, pl.ds(to, HALF)])

        hidden = rows_ref[...].astype(F32)
        normed = (norm_parts(hidden)[0] * gain_ref[0:1]).astype(BF16)
        left_rows[0] = normed
        send_halves(0)
        finish(copies["qkv"])
        for part in range(3):
            columns = pl.ds(part * D, D)
            qkv_rows[:, columns] = dot_nn(normed, qkv_held[:, columns]).astype(BF16)
        send(qkv_rows, qkv_out)
        keys_live = lax.broadcasted_iota(jnp.int32, (ROWS, ROWS), 1) < live
        for pair in range(HEADS // 2):
            queries = qkv_rows[:, pl.ds(pair * 128, 128)] * jnp.asarray(HEAD_DIM**-0.5, BF16)
            keys = qkv_rows[:, pl.ds(D + pair * 128, 128)]
            values = qkv_rows[:, pl.ds(2 * D + pair * 128, 128)]
            context = None
            for which in (0, 1):
                scores = dot_nt(lane_half(queries, which), keys)
                scores = jnp.where(keys_live, scores, MASKED)
                shifted = jnp.exp(scores - jnp.max(scores, axis=-1, keepdims=True))
                total = jnp.sum(shifted, axis=-1, keepdims=True)
                weight = (shifted * (1.0 / total)).astype(BF16)
                probs[2 * pair + which] = weight
                term = dot_nn(weight, lane_half(values, which))
                context = term if context is None else context + term
            left_rows[2, :, pl.ds(pair * 128, 128)] = context.astype(BF16)
        send(probs, probs_out)
        send_halves(2)
        finish(copies["proj"])
        mixed[...] = hidden + dot_nn(left_rows[2], proj_held[...])
        send(mixed, mixed_out)
        second_rows = (norm_parts(mixed[...])[0] * gain_ref[1:2]).astype(BF16)
        left_rows[1] = second_rows
        send_halves(1)
        finish(copies["in", 0])
        for part in range(4):
            columns = pl.ds(part * D, D)
            inner = dot_nn(second_rows, in_held[0, :, columns])
            value, derivative = gelu_pair(inner)
            active[:, columns] = value.astype(BF16)
            slope[:, columns] = derivative.astype(BF16)
        finish(copies["back", 0])
        high[...] = mixed[...] + dot_nn(active[...], back_held[0])

        @pl.when(two)
        def _():
            finish(copies["in", 1])
            tail = pl.ds(TAIL, ROWS - TAIL)
            later = lax.broadcasted_iota(jnp.int32, (ROWS - TAIL, D), 0) >= IMAGE_ROWS - TAIL
            for part in range(4):
                columns = pl.ds(part * D, D)
                inner = dot_nn(left_rows[1, tail], in_held[1, :, columns])
                value, derivative = gelu_pair(inner)
                active[tail, columns] = jnp.where(
                    later, value, active[tail, columns].astype(F32)
                ).astype(BF16)
                slope[tail, columns] = jnp.where(
                    later, derivative, slope[tail, columns].astype(F32)
                ).astype(BF16)
            finish(copies["back", 1])
            patched = mixed[tail] + dot_nn(active[tail], back_held[1])
            high[tail] = jnp.where(later, patched, high[tail])

        low[...] = high[...].astype(BF16)
        send(low, low_out)
        send(high, high_out)
        send(slope, slope_out)
        own_deep = pl.multiple_of(pos * FF_HALF, FF_HALF)
        other_deep = pl.multiple_of((1 - pos) * FF_HALF, FF_HALF)
        send(active.at[:, pl.ds(own_deep, FF_HALF)], keep_out.at[:, pl.ds(0, FF_HALF)])
        send(active.at[:, pl.ds(other_deep, FF_HALF)], send_out.at[:, pl.ds(0, FF_HALF)])
        finish(sent)


def any_specs(count):
    return [pl.BlockSpec(memory_space=pl.ANY)] * count


def held_weights():
    return [
        pltpu.VMEM((D, 3 * D), BF16),
        pltpu.VMEM((D, D), BF16),
        pltpu.VMEM((2, D, FF), BF16),
        pltpu.VMEM((2, FF, D), BF16),
    ]


def forward_item(info, rows, gains, weights, saved=None):
    shapes = [
        jax.ShapeDtypeStruct((ROWS, KEPT), BF16),
        jax.ShapeDtypeStruct((ROWS, KEPT), BF16),
        jax.ShapeDtypeStruct((ROWS, 3 * D), BF16),
        jax.ShapeDtypeStruct((HEADS, ROWS, ROWS), BF16),
        jax.ShapeDtypeStruct((ROWS, D), F32),
        jax.ShapeDtypeStruct((ROWS, FF), BF16),
        jax.ShapeDtypeStruct((ROWS, D), BF16),
        jax.ShapeDtypeStruct((ROWS, D), F32),
    ]
    saved = () if saved is None else tuple(saved)
    vmem = pl.BlockSpec(memory_space=pltpu.VMEM)
    return pl.pallas_call(
        functools.partial(forward_kernel, len(saved)),
        out_shape=shapes,
        in_specs=[pl.BlockSpec(memory_space=pltpu.SMEM), vmem, vmem] + any_specs(8 + len(saved)),
        out_specs=any_specs(8),
        input_output_aliases={11 + place: place for place in range(len(saved))},
        scratch_shapes=held_weights()
        + [
            pltpu.VMEM((3, ROWS, D), BF16),
            pltpu.VMEM((ROWS, 3 * D), BF16),
            pltpu.VMEM((HEADS, ROWS, ROWS), BF16),
            pltpu.VMEM((ROWS, D), F32),
            pltpu.VMEM((ROWS, FF), BF16),
            pltpu.VMEM((ROWS, FF), BF16),
            pltpu.VMEM((ROWS, D), BF16),
            pltpu.VMEM((ROWS, D), F32),
            pltpu.SemaphoreType.DMA((12,)),
            pltpu.SemaphoreType.DMA((16,)),
        ],
        compiler_params=pltpu.CompilerParams(vmem_limit_bytes=VMEM_BYTES),
        cost_estimate=pl.CostEstimate(
            flops=2 * ROWS * 7 * 1024 * 1024, bytes_accessed=32 << 20, transcendentals=0
        ),
        name="forward_item",
    )(info, rows, gains, *weights, *saved)


def backward_kernel(n_alias, info, rows_ref, grad_ref, gain_ref, *rest):
    weights = rest[:8]
    qkv_in, probs_in, mixed_in, slope_in = rest[8:12]
    (
        inner_out,
        outer_out,
        gain_out,
        low_out,
        high_out,
        qkv_held,
        proj_held,
        in_held,
        back_held,
        qkv_rows,
        probs,
        mixed,
        slope,
        inner,
        outer,
        gain_rows,
        middle,
        low,
        high,
        in_sems,
        saved_sems,
        out_sems,
    ) = rest[12 + n_alias :]
    pos, first, second, live = info[1], info[2], info[3], info[4]

    @pl.when(info[0] == 1)
    def _():
        copies = weight_copies(
            pos, first, second, weights, (qkv_held, proj_held, in_held, back_held), in_sems
        )
        saved = [
            pltpu.make_async_copy(source, target, saved_sems.at[place])
            for place, (source, target) in enumerate(
                ((slope_in, slope), (mixed_in, mixed), (qkv_in, qkv_rows), (probs_in, probs))
            )
        ]
        two = first != second
        begin(copies["back", 0])
        begin(saved[:1])
        begin(copies["in", 0])
        begin(saved[1:2])

        @pl.when(two)
        def _():
            begin(copies["back", 1])
            begin(copies["in", 1])

        begin(copies["proj"])
        begin(saved[2:])
        begin(copies["qkv"])
        sent = []

        def send(source, target):
            copy = pltpu.make_async_copy(source, target, out_sems.at[len(sent)])
            copy.start()
            sent.append(copy)

        is_live = lax.broadcasted_iota(jnp.int32, (ROWS, D), 0) < live
        grad = jnp.where(is_live, grad_ref[...].astype(F32), 0.0)
        grad_low = grad.astype(BF16)
        finish(copies["back", 0])
        finish(saved[:1])
        for part in range(4):
            columns = pl.ds(part * D, D)
            grad_active = dot_nt(grad_low, back_held[0, columns])
            inner[:, columns] = (grad_active * slope[:, columns].astype(F32)).astype(BF16)
        finish(copies["in", 0])
        middle[...] = dot_nt(inner[...], in_held[0])

        @pl.when(two)
        def _():
            finish(copies["back", 1])
            tail = pl.ds(TAIL, ROWS - TAIL)
            later = lax.broadcasted_iota(jnp.int32, (ROWS - TAIL, D), 0) >= IMAGE_ROWS - TAIL
            for part in range(4):
                columns = pl.ds(part * D, D)
                grad_active = dot_nt(grad_low[TAIL:], back_held[1, columns])
                patched = grad_active * slope[tail, columns].astype(F32)
                inner[tail, columns] = jnp.where(
                    later, patched, inner[tail, columns].astype(F32)
                ).astype(BF16)
            finish(copies["in", 1])
            patched = dot_nt(inner[tail], in_held[1])
            middle[tail] = jnp.where(later, patched, middle[tail])

        send(inner, inner_out)
        finish(saved[1:2])
        grad_mixed, gain_second = norm_back(middle[...], mixed[...], gain_ref[1:2])
        grad_mixed = grad + grad_mixed
        middle[...] = grad_mixed
        branch = grad_mixed.astype(BF16)
        outer[:, pl.ds(3 * D, D)] = branch
        finish(copies["proj"])
        grad_context = dot_nt(branch, proj_held[...]).astype(BF16)
        finish(saved[2:])
        scale = jnp.asarray(HEAD_DIM**-0.5, BF16)
        for pair in range(HEADS // 2):
            queries = qkv_rows[:, pl.ds(pair * 128, 128)] * scale
            keys = qkv_rows[:, pl.ds(D + pair * 128, 128)] * scale
            values = qkv_rows[:, pl.ds(2 * D + pair * 128, 128)]
            context = grad_context[:, pair * 128 : (pair + 1) * 128]
            grad_q = grad_k = grad_v = None
            for which in (0, 1):
                weight = probs[2 * pair + which]
                context_half = lane_half(context, which)
                grad_probs = dot_nt(context_half, values)
                weight_wide = weight.astype(F32)
                product = weight_wide * grad_probs
                row_total = jnp.sum(product, axis=-1, keepdims=True)
                grad_scores = (product - weight_wide * row_total).astype(BF16)
                term_v = dot_tn(weight, context_half)
                term_q = dot_nn(grad_scores, lane_half(keys, which))
                term_k = dot_tn(grad_scores, lane_half(queries, which))
                grad_q = term_q if grad_q is None else grad_q + term_q
                grad_k = term_k if grad_k is None else grad_k + term_k
                grad_v = term_v if grad_v is None else grad_v + term_v
            outer[:, pl.ds(pair * 128, 128)] = grad_q.astype(BF16)
            outer[:, pl.ds(D + pair * 128, 128)] = grad_k.astype(BF16)
            outer[:, pl.ds(2 * D + pair * 128, 128)] = grad_v.astype(BF16)
        send(outer, outer_out)
        finish(copies["qkv"])
        grad_normed = dot_nt(outer[:, pl.ds(0, 3 * D)], qkv_held[...])
        hidden = rows_ref[...].astype(F32)
        grad_hidden, gain_first = norm_back(grad_normed, hidden, gain_ref[0:1])
        high[...] = middle[...] + grad_hidden
        low[...] = high[...].astype(BF16)
        gain_rows[0:1] = gain_first
        gain_rows[1:2] = gain_second
        send(low, low_out)
        send(high, high_out)
        send(gain_rows, gain_out)
        finish(sent)


def backward_item(info, rows, grad, gains, weights, kept, earlier=None):
    shapes = [
        jax.ShapeDtypeStruct((ROWS, FF), BF16),
        jax.ShapeDtypeStruct((ROWS, 4 * D), BF16),
        jax.ShapeDtypeStruct((2, D), F32),
        jax.ShapeDtypeStruct((ROWS, D), BF16),
        jax.ShapeDtypeStruct((ROWS, D), F32),
    ]
    earlier = () if earlier is None else tuple(earlier)
    vmem = pl.BlockSpec(memory_space=pltpu.VMEM)
    return pl.pallas_call(
        functools.partial(backward_kernel, len(earlier)),
        out_shape=shapes,
        in_specs=[pl.BlockSpec(memory_space=pltpu.SMEM)] + [vmem] * 3 + any_specs(12 + len(earlier)),
        out_specs=any_specs(5),
        input_output_aliases={16 + place: place for place in range(len(earlier))},
        scratch_shapes=held_weights()
        + [
            pltpu.VMEM((ROWS, 3 * D), BF16),
            pltpu.VMEM((HEADS, ROWS, ROWS), BF16),
            pltpu.VMEM((ROWS, D), F32),
            pltpu.VMEM((ROWS, FF), BF16),
            pltpu.VMEM((ROWS, FF), BF16),
            pltpu.VMEM((ROWS, 4 * D), BF16),
            pltpu.VMEM((2, D), F32),
            pltpu.VMEM((ROWS, D), F32),
            pltpu.VMEM((ROWS, D), BF16),
            pltpu.VMEM((ROWS, D), F32),
            pltpu.SemaphoreType.DMA((12,)),
            pltpu.SemaphoreType.DMA((4,)),
            pltpu.SemaphoreType.DMA((8,)),
        ],
        compiler_params=pltpu.CompilerParams(vmem_limit_bytes=VMEM_BYTES),
        cost_estimate=pl.CostEstimate(
            flops=2 * ROWS * 7 * 1024 * 1024, bytes_accessed=32 << 20, transcendentals=0
        ),
        name="backward_item",
    )(info, rows, grad, gains, *weights, *kept, *earlier)


def expert_masks(info, item, expert):
    row = lax.broadcasted_iota(jnp.int32, (ROWS, 1), 0)
    first, second = info[2 * item], info[2 * item + 1]
    mine = jnp.where(row < IMAGE_ROWS, first, second)
    return mine == expert


def back_grads_kernel(info, *refs):
    actives, grads, out, flipped = refs[:4], refs[4:8], refs[8], refs[9]

    @pl.when(pl.program_id(0) == 0)
    def _():
        for expert in (0, 1):
            for item in range(4):
                mask = expert_masks(info, item, expert)
                value = jnp.where(mask, grads[item][...].astype(F32), 0.0)
                flipped[expert, :, pl.ds(item * ROWS, ROWS)] = value.T.astype(BF16)

    for expert in (0, 1):
        total = None
        for item in range(4):
            term = dot_nn(flipped[expert, :, pl.ds(item * ROWS, ROWS)], actives[item][...])
            total = term if total is None else total + term
        out[expert] = total.astype(BF16)


def back_grads(info, kept, grads):
    width = 512
    return pl.pallas_call(
        back_grads_kernel,
        grid=(FF_HALF // width,),
        out_shape=jax.ShapeDtypeStruct((2, D, FF_HALF), BF16),
        in_specs=[pl.BlockSpec(memory_space=pltpu.SMEM)]
        + [pl.BlockSpec((ROWS, width), lambda step: (0, step))] * 4
        + [pl.BlockSpec((ROWS, D), lambda step: (0, 0))] * 4,
        out_specs=pl.BlockSpec((2, D, width), lambda step: (0, 0, step)),
        scratch_shapes=[pltpu.VMEM((2, D, 4 * ROWS), BF16)],
        compiler_params=pltpu.CompilerParams(vmem_limit_bytes=VMEM_BYTES),
        cost_estimate=pl.CostEstimate(
            flops=4 * D * FF_HALF * 4 * ROWS, bytes_accessed=16 << 20, transcendentals=0
        ),
        name="back_grads",
    )(info, *kept, *grads)


def in_grads_kernel(parts, info, *refs):
    seconds, inners, out, flipped = refs[:4], refs[4:8], refs[8], refs[9]

    @pl.when(pl.program_id(0) == 0)
    def _():
        for expert in (0, 1):
            for item in range(4):
                mask = expert_masks(info, item, expert)
                value = jnp.where(mask, seconds[item][...].astype(F32), 0.0)
                flipped[expert, :, pl.ds(item * ROWS, ROWS)] = value.T.astype(BF16)

    width = D // parts
    for expert in (0, 1):
        total = None
        for item in range(4):
            term = dot_nn(flipped[expert, :, pl.ds(item * ROWS, ROWS)], inners[item][...])
            total = term if total is None else total + term
        for part in range(parts):
            out[part, expert] = total[:, part * width : (part + 1) * width].astype(BF16)


def in_grads(info, kept, inners, blocks):
    parts = max(1, blocks * D // FF)
    width = D // parts
    return pl.pallas_call(
        functools.partial(in_grads_kernel, parts),
        grid=(FF // D,),
        out_shape=jax.ShapeDtypeStruct((FF // width, 2, HALF, width), BF16),
        in_specs=[pl.BlockSpec(memory_space=pltpu.SMEM)]
        + [pl.BlockSpec((ROWS, HALF), lambda step: (0, FF_HALF // HALF + 1))] * 4
        + [pl.BlockSpec((ROWS, D), lambda step: (0, step))] * 4,
        out_specs=pl.BlockSpec((parts, 2, HALF, width), lambda step: (step, 0, 0, 0)),
        scratch_shapes=[pltpu.VMEM((2, HALF, 4 * ROWS), BF16)],
        compiler_params=pltpu.CompilerParams(vmem_limit_bytes=VMEM_BYTES),
        cost_estimate=pl.CostEstimate(
            flops=4 * D * FF_HALF * 4 * ROWS, bytes_accessed=16 << 20, transcendentals=0
        ),
        name="in_grads",
    )(info, *kept, *inners)


def outer_grads_kernel(*refs):
    lefts, outers, out = refs[:4], refs[4:8], refs[8]
    total = None
    for item in range(4):
        term = dot_tn(outers[item][...], lefts[item][...])
        total = term if total is None else total + term
    out[...] = total.astype(BF16)


def outer_grads(kept, outers):
    place = FF_HALF // HALF
    return pl.pallas_call(
        outer_grads_kernel,
        grid=(4,),
        out_shape=jax.ShapeDtypeStruct((4 * D, HALF), BF16),
        in_specs=[pl.BlockSpec((ROWS, HALF), lambda step: (0, place + 2 * (step // 3)))] * 4
        + [pl.BlockSpec((ROWS, D), lambda step: (0, step))] * 4,
        out_specs=pl.BlockSpec((D, HALF), lambda step: (step, 0)),
        compiler_params=pltpu.CompilerParams(vmem_limit_bytes=VMEM_BYTES),
        cost_estimate=pl.CostEstimate(
            flops=8 * D * HALF * 4 * ROWS, bytes_accessed=16 << 20, transcendentals=0
        ),
        name="outer_grads",
    )(*kept, *outers)


def swapped(block, axis, bit):
    count = lax.axis_size(axis)
    route = [(place, place ^ 1 << bit) for place in range(count)]
    return lax.ppermute(block, axis, route)


def passed_along(value, steps):
    count = lax.axis_size("section")
    first, last = (max(0, -steps), min(count, count - steps))
    route = [(source, source + steps) for source in range(first, last)]
    return lax.ppermute(value, "section", route)


def split_bit(stacked, bit):
    here = (lax.axis_index("dp") >> bit) & 1
    mine = lax.dynamic_index_in_dim(stacked, here, 0, keepdims=False)
    theirs = lax.dynamic_index_in_dim(stacked, 1 - here, 0, keepdims=False)
    return mine, theirs


def added(left, right):
    return left.astype(F32) + right.astype(F32)


def scattered_sums(pieces):
    bits = lax.axis_size("dp").bit_length() - 1
    waiting = []
    for piece in pieces:
        mine, theirs = split_bit(piece, 0)
        waiting.append([mine, swapped(theirs, "dp", 0)])
    results = [None] * len(pieces)
    last = None
    for step in range(len(pieces) + bits - 1):
        for bit in range(bits):
            place = step - bit
            if not 0 <= place < len(pieces):
                continue
            mine, got = waiting[place]
            if last is not None:
                mine, last = lax.optimization_barrier((mine, last))
            total = added(mine, got)
            if bit == bits - 1:
                results[place] = last = total
            else:
                mine, theirs = split_bit(total.astype(BF16), bit + 1)
                waiting[place] = [mine, swapped(theirs, "dp", bit + 1)]
                last = mine
    return results


def lowest_first(stacked, bits):
    split = stacked.reshape((2,) * bits + stacked.shape[1:])
    return split.transpose(tuple(reversed(range(bits))) + tuple(range(bits, split.ndim)))


def shards(feeds, text_lengths, norm_gains, qkv_weight, out_weight, expert_in, expert_out):
    n_dp = lax.axis_size("dp")
    bits = n_dp.bit_length() - 1
    section_pos = lax.axis_index("section")
    is_lower = section_pos < 2
    pos = section_pos % 2
    qkv_weight, out_weight = qkv_weight[0], out_weight[0]
    expert_in, expert_out = expert_in[0], expert_out[0]
    weights = []
    for own in (qkv_weight, out_weight, expert_in, expert_out):
        weights += [own, swapped(own, "section", 0)]
    own_gains = norm_gains[0]
    other_gains = swapped(own_gains, "section", 0)
    gains = jnp.where(
        pos == 0,
        jnp.concatenate([own_gains, other_gains], axis=1),
        jnp.concatenate([other_gains, own_gains], axis=1),
    ).astype(F32)

    def experts_of(lengths):
        kinds = (lengths > 0).astype(jnp.int32)
        return jnp.where(is_lower, 0, kinds), jnp.where(is_lower, 1, kinds)

    lengths_mine = lax.dynamic_slice_in_dim(text_lengths, pos * MB, MB)
    lengths_other = lax.dynamic_slice_in_dim(text_lengths, (1 - pos) * MB, MB)
    first, second = experts_of(lengths_mine)
    live = IMAGE_ROWS + lengths_mine

    def item_info(item, active):
        return jnp.stack([active.astype(jnp.int32), pos, first[item], second[item], live[item]])

    expert_info = jnp.stack(experts_of(jnp.concatenate([lengths_mine, lengths_other])), axis=1)
    expert_info = expert_info.reshape(-1)
    blocks = [feeds[item * ROWS : (item + 1) * ROWS] for item in range(MB)]

    def live_rows(item, value):
        row = lax.broadcasted_iota(jnp.int32, (ROWS, 1), 0)
        return jnp.where(row < live[item], value, jnp.zeros_like(value))

    lower = [
        forward_item(item_info(item, is_lower), blocks[item], gains, weights)
        for item in range(MB)
    ]
    passed = [passed_along(lower[item][6], 2) for item in range(MB)]
    kept, back, ups, ends_up = [], [], [], []
    for item in range(MB):
        info = item_info(item, ~is_lower)
        upper = forward_item(info, passed[item], gains, weights, saved=lower[item][:6])
        kept.append(upper[:6])
        ends_up.append(upper[7])
        back.append(backward_item(info, passed[item], blocks[item], gains, weights, upper[2:6]))
        ups.append(passed_along(back[item][3], -2))
    grads_low = [
        live_rows(item, jnp.where(is_lower, ups[item], blocks[item])) for item in range(MB)
    ]
    kept_rows = [kept[item][0] for item in range(MB)]
    kept_rows += [swapped(kept[item][1], "section", 0) for item in range(MB)]
    grads_all = grads_low + [swapped(grads_low[item], "section", 0) for item in range(MB)]
    back_full = back_grads(expert_info, kept_rows, grads_all)
    for item in range(MB):
        info = item_info(item, is_lower)
        back[item] = backward_item(
            info, blocks[item], grads_low[item], gains, weights, kept[item][2:6], back[item][:3]
        )
    inners = [back[item][0] for item in range(MB)]
    inners += [swapped(back[item][0], "section", 0) for item in range(MB)]
    outers = [back[item][1] for item in range(MB)]
    outers += [swapped(back[item][1], "section", 0) for item in range(MB)]
    in_full = in_grads(expert_info, kept_rows, inners, n_dp if FF // n_dp % 128 == 0 else 1)
    outer_full = outer_grads(kept_rows, outers)
    ends = jnp.concatenate(
        [jnp.where(is_lower, back[item][4], ends_up[item]) for item in range(MB)], axis=0
    )

    gain_sum = back[0][2] + back[1][2]
    gain_halves = gain_sum.reshape(2, 2, HALF)
    gain_own = lax.dynamic_index_in_dim(gain_halves, pos, 1, keepdims=False)
    gain_theirs = lax.dynamic_index_in_dim(gain_halves, 1 - pos, 1, keepdims=False)
    gain_own = gain_own + swapped(gain_theirs, "section", 0)
    gain_stack = gain_own.reshape(2, n_dp, HALF // n_dp).transpose(1, 0, 2)
    gain_stack = gain_stack.reshape(n_dp, 1, 2 * HALF // n_dp)
    gain_stack = jnp.pad(gain_stack, ((0, 0), (0, 15), (0, HALF - 2 * HALF // n_dp)))

    pieces = []
    back_split = back_full.reshape(2, n_dp, D // n_dp, FF_HALF)
    for expert in (0, 1):
        pieces.append(lowest_first(back_split[expert], bits))
    if in_full.shape[0] == n_dp:
        in_split = [in_full[:, expert] for expert in (0, 1)]
    else:
        wide = in_full.transpose(1, 2, 0, 3).reshape(2, HALF, n_dp, FF // n_dp)
        in_split = [wide[expert].transpose(1, 0, 2) for expert in (0, 1)]
    pieces += [lowest_first(part, bits) for part in in_split]
    last = jnp.concatenate(
        [
            outer_full[: 3 * D].reshape(n_dp, 3 * D // n_dp, HALF),
            outer_full[3 * D :].reshape(n_dp, D // n_dp, HALF),
            gain_stack.astype(BF16),
        ],
        axis=1,
    )
    pieces.append(lowest_first(last, bits))
    sums = scattered_sums(pieces)
    qkv_rows, proj_rows = 3 * D // n_dp, D // n_dp
    qkv_sum = sums[4][:qkv_rows].T
    proj_sum = sums[4][qkv_rows : qkv_rows + proj_rows].T
    gain_total = sums[4][qkv_rows + proj_rows, : 2 * HALF // n_dp].reshape(2, HALF // n_dp)
    back_sum = jnp.stack([sums[0].T, sums[1].T])
    in_sum = jnp.stack([sums[2], sums[3]])
    return (
        ends,
        gain_total[None],
        qkv_sum[None],
        proj_sum[None],
        in_sum[None],
        back_sum[None],
    )


def solution(mesh):
    return jax.shard_map(
        shards,
        mesh=mesh,
        in_specs=(
            P(("dp", "section"), None),
            P("dp"),
            P("section", None, None),
            P("section", None, None),
            P("section", None, None),
            P("section", None, None, None),
            P("section", None, None, None),
        ),
        out_specs=(
            P(("dp", "section"), None),
            P("section", None, "dp"),
            P("section", None, "dp"),
            P("section", None, "dp"),
            P("section", None, None, "dp"),
            P("section", None, None, "dp"),
        ),
        check_vma=False,
    )
```

```python
import functools

import jax
import jax.numpy as jnp
from jax import lax
from jax.experimental import pallas as pl
from jax.experimental.pallas import tpu as pltpu
from jax.sharding import PartitionSpec as P

D = 768
HALF = D // 2
HEADS = 12
FF = 3072
FF_HALF = FF // 2
HEAD_DIM = 64
IMAGE_ROWS = 197
ROWS = 256
MB = 2
TAIL = 192

EPSILON = 1e-05
MASKED = -1e30
F32 = jnp.float32
BF16 = jnp.bfloat16
VMEM_BYTES = 12 * 1024 * 1024


def dot_nn(left, right):
    return lax.dot_general(left, right, (((1,), (0,)), ((), ())), preferred_element_type=F32)


def dot_nt(left, right):
    return lax.dot_general(left, right, (((1,), (1,)), ((), ())), preferred_element_type=F32)


def dot_tn(left, right):
    return lax.dot_general(left, right, (((0,), (0,)), ((), ())), preferred_element_type=F32)


def norm_parts(hidden):
    centred = hidden - jnp.mean(hidden, axis=-1, keepdims=True)
    spread = jnp.mean(centred * centred, axis=-1, keepdims=True)
    inverse = lax.rsqrt(spread + EPSILON)
    return centred * inverse, inverse


def norm_back(grad, hidden, gain_row):
    unit, inverse = norm_parts(hidden)
    gain_grad = jnp.sum(grad * unit, axis=0, keepdims=True)
    scaled = grad * gain_row
    mean_plain = jnp.mean(scaled, axis=-1, keepdims=True)
    mean_unit = jnp.mean(scaled * unit, axis=-1, keepdims=True)
    return inverse * (scaled - mean_plain - unit * mean_unit), gain_grad


def gelu_pair(values):
    size = jnp.abs(values)
    denom = 1.0 + (0.3275911 * 0.7071067811865476) * size
    rough = pl.reciprocal(denom, approx=True)
    t = rough * (2.0 - denom * rough)
    poly = 0.5 * 1.061405429
    for factor in (-1.453152027, 1.421413741, -0.284496736, 0.254829592):
        poly = poly * t + 0.5 * factor
    bell = jnp.exp(values * values * -0.5)
    upper_tail = poly * t * bell
    cdf = jnp.where(values < 0, upper_tail, 1.0 - upper_tail)
    return values * cdf, cdf + values * bell * 0.3989422804014327


def lane_half(value, which):
    lanes = lax.broadcasted_iota(jnp.int32, value.shape, 1)
    picked = lanes < HEAD_DIM if which == 0 else lanes >= HEAD_DIM
    return jnp.where(picked, value, jnp.zeros_like(value))


def call(kernel, name, ins, outs, scratch, aliases=None, flops=0):
    spaces = {"vmem": pltpu.VMEM, "smem": pltpu.SMEM, "any": pl.ANY}
    shapes = [
        pltpu.VMEM(shape, kind) if space == "vmem" else jax.ShapeDtypeStruct(shape, kind)
        for shape, kind, space in outs
    ]
    return pl.pallas_call(
        kernel,
        out_shape=shapes,
        in_specs=[pl.BlockSpec(memory_space=spaces[space]) for _, space in ins],
        out_specs=[pl.BlockSpec(memory_space=spaces[space]) for _, _, space in outs],
        input_output_aliases=aliases or {},
        scratch_shapes=scratch,
        compiler_params=pltpu.CompilerParams(vmem_limit_bytes=VMEM_BYTES),
        cost_estimate=pl.CostEstimate(flops=flops, bytes_accessed=0, transcendentals=0),
        name=name,
    )(*[value for value, _ in ins])


class Place:
    def __init__(self, lengths):
        section = lax.axis_index("section")
        self.lengths = lengths
        self.is_lower = section < 2
        self.pos = section % 2

    def length(self, item, partner=False):
        pos = 1 - self.pos if partner else self.pos
        return self.lengths[pos * MB + item]

    def live(self, item, partner=False):
        return IMAGE_ROWS + self.length(item, partner)

    def experts(self, item, partner=False):
        kind = jnp.where(self.length(item, partner) > 0, 1, 0)
        return jnp.where(self.is_lower, 0, kind), jnp.where(self.is_lower, 1, kind)


def with_earlier(ins, outs, earlier):
    if earlier is None:
        return ins, {}
    aliases = {len(ins) + place: place for place in range(len(earlier))}
    return ins + [(value, outs[place][2]) for place, value in enumerate(earlier)], aliases


class Sender:
    def __init__(self, sems):
        self.sems = sems
        self.sent = []

    def send(self, source, target):
        copy = pltpu.make_async_copy(source, target, self.sems.at[len(self.sent)])
        copy.start()
        self.sent.append(copy)

    def finish(self):
        for copy in self.sent:
            copy.wait()


def join_kernel(count, *refs):
    own, other, joined, sems = refs[:count], refs[count : 2 * count], refs[2 * count : -1], refs[-1]
    pos = lax.axis_index("section") % 2
    sender = Sender(sems)
    for mine, theirs, whole in zip(own, other, joined):
        depth = mine.shape[-2]
        for source, at in ((mine, pos), (theirs, 1 - pos)):
            rows = pl.ds(pl.multiple_of(at * depth, depth), depth)
            if len(whole.shape) == 2:
                sender.send(source, whole.at[rows])
            else:
                for expert in range(whole.shape[0]):
                    sender.send(source.at[expert], whole.at[expert, rows])
    sender.finish()


def joined_halves(own, other):
    outs = []
    for part in own:
        shape = part.shape[:-2] + (2 * part.shape[-2], part.shape[-1])
        outs.append((shape, BF16, "vmem"))
    return call(
        functools.partial(join_kernel, len(own)),
        "joined_halves",
        [(value, "any") for value in own + other],
        outs,
        [pltpu.SemaphoreType.DMA((4 * len(own),))],
    )


def gains_kernel(own, other, gains):
    first = lax.axis_index("section") % 2 == 0
    mine, theirs = own[...].astype(F32), other[...].astype(F32)
    gains[:, pl.ds(0, HALF)] = jnp.where(first, mine, theirs)
    gains[:, pl.ds(HALF, HALF)] = jnp.where(first, theirs, mine)


def joined_gains(own, other):
    return call(
        gains_kernel, "joined_gains", [(own, "vmem"), (other, "vmem")], [((2, D), F32, "vmem")], []
    )[0]


def places(pos, size):
    return (
        pl.ds(pl.multiple_of(pos * size, size), size),
        pl.ds(pl.multiple_of((1 - pos) * size, size), size),
    )


def attend_kernel(n_alias, lower, item, lengths, feed_ref, gain_ref, qkv_held, proj_held, *rest):
    qkv_rows, probs, mixed, keep_out, send_out, left_rows, sems = rest[n_alias:]
    place = Place(lengths)
    live = place.live(item)
    rows_ref = feed_ref.at[pl.ds(item * ROWS, ROWS)] if lower else feed_ref

    @pl.when(place.is_lower == lower)
    def _():
        sender = Sender(sems)
        own, other = places(place.pos, HALF)

        def send_halves(place):
            to = pl.ds(place * HALF, HALF)
            sender.send(left_rows.at[place, :, own], keep_out.at[:, to])
            sender.send(left_rows.at[place, :, other], send_out.at[:, to])

        hidden = rows_ref[...].astype(F32)
        normed = (norm_parts(hidden)[0] * gain_ref[0:1]).astype(BF16)
        left_rows[0] = normed
        send_halves(0)
        for part in range(3):
            columns = pl.ds(part * D, D)
            qkv_rows[:, columns] = dot_nn(normed, qkv_held[:, columns]).astype(BF16)
        keys_live = lax.broadcasted_iota(jnp.int32, (ROWS, ROWS), 1) < live
        for pair in range(HEADS // 2):
            queries = qkv_rows[:, pl.ds(pair * 128, 128)] * jnp.asarray(HEAD_DIM**-0.5, BF16)
            keys = qkv_rows[:, pl.ds(D + pair * 128, 128)]
            values = qkv_rows[:, pl.ds(2 * D + pair * 128, 128)]
            context = None
            for which in (0, 1):
                scores = dot_nt(lane_half(queries, which), keys)
                scores = jnp.where(keys_live, scores, MASKED)
                shifted = jnp.exp(scores - jnp.max(scores, axis=-1, keepdims=True))
                total = jnp.sum(shifted, axis=-1, keepdims=True)
                weight = (shifted * (1.0 / total)).astype(BF16)
                probs[2 * pair + which] = weight
                term = dot_nn(weight, lane_half(values, which))
                context = term if context is None else context + term
            left_rows[1, :, pl.ds(pair * 128, 128)] = context.astype(BF16)
        send_halves(1)
        mixed[...] = rows_ref[...].astype(F32) + dot_nn(left_rows[1], proj_held[...])
        sender.finish()


def attend(lower, item, lengths, rows, gains, qkv_held, proj_held, earlier=None):
    outs = [
        ((ROWS, 3 * D), BF16, "vmem"),
        ((HEADS, ROWS, ROWS), BF16, "vmem"),
        ((ROWS, D), F32, "vmem"),
        ((ROWS, D), BF16, "any"),
        ((ROWS, D), BF16, "any"),
    ]
    ins = [(lengths, "smem"), (rows, "vmem"), (gains, "vmem")]
    ins += [(qkv_held, "vmem"), (proj_held, "vmem")]
    ins, aliases = with_earlier(ins, outs, earlier)
    scratch = [pltpu.VMEM((2, ROWS, D), BF16), pltpu.SemaphoreType.DMA((4,))]
    kernel = functools.partial(attend_kernel, len(aliases), lower, item)
    return call(kernel, "attend", ins, outs, scratch, aliases, 1 << 32)


def expand_kernel(n_alias, lower, item, lengths, mixed, gain_ref, in_held, back_held, *rest):
    results = rest[n_alias:]
    if lower:
        slope, keep_out, send_out, low = results[:4]
    else:
        slope, keep_out, send_out, ends_out = results[:4]
    second_rows, active, high, sems = results[-4:]
    place = Place(lengths)
    first, second = place.experts(item)

    @pl.when(place.is_lower == lower)
    def _():
        sender = Sender(sems)
        own, other = places(place.pos, HALF)
        own_deep, other_deep = places(place.pos, FF_HALF)
        normed = (norm_parts(mixed[...])[0] * gain_ref[1:2]).astype(BF16)
        second_rows[...] = normed
        sender.send(second_rows.at[:, own], keep_out.at[:, pl.ds(FF_HALF, HALF)])
        sender.send(second_rows.at[:, other], send_out.at[:, pl.ds(FF_HALF, HALF)])
        for part in range(4):
            columns = pl.ds(part * D, D)
            value, derivative = gelu_pair(dot_nn(normed, in_held[first, :, columns]))
            active[:, columns] = value.astype(BF16)
            slope[:, columns] = derivative.astype(BF16)
        high[...] = mixed[...] + dot_nn(active[...], back_held[first])

        def language_rows():
            tail = pl.ds(TAIL, ROWS - TAIL)
            later = lax.broadcasted_iota(jnp.int32, (ROWS - TAIL, D), 0) >= IMAGE_ROWS - TAIL
            for part in range(4):
                columns = pl.ds(part * D, D)
                value, derivative = gelu_pair(dot_nn(second_rows[tail], in_held[second, :, columns]))
                active[tail, columns] = jnp.where(
                    later, value, active[tail, columns].astype(F32)
                ).astype(BF16)
                slope[tail, columns] = jnp.where(
                    later, derivative, slope[tail, columns].astype(F32)
                ).astype(BF16)
            patched = mixed[tail] + dot_nn(active[tail], back_held[second])
            high[tail] = jnp.where(later, patched, high[tail])

        if lower:
            language_rows()
            low[...] = high[...].astype(BF16)
        sender.send(active.at[:, own_deep], keep_out.at[:, pl.ds(0, FF_HALF)])
        sender.send(active.at[:, other_deep], send_out.at[:, pl.ds(0, FF_HALF)])
        if not lower:
            sender.send(high, ends_out.at[pl.ds(item * ROWS, ROWS)])
        sender.finish()


def expand(lower, item, lengths, mixed, gains, in_held, back_held, earlier=None):
    outs = [
        ((ROWS, FF), BF16, "vmem"),
        ((ROWS, FF_HALF + HALF), BF16, "any"),
        ((ROWS, FF_HALF + HALF), BF16, "any"),
        ((ROWS, D), BF16, "vmem") if lower else ((MB * ROWS, D), F32, "any"),
    ]
    ins = [(lengths, "smem"), (mixed, "vmem"), (gains, "vmem")]
    ins += [(in_held, "vmem"), (back_held, "vmem")]
    ins, aliases = with_earlier(ins, outs, earlier)
    scratch = [
        pltpu.VMEM((ROWS, D), BF16),
        pltpu.VMEM((ROWS, FF), BF16),
        pltpu.VMEM((ROWS, D), F32),
        pltpu.SemaphoreType.DMA((5,)),
    ]
    kernel = functools.partial(expand_kernel, len(aliases), lower, item)
    return call(kernel, "expand", ins, outs, scratch, aliases, 1 << 32)


def expand_back_kernel(
    n_alias, lower, item, lengths, end_ref, mixed, slope, gain_ref, in_held, back_held, *rest
):
    inner_out, gain_out, middle, inner, sems = rest[n_alias:]
    place = Place(lengths)
    first, second = place.experts(item)
    grad_ref = end_ref if lower else end_ref.at[pl.ds(item * ROWS, ROWS)]

    @pl.when(place.is_lower == lower)
    def _():
        sender = Sender(sems)
        is_live = lax.broadcasted_iota(jnp.int32, (ROWS, D), 0) < place.live(item)
        grad = jnp.where(is_live, grad_ref[...].astype(F32), 0.0)
        grad_low = grad.astype(BF16)
        for part in range(4):
            columns = pl.ds(part * D, D)
            grad_active = dot_nt(grad_low, back_held[first, columns])
            inner[:, columns] = (grad_active * slope[:, columns].astype(F32)).astype(BF16)
        middle[...] = dot_nt(inner[...], in_held[first])

        def language_rows():
            tail = pl.ds(TAIL, ROWS - TAIL)
            later = lax.broadcasted_iota(jnp.int32, (ROWS - TAIL, D), 0) >= IMAGE_ROWS - TAIL
            for part in range(4):
                columns = pl.ds(part * D, D)
                grad_active = dot_nt(grad_low[TAIL:], back_held[second, columns])
                patched = grad_active * slope[tail, columns].astype(F32)
                inner[tail, columns] = jnp.where(
                    later, patched, inner[tail, columns].astype(F32)
                ).astype(BF16)
            patched = dot_nt(inner[tail], in_held[second])
            middle[tail] = jnp.where(later, patched, middle[tail])

        if lower:
            language_rows()
        sender.send(inner, inner_out)
        grad_mixed, gain_out[...] = norm_back(middle[...], mixed[...], gain_ref[1:2])
        middle[...] = grad + grad_mixed
        sender.finish()


def expand_back(lower, item, lengths, grad, mixed, slope, gains, in_held, back_held, earlier=None):
    outs = [((ROWS, FF), BF16, "any"), ((1, D), F32, "vmem"), ((ROWS, D), F32, "vmem")]
    ins = [(lengths, "smem")]
    ins += [(value, "vmem") for value in (grad, mixed, slope, gains, in_held, back_held)]
    ins, aliases = with_earlier(ins, outs, earlier)
    scratch = [pltpu.VMEM((ROWS, FF), BF16), pltpu.SemaphoreType.DMA((1,))]
    kernel = functools.partial(expand_back_kernel, len(aliases), lower, item)
    return call(kernel, "expand_back", ins, outs, scratch, aliases, 1 << 32)


def attend_back_kernel(
    n_alias, lower, item, lengths, feed_ref, middle, qkv_rows, probs, gain_ref, qkv_held, proj_held, *rest
):
    outer_out, gain_out, end_out, outer, high, sems = rest[n_alias:]
    place = Place(lengths)
    rows_ref = feed_ref.at[pl.ds(item * ROWS, ROWS)] if lower else feed_ref

    @pl.when(place.is_lower == lower)
    def _():
        sender = Sender(sems)
        branch = middle[...].astype(BF16)
        outer[:, pl.ds(3 * D, D)] = branch
        grad_context = dot_nt(branch, proj_held[...]).astype(BF16)
        scale = jnp.asarray(HEAD_DIM**-0.5, BF16)
        for pair in range(HEADS // 2):
            queries = qkv_rows[:, pl.ds(pair * 128, 128)] * scale
            keys = qkv_rows[:, pl.ds(D + pair * 128, 128)] * scale
            values = qkv_rows[:, pl.ds(2 * D + pair * 128, 128)]
            context = grad_context[:, pair * 128 : (pair + 1) * 128]
            grad_q = grad_k = grad_v = None
            for which in (0, 1):
                weight = probs[2 * pair + which]
                context_half = lane_half(context, which)
                grad_probs = dot_nt(context_half, values)
                weight_wide = weight.astype(F32)
                product = weight_wide * grad_probs
                row_total = jnp.sum(product, axis=-1, keepdims=True)
                grad_scores = (product - weight_wide * row_total).astype(BF16)
                term_v = dot_tn(weight, context_half)
                term_q = dot_nn(grad_scores, lane_half(keys, which))
                term_k = dot_tn(grad_scores, lane_half(queries, which))
                grad_q = term_q if grad_q is None else grad_q + term_q
                grad_k = term_k if grad_k is None else grad_k + term_k
                grad_v = term_v if grad_v is None else grad_v + term_v
            outer[:, pl.ds(pair * 128, 128)] = grad_q.astype(BF16)
            outer[:, pl.ds(D + pair * 128, 128)] = grad_k.astype(BF16)
            outer[:, pl.ds(2 * D + pair * 128, 128)] = grad_v.astype(BF16)
        sender.send(outer, outer_out)
        grad_normed = dot_nt(outer[:, pl.ds(0, 3 * D)], qkv_held[...])
        hidden = rows_ref[...].astype(F32)
        grad_hidden, gain_out[...] = norm_back(grad_normed, hidden, gain_ref[0:1])
        if lower:
            high[...] = middle[...] + grad_hidden
            sender.send(high, end_out.at[pl.ds(item * ROWS, ROWS)])
        else:
            end_out[...] = (middle[...] + grad_hidden).astype(BF16)
        sender.finish()


def attend_back(
    lower, item, lengths, rows, middle, qkv, probs, gains, qkv_held, proj_held, earlier=None
):
    outs = [
        ((ROWS, 4 * D), BF16, "any"),
        ((1, D), F32, "vmem"),
        ((MB * ROWS, D), F32, "any") if lower else ((ROWS, D), BF16, "vmem"),
    ]
    ins = [(lengths, "smem")]
    ins += [(value, "vmem") for value in (rows, middle, qkv, probs, gains, qkv_held, proj_held)]
    ins, aliases = with_earlier(ins, outs, earlier)
    scratch = [
        pltpu.VMEM((ROWS, 4 * D), BF16),
        pltpu.VMEM((ROWS, D), F32),
        pltpu.SemaphoreType.DMA((2,)),
    ]
    kernel = functools.partial(attend_back_kernel, len(aliases), lower, item)
    return call(kernel, "attend_back", ins, outs, scratch, aliases, 1 << 32)


def expert_rows(place, index, expert, value, live_only=False):
    item, partner = index % MB, index >= MB
    row = lax.broadcasted_iota(jnp.int32, (ROWS, 1), 0)
    first, second = place.experts(item, partner)
    mine = jnp.where(row < IMAGE_ROWS, first, second) == expert
    if live_only:
        mine = mine & (row < place.live(item, partner))
    return jnp.where(mine, value.astype(F32), 0.0)


def back_grads_kernel(lengths, *refs):
    place = Place(lengths)
    actives, grads, out, flipped = refs[:4], refs[4:8], refs[8], refs[9]

    @pl.when(pl.program_id(0) == 0)
    def _():
        for expert in (0, 1):
            for item in range(4):
                value = expert_rows(place, item, expert, grads[item][...], live_only=True)
                flipped[expert, :, pl.ds(item * ROWS, ROWS)] = value.T.astype(BF16)

    for expert in (0, 1):
        total = None
        for item in range(4):
            term = dot_nn(flipped[expert, :, pl.ds(item * ROWS, ROWS)], actives[item][...])
            total = term if total is None else total + term
        out[expert] = total.astype(BF16)


def back_grads(lengths, kept, grads):
    width = 512
    return pl.pallas_call(
        back_grads_kernel,
        grid=(FF_HALF // width,),
        out_shape=jax.ShapeDtypeStruct((2, D, FF_HALF), BF16),
        in_specs=[pl.BlockSpec(memory_space=pltpu.SMEM)]
        + [pl.BlockSpec((ROWS, width), lambda step: (0, step))] * 4
        + [pl.BlockSpec((ROWS, D), lambda step: (0, 0))] * 4,
        out_specs=pl.BlockSpec((2, D, width), lambda step: (0, 0, step)),
        scratch_shapes=[pltpu.VMEM((2, D, 4 * ROWS), BF16)],
        compiler_params=pltpu.CompilerParams(vmem_limit_bytes=2 * VMEM_BYTES),
        cost_estimate=pl.CostEstimate(
            flops=4 * D * FF_HALF * 4 * ROWS, bytes_accessed=16 << 20, transcendentals=0
        ),
        name="back_grads",
    )(lengths, *kept, *grads)


def in_grads_kernel(parts, lengths, *refs):
    place = Place(lengths)
    seconds, inners, out, flipped = refs[:4], refs[4:8], refs[8], refs[9]

    @pl.when(pl.program_id(0) == 0)
    def _():
        for expert in (0, 1):
            for item in range(4):
                value = expert_rows(place, item, expert, seconds[item][...])
                flipped[expert, :, pl.ds(item * ROWS, ROWS)] = value.T.astype(BF16)

    width = D // parts
    for expert in (0, 1):
        total = None
        for item in range(4):
            term = dot_nn(flipped[expert, :, pl.ds(item * ROWS, ROWS)], inners[item][...])
            total = term if total is None else total + term
        for part in range(parts):
            out[part, expert] = total[:, part * width : (part + 1) * width].astype(BF16)


def in_grads(lengths, kept, inners, blocks):
    parts = max(1, blocks * D // FF)
    width = D // parts
    return pl.pallas_call(
        functools.partial(in_grads_kernel, parts),
        grid=(FF // D,),
        out_shape=jax.ShapeDtypeStruct((FF // width, 2, HALF, width), BF16),
        in_specs=[pl.BlockSpec(memory_space=pltpu.SMEM)]
        + [pl.BlockSpec((ROWS, HALF), lambda step: (0, FF_HALF // HALF))] * 4
        + [pl.BlockSpec((ROWS, D), lambda step: (0, step))] * 4,
        out_specs=pl.BlockSpec((parts, 2, HALF, width), lambda step: (step, 0, 0, 0)),
        scratch_shapes=[pltpu.VMEM((2, HALF, 4 * ROWS), BF16)],
        compiler_params=pltpu.CompilerParams(vmem_limit_bytes=VMEM_BYTES),
        cost_estimate=pl.CostEstimate(
            flops=4 * D * FF_HALF * 4 * ROWS, bytes_accessed=16 << 20, transcendentals=0
        ),
        name="in_grads",
    )(lengths, *kept, *inners)


def outer_grads_kernel(*refs):
    lefts, outers, out = refs[:4], refs[4:8], refs[8]
    total = None
    for item in range(4):
        term = dot_tn(outers[item][...], lefts[item][...])
        total = term if total is None else total + term
    out[...] = total.astype(BF16)


def outer_grads(kept, outers):
    return pl.pallas_call(
        outer_grads_kernel,
        grid=(4,),
        out_shape=jax.ShapeDtypeStruct((4 * D, HALF), BF16),
        in_specs=[pl.BlockSpec((ROWS, HALF), lambda step: (0, step // 3))] * 4
        + [pl.BlockSpec((ROWS, D), lambda step: (0, step))] * 4,
        out_specs=pl.BlockSpec((D, HALF), lambda step: (step, 0)),
        compiler_params=pltpu.CompilerParams(vmem_limit_bytes=VMEM_BYTES),
        cost_estimate=pl.CostEstimate(
            flops=8 * D * HALF * 4 * ROWS, bytes_accessed=16 << 20, transcendentals=0
        ),
        name="outer_grads",
    )(*kept, *outers)


def swapped(block, axis, bit):
    count = lax.axis_size(axis)
    route = [(place, place ^ 1 << bit) for place in range(count)]
    return lax.ppermute(block, axis, route)


def passed_along(value, steps):
    count = lax.axis_size("section")
    first, last = (max(0, -steps), min(count, count - steps))
    route = [(source, source + steps) for source in range(first, last)]
    return lax.ppermute(value, "section", route)


def split_bit(stacked, bit):
    here = (lax.axis_index("dp") >> bit) & 1
    mine = lax.dynamic_index_in_dim(stacked, here, 0, keepdims=False)
    theirs = lax.dynamic_index_in_dim(stacked, 1 - here, 0, keepdims=False)
    return mine, theirs


def added(left, right):
    return left.astype(F32) + right.astype(F32)


def step_order(sizes, ready, orders):
    free, done, ends = {}, [0] * len(sizes), []
    since = list(ready)
    while True:
        choices = []
        for place, order in enumerate(orders):
            if done[place] < len(order):
                bit = order[done[place]]
                link = min(bit, 1)
                choices.append((max(since[place], free.get(link, 0.0)), place, bit, link))
        if not choices:
            return sorted(ends)
        start, place, bit, link = min(choices)
        done[place] += 1
        stop = start + sizes[place] / 2 ** done[place] * (1.5 if bit > 1 else 1.0)
        free[link] = stop
        since[place] = stop + 4.0
        ends.append((since[place], place, done[place] - 1))


def after(value, *earlier):
    return lax.optimization_barrier((value, earlier))[0]


def scattered_sums(pieces, ready, orders):
    waiting = []
    coming = []
    for piece, since, order in zip(pieces, ready, orders):
        mine, theirs = split_bit(piece, order[0])
        waiting.append([mine, swapped(theirs, "dp", order[0])])
        coming.append((since, theirs))
    results = [None] * len(pieces)
    last = []
    sizes = [piece.size / (1 << 20) * 43.0 for piece in pieces]
    for end, place, step in step_order(sizes, ready, orders):
        mine, got = waiting[place]
        started = [theirs for since, theirs in coming if since <= end]
        coming = [(since, theirs) for since, theirs in coming if since > end]
        mine = after(mine, *last, *started)
        total = added(mine, got)
        order = orders[place]
        if step == len(order) - 1:
            results[place] = total
            last = [total]
        else:
            mine, theirs = split_bit(total.astype(BF16), order[step + 1])
            waiting[place] = [mine, swapped(theirs, "dp", order[step + 1])]
            last = [theirs]
    return results


def by_bits(stacked, order):
    bits = len(order)
    split = stacked.reshape((2,) * bits + stacked.shape[1:])
    return split.transpose(tuple(bits - 1 - bit for bit in order) + tuple(range(bits, split.ndim)))


def shards(feeds, text_lengths, norm_gains, qkv_weight, out_weight, expert_in, expert_out):
    n_dp = lax.axis_size("dp")
    bits = n_dp.bit_length() - 1
    section_pos = lax.axis_index("section")
    is_lower = section_pos < 2
    pos = section_pos % 2

    gains = joined_gains(norm_gains[0], swapped(norm_gains[0], "section", 0))
    own = [qkv_weight[0], out_weight[0]]
    other = [swapped(part, "section", 0) for part in own]
    held = joined_halves(own, other)
    in_other = swapped(after(expert_in[0], *other), "section", 0)
    back_other = swapped(after(expert_out[0], in_other), "section", 0)

    attended, expanded = [], []
    rows = feeds
    for item in range(MB):
        attended.append(attend(True, item, text_lengths, rows, gains, *held))
        rows = after(feeds, attended[-1][2])
    earlier = attended[-1][2]
    held += joined_halves([expert_in[0]], [after(in_other, earlier)])
    held += joined_halves([expert_out[0]], [after(back_other, earlier)])
    for item in range(MB):
        mixed = after(attended[item][2], earlier)
        expanded.append(expand(True, item, text_lengths, mixed, gains, *held[2:]))
        earlier = expanded[-1][3]
    passed = [passed_along(expanded[item][3], 2) for item in range(MB)]
    experts_back, heads_back, ups = [], [], []
    ends = ()
    for item in range(MB):
        rows = after(passed[item], earlier)
        attended[item] = attend(
            False, item, text_lengths, rows, gains, *held[:2], attended[item]
        )
        mixed = attended[item][2]
        buffers = tuple(expanded[item][:3]) + ends
        expanded[item] = expand(False, item, text_lengths, mixed, gains, *held[2:], buffers)
        slope = expanded[item][0]
        ends = (expanded[item][3],)
        experts_back.append(
            expand_back(False, item, text_lengths, feeds, mixed, slope, gains, *held[2:])
        )
        middle = experts_back[item][2]
        heads_back.append(
            attend_back(
                False, item, text_lengths, rows, middle, *attended[item][:2], gains, *held[:2]
            )
        )
        earlier = heads_back[item][2]
        ups.append(passed_along(earlier, -2))
    ends = ends[0]
    outer_lefts = [attended[item][3] for item in range(MB)]
    outer_lefts += [swapped(attended[item][4], "section", 0) for item in range(MB)]
    deep_lefts = [expanded[item][1] for item in range(MB)]
    deep_lefts += [swapped(expanded[item][2], "section", 0) for item in range(MB)]
    upward = tuple(range(bits))
    orders = [upward[1:] + upward[:1]] + [upward] * 4
    grads_low, inners, inners_other, outers, outers_other = [], [], [], [], []
    pieces = []
    for item in range(MB):
        up = after(ups[item], earlier)
        grads_low.append(jnp.where(is_lower, up, feeds[item * ROWS : (item + 1) * ROWS]))
        grad = up
        if item == MB - 1:
            grads_all = grads_low + [swapped(part, "section", 0) for part in grads_low]
            back_full = back_grads(text_lengths, deep_lefts, grads_all)
            back_split = back_full.reshape(2, n_dp, D // n_dp, FF_HALF)
            pieces = [by_bits(back_split[expert], orders[expert]) for expert in (0, 1)]
            grad = after(grad, *[split_bit(pieces[k], orders[k][0])[1] for k in (0, 1)])
        mixed, slope = attended[item][2], expanded[item][0]
        part = expand_back(
            True, item, text_lengths, grad, mixed, slope, gains, *held[2:], experts_back[item][:2]
        )
        experts_back[item] = part
        inners.append(part[0])
        inners_other.append(swapped(part[0], "section", 0))
        middle = part[2]
        if item == MB - 1:
            blocked = n_dp if FF // n_dp % 128 == 0 else 1
            in_full = in_grads(text_lengths, deep_lefts, inners + inners_other, blocked)
            middle = after(middle, in_full)
        part = attend_back(
            True,
            item,
            text_lengths,
            feeds,
            middle,
            *attended[item][:2],
            gains,
            *held[:2],
            tuple(heads_back[item][:2]) + (ends,),
        )
        heads_back[item] = part
        earlier = ends = part[2]
        outers.append(part[0])
        outers_other.append(swapped(part[0], "section", 0))
    outer_full = outer_grads(outer_lefts, outers + outers_other)

    gain_sum = jnp.concatenate(
        [
            heads_back[0][1] + heads_back[1][1],
            experts_back[0][1] + experts_back[1][1],
        ],
        axis=0,
    )
    gain_halves = gain_sum.reshape(2, 2, HALF)
    gain_own = lax.dynamic_index_in_dim(gain_halves, pos, 1, keepdims=False)
    gain_theirs = lax.dynamic_index_in_dim(gain_halves, 1 - pos, 1, keepdims=False)
    gain_own = gain_own + swapped(gain_theirs, "section", 0)
    gain_stack = gain_own.reshape(2, n_dp, HALF // n_dp).transpose(1, 0, 2)
    gain_stack = gain_stack.reshape(n_dp, 1, 2 * HALF // n_dp)
    gain_stack = jnp.pad(gain_stack, ((0, 0), (0, 15), (0, HALF - 2 * HALF // n_dp)))

    if in_full.shape[0] == n_dp:
        in_split = [in_full[:, expert] for expert in (0, 1)]
    else:
        wide = in_full.transpose(1, 2, 0, 3).reshape(2, HALF, n_dp, FF // n_dp)
        in_split = [wide[expert].transpose(1, 0, 2) for expert in (0, 1)]
    pieces += [by_bits(part, order) for part, order in zip(in_split, orders[2:])]
    last = jnp.concatenate(
        [
            outer_full[: 3 * D].reshape(n_dp, 3 * D // n_dp, HALF),
            outer_full[3 * D :].reshape(n_dp, D // n_dp, HALF),
            gain_stack.astype(BF16),
        ],
        axis=1,
    )
    pieces.append(by_bits(last, orders[4]))
    sums = scattered_sums(pieces, (0.0, 0.0, 20.0, 20.0, 35.0), orders)
    qkv_rows, proj_rows = 3 * D // n_dp, D // n_dp
    qkv_sum = sums[4][:qkv_rows].T
    proj_sum = sums[4][qkv_rows : qkv_rows + proj_rows].T
    gain_total = sums[4][qkv_rows + proj_rows, : 2 * HALF // n_dp].reshape(2, HALF // n_dp)
    back_sum = jnp.stack([sums[0].T, sums[1].T])
    in_sum = jnp.stack([sums[2], sums[3]])
    return (
        ends,
        gain_total[None],
        qkv_sum[None],
        proj_sum[None],
        in_sum[None],
        back_sum[None],
    )


def solution(mesh):
    return jax.shard_map(
        shards,
        mesh=mesh,
        in_specs=(
            P(("dp", "section"), None),
            P("dp"),
            P("section", None, None),
            P("section", None, None),
            P("section", None, None),
            P("section", None, None, None),
            P("section", None, None, None),
        ),
        out_specs=(
            P(("dp", "section"), None),
            P("section", None, "dp"),
            P("section", None, "dp"),
            P("section", None, "dp"),
            P("section", None, None, "dp"),
            P("section", None, None, "dp"),
        ),
        check_vma=False,
    )
```

```python
import functools

import jax
import jax.numpy as jnp
from jax import lax
from jax.experimental import pallas as pl
from jax.experimental.pallas import tpu as pltpu
from jax.sharding import PartitionSpec as P

D = 768
HALF = D // 2
HEADS = 12
FF = 3072
FF_HALF = FF // 2
HEAD_DIM = 64
IMAGE_ROWS = 197
ROWS = 256
MB = 2
KEPT = FF_HALF + 3 * HALF
TAIL = 192

EPSILON = 1e-05
MASKED = -1e30
F32 = jnp.float32
BF16 = jnp.bfloat16
VMEM_BYTES = 10 * 1024 * 1024


def cost(size):
    return pl.CostEstimate(flops=size << 20, bytes_accessed=1 << 10, transcendentals=0)


def dot_nn(left, right):
    return lax.dot_general(left, right, (((1,), (0,)), ((), ())), preferred_element_type=F32)


def dot_nt(left, right):
    return lax.dot_general(left, right, (((1,), (1,)), ((), ())), preferred_element_type=F32)


def dot_tn(left, right):
    return lax.dot_general(left, right, (((0,), (0,)), ((), ())), preferred_element_type=F32)


def norm_parts(hidden):
    centred = hidden - jnp.mean(hidden, axis=-1, keepdims=True)
    spread = jnp.mean(centred * centred, axis=-1, keepdims=True)
    inverse = lax.rsqrt(spread + EPSILON)
    return centred * inverse, inverse


def norm_back(grad, hidden, gain_row):
    unit, inverse = norm_parts(hidden)
    gain_grad = jnp.sum(grad * unit, axis=0, keepdims=True)
    scaled = grad * gain_row
    mean_plain = jnp.mean(scaled, axis=-1, keepdims=True)
    mean_unit = jnp.mean(scaled * unit, axis=-1, keepdims=True)
    return inverse * (scaled - mean_plain - unit * mean_unit), gain_grad


def gelu_pair(values):
    size = jnp.abs(values)
    denom = 1.0 + (0.3275911 * 0.7071067811865476) * size
    rough = pl.reciprocal(denom, approx=True)
    t = rough * (2.0 - denom * rough)
    poly = 0.5 * 1.061405429
    for factor in (-1.453152027, 1.421413741, -0.284496736, 0.254829592):
        poly = poly * t + 0.5 * factor
    bell = jnp.exp(values * values * -0.5)
    upper_tail = poly * t * bell
    cdf = jnp.where(values < 0, upper_tail, 1.0 - upper_tail)
    return values * cdf, cdf + values * bell * 0.3989422804014327


def lane_half(value, which):
    lanes = lax.broadcasted_iota(jnp.int32, value.shape, 1)
    picked = lanes < HEAD_DIM if which == 0 else lanes >= HEAD_DIM
    return jnp.where(picked, value, jnp.zeros_like(value))


def call(kernel, name, ins, outs, scratch, aliases=None, size=1):
    spaces = {"vmem": pltpu.VMEM, "smem": pltpu.SMEM, "any": pl.ANY, "hbm": pltpu.HBM}
    shapes = [
        pltpu.VMEM(shape, kind) if space == "vmem" else jax.ShapeDtypeStruct(shape, kind)
        for shape, kind, space in outs
    ]
    return pl.pallas_call(
        kernel,
        out_shape=shapes,
        in_specs=[pl.BlockSpec(memory_space=spaces[space]) for _, space in ins],
        out_specs=[pl.BlockSpec(memory_space=spaces[space]) for _, _, space in outs],
        input_output_aliases=aliases or {},
        scratch_shapes=scratch,
        compiler_params=pltpu.CompilerParams(vmem_limit_bytes=VMEM_BYTES),
        cost_estimate=cost(size),
        name=name,
    )(
        *[
            pltpu.with_memory_space_constraint(value, pltpu.HBM) if space == "hbm" else value
            for value, space in ins
        ]
    )


class Place:
    def __init__(self, lengths):
        section = lax.axis_index("section")
        self.lengths = lengths
        self.is_lower = section < 2
        self.pos = section % 2

    def length(self, item, partner=False):
        pos = 1 - self.pos if partner else self.pos
        return self.lengths[pos * MB + item]

    def live(self, item, partner=False):
        return IMAGE_ROWS + self.length(item, partner)

    def experts(self, item, partner=False):
        kind = jnp.where(self.length(item, partner) > 0, 1, 0)
        return jnp.where(self.is_lower, 0, kind), jnp.where(self.is_lower, 1, kind)


def with_earlier(ins, outs, earlier):
    aliases = {}
    for number, value in (earlier or {}).items():
        aliases[len(ins)] = number
        ins = ins + [(value, outs[number][2])]
    return ins, aliases


class Sender:
    def __init__(self, sems):
        self.sems = sems
        self.sent = []

    def send(self, source, target):
        copy = pltpu.make_async_copy(source, target, self.sems.at[len(self.sent)])
        copy.start()
        self.sent.append(copy)

    def finish(self):
        for copy in self.sent:
            copy.wait()


def join_kernel(count, *refs):
    own, other, joined, sems = refs[:count], refs[count : 2 * count], refs[2 * count : -1], refs[-1]
    pos = lax.axis_index("section") % 2
    sender = Sender(sems)
    for mine, theirs, whole in zip(own, other, joined):
        depth = mine.shape[-2]
        for source, at in ((mine, pos), (theirs, 1 - pos)):
            rows = pl.ds(pl.multiple_of(at * depth, depth), depth)
            if len(whole.shape) == 2:
                sender.send(source, whole.at[rows])
            else:
                for expert in range(whole.shape[0]):
                    sender.send(source.at[expert], whole.at[expert, rows])
    sender.finish()


def joined_halves(own, other):
    outs = []
    for part in own:
        shape = part.shape[:-2] + (2 * part.shape[-2], part.shape[-1])
        outs.append((shape, BF16, "vmem"))
    return call(
        functools.partial(join_kernel, len(own)),
        "joined_halves",
        [(value, "hbm") for value in own] + [(value, "any") for value in other],
        outs,
        [pltpu.SemaphoreType.DMA((4 * len(own),))],
    )


def gains_kernel(own, other, gains):
    first = lax.axis_index("section") % 2 == 0
    mine, theirs = own[...].astype(F32), other[...].astype(F32)
    gains[:, pl.ds(0, HALF)] = jnp.where(first, mine, theirs)
    gains[:, pl.ds(HALF, HALF)] = jnp.where(first, theirs, mine)


def joined_gains(own, other):
    return call(
        gains_kernel, "joined_gains", [(own, "vmem"), (other, "vmem")], [((2, D), F32, "vmem")], []
    )[0]


def gain_sums_kernel(*refs):
    heads, experts, (keep, send) = refs[:MB], refs[MB : 2 * MB], refs[2 * MB :]
    own, other = places(lax.axis_index("section") % 2, HALF)
    for row, parts in enumerate((heads, experts)):
        for columns, out in ((own, keep), (other, send)):
            out[row : row + 1] = sum(part[:, columns] for part in parts)


def gain_sums(heads, experts):
    ins = [(value, "vmem") for value in heads + experts]
    return call(gain_sums_kernel, "gain_sums", ins, [((2, HALF), F32, "vmem")] * 2, [])


def places(pos, size):
    return (
        pl.ds(pl.multiple_of(pos * size, size), size),
        pl.ds(pl.multiple_of((1 - pos) * size, size), size),
    )


def attend_kernel(n_alias, lower, item, lengths, feed_ref, gain_ref, qkv_held, proj_held, *rest):
    qkv_rows, probs, mixed, keep_out, send_out, left_rows, sems = rest[n_alias:]
    place = Place(lengths)
    live = place.live(item)
    rows_ref = feed_ref.at[pl.ds(item * ROWS, ROWS)] if lower else feed_ref

    @pl.when(place.is_lower == lower)
    def _():
        sender = Sender(sems)
        own, other = places(place.pos, HALF)

        def send_halves(place):
            to = (pl.ds(item * ROWS, ROWS), pl.ds(FF_HALF + (1 + place) * HALF, HALF))
            sender.send(left_rows.at[place, :, own], keep_out.at[to])
            sender.send(left_rows.at[place, :, other], send_out.at[to])

        hidden = rows_ref[...].astype(F32)
        normed = (norm_parts(hidden)[0] * gain_ref[0:1]).astype(BF16)
        left_rows[0] = normed
        send_halves(0)
        for part in range(3):
            columns = pl.ds(part * D, D)
            qkv_rows[:, columns] = dot_nn(normed, qkv_held[:, columns]).astype(BF16)
        keys_live = lax.broadcasted_iota(jnp.int32, (ROWS, ROWS), 1) < live
        for pair in range(HEADS // 2):
            queries = qkv_rows[:, pl.ds(pair * 128, 128)] * jnp.asarray(HEAD_DIM**-0.5, BF16)
            keys = qkv_rows[:, pl.ds(D + pair * 128, 128)]
            values = qkv_rows[:, pl.ds(2 * D + pair * 128, 128)]
            context = None
            for which in (0, 1):
                scores = dot_nt(lane_half(queries, which), keys)
                scores = jnp.where(keys_live, scores, MASKED)
                shifted = jnp.exp(scores - jnp.max(scores, axis=-1, keepdims=True))
                total = jnp.sum(shifted, axis=-1, keepdims=True)
                weight = (shifted * (1.0 / total)).astype(BF16)
                probs[2 * pair + which] = weight
                term = dot_nn(weight, lane_half(values, which))
                context = term if context is None else context + term
            left_rows[1, :, pl.ds(pair * 128, 128)] = context.astype(BF16)
        send_halves(1)
        mixed[...] = rows_ref[...].astype(F32) + dot_nn(left_rows[1], proj_held[...])
        sender.finish()


def attend(lower, item, lengths, rows, gains, qkv_held, proj_held, earlier=None):
    outs = [
        ((ROWS, 3 * D), BF16, "vmem"),
        ((HEADS, ROWS, ROWS), BF16, "vmem"),
        ((ROWS, D), F32, "vmem"),
        ((MB * ROWS, KEPT), BF16, "any"),
        ((MB * ROWS, KEPT), BF16, "any"),
    ]
    ins = [(lengths, "smem"), (rows, "vmem"), (gains, "vmem")]
    ins += [(qkv_held, "vmem"), (proj_held, "vmem")]
    ins, aliases = with_earlier(ins, outs, earlier)
    scratch = [pltpu.VMEM((2, ROWS, D), BF16), pltpu.SemaphoreType.DMA((4,))]
    kernel = functools.partial(attend_kernel, len(aliases), lower, item)
    return call(kernel, "attend", ins, outs, scratch, aliases)


def expand_kernel(n_alias, lower, item, lengths, mixed, gain_ref, in_held, back_held, *rest):
    slope, keep_out, send_out, end_out, second_rows, active, high, sems = rest[n_alias:]
    place = Place(lengths)
    first, second = place.experts(item)

    @pl.when(place.is_lower == lower)
    def _():
        sender = Sender(sems)
        own, other = places(place.pos, HALF)
        own_deep, other_deep = places(place.pos, FF_HALF)
        normed = (norm_parts(mixed[...])[0] * gain_ref[1:2]).astype(BF16)
        second_rows[...] = normed
        rows = pl.ds(item * ROWS, ROWS)
        place_b = pl.ds(FF_HALF, HALF)
        sender.send(second_rows.at[:, own], keep_out.at[rows, place_b])
        sender.send(second_rows.at[:, other], send_out.at[rows, place_b])
        for part in range(4):
            columns = pl.ds(part * D, D)
            value, derivative = gelu_pair(dot_nn(normed, in_held[first, :, columns]))
            active[:, columns] = value.astype(BF16)
            slope[:, columns] = derivative.astype(BF16)
        high[...] = mixed[...] + dot_nn(active[...], back_held[first])

        def language_rows():
            tail = pl.ds(TAIL, ROWS - TAIL)
            later = lax.broadcasted_iota(jnp.int32, (ROWS - TAIL, D), 0) >= IMAGE_ROWS - TAIL
            for part in range(4):
                columns = pl.ds(part * D, D)
                value, derivative = gelu_pair(dot_nn(second_rows[tail], in_held[second, :, columns]))
                active[tail, columns] = jnp.where(
                    later, value, active[tail, columns].astype(F32)
                ).astype(BF16)
                slope[tail, columns] = jnp.where(
                    later, derivative, slope[tail, columns].astype(F32)
                ).astype(BF16)
            patched = mixed[tail] + dot_nn(active[tail], back_held[second])
            high[tail] = jnp.where(later, patched, high[tail])

        if lower:
            language_rows()
            end_out[...] = high[...].astype(BF16)
        place_q = pl.ds(0, FF_HALF)
        sender.send(active.at[:, own_deep], keep_out.at[rows, place_q])
        sender.send(active.at[:, other_deep], send_out.at[rows, place_q])
        if not lower:
            sender.send(high, end_out.at[rows])
        sender.finish()


def expand(lower, item, lengths, mixed, gains, in_held, back_held, earlier=None):
    outs = [
        ((ROWS, FF), BF16, "vmem"),
        ((MB * ROWS, KEPT), BF16, "any"),
        ((MB * ROWS, KEPT), BF16, "any"),
        ((ROWS, D), BF16, "vmem") if lower else ((MB * ROWS, D), F32, "any"),
    ]
    ins = [(lengths, "smem"), (mixed, "vmem"), (gains, "vmem")]
    ins += [(in_held, "vmem"), (back_held, "vmem")]
    ins, aliases = with_earlier(ins, outs, earlier)
    scratch = [
        pltpu.VMEM((ROWS, D), BF16),
        pltpu.VMEM((ROWS, FF), BF16),
        pltpu.VMEM((ROWS, D), F32),
        pltpu.SemaphoreType.DMA((5,)),
    ]
    kernel = functools.partial(expand_kernel, len(aliases), lower, item)
    return call(kernel, "expand", ins, outs, scratch, aliases)


def expand_back_kernel(
    n_alias, lower, item, lengths, end_ref, mixed, slope, gain_ref, in_held, back_held, *rest
):
    inner_out, gain_out, middle, inner, sems = rest[n_alias:]
    place = Place(lengths)
    first, second = place.experts(item)
    grad_ref = end_ref if lower else end_ref.at[pl.ds(item * ROWS, ROWS)]

    @pl.when(place.is_lower == lower)
    def _():
        sender = Sender(sems)
        is_live = lax.broadcasted_iota(jnp.int32, (ROWS, D), 0) < place.live(item)
        grad = jnp.where(is_live, grad_ref[...].astype(F32), 0.0)
        grad_low = grad.astype(BF16)
        for part in range(4):
            columns = pl.ds(part * D, D)
            grad_active = dot_nt(grad_low, back_held[first, columns])
            inner[:, columns] = (grad_active * slope[:, columns].astype(F32)).astype(BF16)
        middle[...] = dot_nt(inner[...], in_held[first])

        def language_rows():
            tail = pl.ds(TAIL, ROWS - TAIL)
            later = lax.broadcasted_iota(jnp.int32, (ROWS - TAIL, D), 0) >= IMAGE_ROWS - TAIL
            for part in range(4):
                columns = pl.ds(part * D, D)
                grad_active = dot_nt(grad_low[TAIL:], back_held[second, columns])
                patched = grad_active * slope[tail, columns].astype(F32)
                inner[tail, columns] = jnp.where(
                    later, patched, inner[tail, columns].astype(F32)
                ).astype(BF16)
            patched = dot_nt(inner[tail], in_held[second])
            middle[tail] = jnp.where(later, patched, middle[tail])

        if lower:
            language_rows()
        sender.send(inner, inner_out.at[:, pl.ds(0, FF)])
        grad_mixed, gain_out[...] = norm_back(middle[...], mixed[...], gain_ref[1:2])
        middle[...] = grad + grad_mixed
        sender.finish()


def expand_back(lower, item, lengths, grad, mixed, slope, gains, in_held, back_held, earlier=None):
    size = 1 << 13 if lower and item < MB - 1 else 1
    width = FF if item == MB - 1 else FF + 4 * D
    outs = [((ROWS, width), BF16, "any"), ((1, D), F32, "vmem"), ((ROWS, D), F32, "vmem")]
    ins = [(lengths, "smem")]
    ins += [(value, "vmem") for value in (grad, mixed, slope, gains, in_held, back_held)]
    ins, aliases = with_earlier(ins, outs, earlier)
    scratch = [pltpu.VMEM((ROWS, FF), BF16), pltpu.SemaphoreType.DMA((1,))]
    kernel = functools.partial(expand_back_kernel, len(aliases), lower, item)
    return call(kernel, "expand_back", ins, outs, scratch, aliases, size)


def attend_back_kernel(
    n_alias, lower, item, lengths, feed_ref, middle, qkv_rows, probs, gain_ref, qkv_held, proj_held, *rest
):
    *outer_outs, gain_out, end_out, outer, high, sems = rest[n_alias:]
    place = Place(lengths)
    rows_ref = feed_ref.at[pl.ds(item * ROWS, ROWS)] if lower else feed_ref

    @pl.when(place.is_lower == lower)
    def _():
        sender = Sender(sems)
        branch = middle[...].astype(BF16)
        outer[:, pl.ds(3 * D, D)] = branch
        grad_context = dot_nt(branch, proj_held[...]).astype(BF16)
        scale = jnp.asarray(HEAD_DIM**-0.5, BF16)
        for pair in range(HEADS // 2):
            queries = qkv_rows[:, pl.ds(pair * 128, 128)] * scale
            keys = qkv_rows[:, pl.ds(D + pair * 128, 128)] * scale
            values = qkv_rows[:, pl.ds(2 * D + pair * 128, 128)]
            context = grad_context[:, pair * 128 : (pair + 1) * 128]
            grad_q = grad_k = grad_v = None
            for which in (0, 1):
                weight = probs[2 * pair + which]
                context_half = lane_half(context, which)
                grad_probs = dot_nt(context_half, values)
                weight_wide = weight.astype(F32)
                product = weight_wide * grad_probs
                row_total = jnp.sum(product, axis=-1, keepdims=True)
                grad_scores = (product - weight_wide * row_total).astype(BF16)
                term_v = dot_tn(weight, context_half)
                term_q = dot_nn(grad_scores, lane_half(keys, which))
                term_k = dot_tn(grad_scores, lane_half(queries, which))
                grad_q = term_q if grad_q is None else grad_q + term_q
                grad_k = term_k if grad_k is None else grad_k + term_k
                grad_v = term_v if grad_v is None else grad_v + term_v
            outer[:, pl.ds(pair * 128, 128)] = grad_q.astype(BF16)
            outer[:, pl.ds(D + pair * 128, 128)] = grad_k.astype(BF16)
            outer[:, pl.ds(2 * D + pair * 128, 128)] = grad_v.astype(BF16)
        if len(outer_outs) == 1:
            sender.send(outer, outer_outs[0].at[:, pl.ds(FF, 4 * D)])
        else:
            for part, target in enumerate(outer_outs):
                sender.send(outer.at[:, pl.ds(2 * part * D, 2 * D)], target)
        grad_normed = dot_nt(outer[:, pl.ds(0, 3 * D)], qkv_held[...])
        hidden = rows_ref[...].astype(F32)
        grad_hidden, gain_out[...] = norm_back(grad_normed, hidden, gain_ref[0:1])
        if lower:
            high[...] = middle[...] + grad_hidden
            sender.send(high, end_out.at[pl.ds(item * ROWS, ROWS)])
        else:
            end_out[...] = (middle[...] + grad_hidden).astype(BF16)
        sender.finish()


def attend_back(
    lower, item, lengths, rows, middle, qkv, probs, gains, qkv_held, proj_held, earlier=None
):
    size = 1 << 13 if lower and item < MB - 1 else 1
    outs = [((ROWS, FF + 4 * D), BF16, "any")]
    if item == MB - 1:
        outs = [((ROWS, 2 * D), BF16, "any")] * 2
    outs += [
        ((1, D), F32, "vmem"),
        ((MB * ROWS, D), F32, "any") if lower else ((ROWS, D), BF16, "vmem"),
    ]
    ins = [(lengths, "smem")]
    ins += [(value, "vmem") for value in (rows, middle, qkv, probs, gains, qkv_held, proj_held)]
    ins, aliases = with_earlier(ins, outs, earlier)
    scratch = [
        pltpu.VMEM((ROWS, 4 * D), BF16),
        pltpu.VMEM((ROWS, D), F32),
        pltpu.SemaphoreType.DMA((3,)),
    ]
    kernel = functools.partial(attend_back_kernel, len(aliases), lower, item)
    return call(kernel, "attend_back", ins, outs, scratch, aliases, size)


def expert_rows(place, item, partner, expert, live_only=False):
    row = lax.broadcasted_iota(jnp.int32, (1, ROWS), 1)
    first, second = place.experts(item, partner)
    mine = jnp.where(row < IMAGE_ROWS, first, second) == expert
    if live_only:
        mine = mine & (row < place.live(item, partner))
    return mine


def bits_but(*taken):
    count = lax.axis_size("dp").bit_length() - 1
    return [bit for bit in reversed(range(count)) if bit not in taken]


def block_numbers(first_bit):
    here = (lax.axis_index("dp") >> first_bit) & 1
    rest = bits_but(first_bit)
    for number in range(1 << len(rest)):
        where = tuple((number >> (len(rest) - 1 - place)) & 1 for place in range(len(rest)))
        base = sum(value << bit for value, bit in zip(where, rest))
        yield where, base + (here << first_bit), base + ((1 - here) << first_bit)


def write_blocks(total, rows, first_bit, mine, theirs):
    for where, own, other in block_numbers(first_bit):
        own_at = pl.ds(pl.multiple_of(own * rows, rows), rows)
        other_at = pl.ds(pl.multiple_of(other * rows, rows), rows)
        mine[where] = total[own_at].astype(BF16)
        theirs[where] = total[other_at].astype(BF16)


def back_grads_kernel(orders, n_items, lengths, *refs):
    actives, grads, feeds = refs[:n_items], refs[n_items : 2 * n_items], refs[2 * n_items : 2 * n_items + 2]
    outs, (flipped, total) = refs[2 * n_items + 2 : -2], refs[-2:]
    place = Place(lengths)
    tail = ROWS - TAIL
    rows = D // lax.axis_size("dp")

    @pl.when(pl.program_id(0) == 0)
    def _():
        for index in range(n_items):
            item, partner = index % MB, index >= MB
            top = feeds[index // MB][pl.ds(item * ROWS, ROWS)]
            value = jnp.where(place.is_lower, grads[index][...], top).T
            for expert in (0, 1):
                mask = expert_rows(place, item, partner, expert, live_only=True)
                flipped[expert, :, pl.ds(index * ROWS, ROWS)] = jnp.where(mask, value, 0)

    def finished(expert):
        write_blocks(total, rows, orders[expert][0], outs[2 * expert], outs[2 * expert + 1])

    def whole(expert):
        result = None
        for index in range(n_items):
            term = dot_nn(flipped[expert, :, pl.ds(index * ROWS, ROWS)], actives[index][...])
            result = term if result is None else result + term
        total[...] = result

    whole(0)
    finished(0)

    @pl.when(place.is_lower)
    def _():
        left = [
            flipped[1, :, pl.ds(index * ROWS + ROWS // 2, ROWS // 2)] for index in range(n_items)
        ]
        right = [actives[index][pl.ds(ROWS // 2, ROWS // 2)] for index in range(n_items)]
        total[...] = dot_nn(jnp.concatenate(left, axis=1), jnp.concatenate(right, axis=0))

    @pl.when(jnp.logical_not(place.is_lower))
    def _():
        whole(1)

    finished(1)


def halves_shape(block):
    return jax.ShapeDtypeStruct((2,) * len(bits_but(0)) + block, BF16)


def halves_spec(block, place):
    lead = len(bits_but(0))
    return pl.BlockSpec((2,) * lead + block, lambda step: (0,) * lead + place(step))


def by_item(width, count, column, **options):
    return [
        pl.BlockSpec((ROWS, width), lambda step, item=index % MB: (item, column(step)), **options)
        for index in range(count)
    ]


def back_grads(lengths, kept, grads, feeds, orders):
    width = 256
    block = (D // lax.axis_size("dp"), width)
    once = pl.Buffered(1)
    fixed = [pl.BlockSpec((ROWS, D), lambda step: (0, 0), pipeline_mode=once)] * len(kept)
    fixed += [pl.BlockSpec((MB * ROWS, D), lambda step: (0, 0), pipeline_mode=once)] * 2
    results = pl.pallas_call(
        functools.partial(back_grads_kernel, orders, len(kept)),
        grid=(FF_HALF // width,),
        out_shape=[halves_shape((block[0], FF_HALF)) for _ in orders for _ in (0, 1)],
        in_specs=[pl.BlockSpec(memory_space=pltpu.SMEM)]
        + by_item(width, len(kept), lambda step: step)
        + fixed,
        out_specs=[
            halves_spec(block, lambda step: (0, step)) for _ in orders for _ in (0, 1)
        ],
        scratch_shapes=[
            pltpu.VMEM((2, D, len(kept) * ROWS), BF16),
            pltpu.VMEM((D, width), F32),
        ],
        compiler_params=pltpu.CompilerParams(vmem_limit_bytes=VMEM_BYTES),
        cost_estimate=cost(1),
        name="back_grads",
    )(lengths, *kept, *grads, *feeds)
    return [tuple(results[2 * expert : 2 * expert + 2]) for expert in (0, 1)]


def in_grads_kernel(width, n_items, lengths, *refs):
    seconds, inners = refs[:n_items], refs[n_items : 2 * n_items]
    outs, (flipped, total) = refs[2 * n_items : -2], refs[-2:]
    place = Place(lengths)
    half = ROWS // 2
    low_bit = lax.axis_index("dp") % 2

    @pl.when(pl.program_id(0) == 0)
    def _():
        for index in range(n_items):
            item, partner = index % MB, index >= MB
            value = seconds[index][...].T
            for expert in (0, 1):
                mask = expert_rows(place, item, partner, expert)
                flipped[expert, :, pl.ds(index * ROWS, ROWS)] = jnp.where(mask, value, 0)

    def whole(expert):
        result = None
        for index in range(n_items):
            term = dot_nn(flipped[expert, :, pl.ds(index * ROWS, ROWS)], inners[index][...])
            result = term if result is None else result + term
        total[...] = result

    def finished(expert):
        if len(outs) == 2:
            outs[expert][0] = total[...].astype(BF16)
            return
        for out, bit in zip(outs[2 * expert : 2 * expert + 2], (low_bit, 1 - low_bit)):
            out[0] = total[:, pl.ds(pl.multiple_of(bit * width, width), width)].astype(BF16)

    whole(0)
    finished(0)

    @pl.when(place.is_lower)
    def _():
        left = [flipped[1, :, pl.ds(index * ROWS + half, half)] for index in range(n_items)]
        right = [inners[index][pl.ds(half, half)] for index in range(n_items)]
        total[...] = dot_nn(jnp.concatenate(left, axis=1), jnp.concatenate(right, axis=0))

    @pl.when(jnp.logical_not(place.is_lower))
    def _():
        whole(1)

    finished(1)


def in_grads(lengths, kept, inners):
    size = lax.axis_size("dp")
    width = FF // size
    aligned = width % 128 == 0
    columns = 2 * width if aligned else D
    steps = FF // columns
    once = pl.Buffered(1)
    block = (1, HALF, width if aligned else columns)
    count = 4 if aligned else 2
    results = pl.pallas_call(
        functools.partial(in_grads_kernel, width, len(kept)),
        grid=(steps,),
        out_shape=[jax.ShapeDtypeStruct((steps,) + block[1:], BF16)] * count,
        in_specs=[pl.BlockSpec(memory_space=pltpu.SMEM)]
        + by_item(HALF, len(kept), lambda step: FF_HALF // HALF, pipeline_mode=once)
        + [pl.BlockSpec((ROWS, columns), lambda step: (0, step))] * len(inners),
        out_specs=[pl.BlockSpec(block, lambda step: (step, 0, 0))] * count,
        scratch_shapes=[
            pltpu.VMEM((2, HALF, len(kept) * ROWS), BF16),
            pltpu.VMEM((HALF, columns), F32),
        ],
        compiler_params=pltpu.CompilerParams(vmem_limit_bytes=VMEM_BYTES),
        cost_estimate=cost(1),
        name="in_grads",
    )(lengths, *kept, *inners)
    if not aligned:
        whole = [part.transpose(1, 0, 2).reshape(HALF, size, width) for part in results]
        return [by_lowest_bit(part.transpose(1, 0, 2)) for part in whole]
    shape = (2,) * len(bits_but(0)) + block[1:]
    return [tuple(part.reshape(shape) for part in results[2 * e : 2 * e + 2]) for e in (0, 1)]


def outer_grads_kernel(order, *refs):
    lefts, outers, mine, theirs, total = refs[:4], refs[4:10], refs[10], refs[11], refs[12]
    step = pl.program_id(0)
    result = None
    for index in range(4):
        outer = outers[3 * (index // MB)][...]
        if index % MB == MB - 1:
            first, second = outers[3 * (index // MB) + 1 : 3 * (index // MB) + 3]
            outer = jnp.where(step < 2, first[...], second[...])
        term = dot_tn(outer, lefts[index][...])
        result = term if result is None else result + term
    total[pl.ds(pl.multiple_of(step * D, D), D)] = result

    @pl.when(step == 3)
    def _():
        size = lax.axis_size("dp")
        qkv_rows, proj_rows = 3 * D // size, D // size
        for where, *numbers in block_numbers(order[0]):
            for target, number in zip((mine, theirs), numbers):
                at = pl.multiple_of(number * qkv_rows, qkv_rows)
                below = pl.multiple_of(3 * D + number * proj_rows, proj_rows)
                target[where + (pl.ds(0, qkv_rows),)] = total[pl.ds(at, qkv_rows)].astype(BF16)
                target[where + (pl.ds(qkv_rows, proj_rows),)] = total[
                    pl.ds(below, proj_rows)
                ].astype(BF16)


def outer_grads(kept, outers, order):
    block = (4 * D // lax.axis_size("dp"), HALF)
    return pl.pallas_call(
        functools.partial(outer_grads_kernel, order),
        grid=(4,),
        out_shape=[halves_shape(block)] * 2,
        in_specs=by_item(HALF, 4, lambda step: FF_HALF // HALF + 1 + step // 3)
        + [
            pl.BlockSpec((ROWS, D), lambda step: (0, FF // D + step)),
            pl.BlockSpec((ROWS, D), lambda step: (0, jnp.minimum(step, 1))),
            pl.BlockSpec((ROWS, D), lambda step: (0, jnp.maximum(step - 2, 0))),
        ]
        * 2,
        out_specs=[halves_spec(block, lambda step: (0, 0))] * 2,
        scratch_shapes=[pltpu.VMEM((4 * D, HALF), F32)],
        compiler_params=pltpu.CompilerParams(vmem_limit_bytes=2 * VMEM_BYTES),
        cost_estimate=cost(1),
        name="outer_grads",
    )(*kept, *outers)


def swapped(block, axis, bit, among=None):
    among = range(lax.axis_size(axis)) if among is None else among
    return lax.ppermute(block, axis, [(place, place ^ 1 << bit) for place in among])


def per_item(arrays):
    return [array for array in arrays for _ in range(MB)]


def passed_along(value, steps):
    count = lax.axis_size("section")
    first, last = (max(0, -steps), min(count, count - steps))
    route = [(source, source + steps) for source in range(first, last)]
    return lax.ppermute(value, "section", route)


def split_bit(stacked, bit):
    here = (lax.axis_index("dp") >> bit) & 1
    mine = lax.dynamic_index_in_dim(stacked, here, 0, keepdims=False)
    theirs = lax.dynamic_index_in_dim(stacked, 1 - here, 0, keepdims=False)
    return mine, theirs


def added_kernel(left, right, out):
    out[...] = left[...].astype(F32) + right[...].astype(F32)


def added(left, right):
    ins = [(left, "vmem"), (right, "vmem")]
    return call(added_kernel, "added", ins, [(left.shape, F32, "vmem")], [])[0]


def added_halves_kernel(axis, bit, left, right, mine, theirs):
    here = (lax.axis_index("dp") >> bit) & 1
    lead = (slice(None),) * axis
    for out, at in ((mine, lead + (here,)), (theirs, lead + (1 - here,))):
        out[...] = (left[at].astype(F32) + right[at].astype(F32)).astype(BF16)


def added_halves(left, right, axis, bit):
    ins = [(left, "vmem"), (right, "vmem")]
    outs = [(left.shape[:axis] + left.shape[axis + 1 :], BF16, "vmem")] * 2
    kernel = functools.partial(added_halves_kernel, axis, bit)
    return call(kernel, "added_halves", ins, outs, [])


def after(value, *earlier):
    return lax.optimization_barrier((value, earlier))[0]


class Sums:
    def __init__(self):
        self.open = {}
        self.results = {}
        self.last = []

    def begin(self, name, piece, order, taken=()):
        mine, theirs = piece
        self.open[name] = (mine, swapped(theirs, "dp", order[0]), order[1:], (*taken, order[0]))

    def step(self, name):
        mine, got, rest, taken = self.open.pop(name)
        mine = after(mine, *self.last)
        if len(rest) == 0:
            self.results[name] = added(mine, got)
            self.last = [self.results[name]]
            return
        mine, theirs = added_halves(mine, got, bits_but(*taken).index(rest[0]), rest[0])
        self.begin(name, (mine, theirs), rest, taken)
        self.last = [theirs]

    def finish(self, names):
        while any(name in self.open for name in names):
            for name in names:
                if name in self.open:
                    self.step(name)


def by_lowest_bit(stacked):
    bits = lax.axis_size("dp").bit_length() - 1
    split = jnp.moveaxis(stacked.reshape((2,) * bits + stacked.shape[1:]), bits - 1, 0)
    return split_bit(split, 0)


def shards(feeds, text_lengths, norm_gains, qkv_weight, out_weight, expert_in, expert_out):
    n_dp = lax.axis_size("dp")
    bits = n_dp.bit_length() - 1
    pos = lax.axis_index("section") % 2

    gains_other = swapped(norm_gains[0], "section", 0)
    gains = joined_gains(norm_gains[0], gains_other)
    own = [qkv_weight[0], out_weight[0]]
    other = [swapped(part, "section", 0) for part in own]
    held = joined_halves(own, other)
    in_other = swapped(after(expert_in[0], gains_other, *other), "section", 0)
    back_other = swapped(after(expert_out[0], gains_other, *other), "section", 0)

    attended, expanded = [], []
    rows, lefts = feeds, {}
    for item in range(MB):
        attended.append(attend(True, item, text_lengths, rows, gains, *held, lefts))
        earlier = attended[-1][2]
        rows = after(feeds, earlier)
        lefts = dict(zip((3, 4), attended[-1][3:]))
    held += joined_halves([expert_in[0]], [after(in_other, earlier)])
    held += joined_halves([expert_out[0]], [after(back_other, earlier)])
    deep = {1: lefts[3], 2: lefts[4]}
    for item in range(MB):
        mixed = after(attended[item][2], earlier)
        expanded.append(expand(True, item, text_lengths, mixed, gains, *held[2:], deep))
        earlier = expanded[-1][3]
        deep = dict(zip((1, 2), expanded[-1][1:3]))
    passed = [passed_along(expanded[item][3], 2) for item in range(MB)]
    feeds_pair = [feeds, swapped(after(feeds, earlier), "section", 0, (2, 3))]
    experts_back, heads_back, ups = [], [], []
    for item in range(MB):
        rows = after(passed[item], earlier, *feeds_pair[1:])
        lefts = dict(enumerate(attended[item][:3])) | {3: deep[1], 4: deep[2]}
        attended[item] = attend(False, item, text_lengths, rows, gains, *held[:2], lefts)
        mixed = attended[item][2]
        deep |= {0: expanded[item][0], 1: attended[item][3], 2: attended[item][4]}
        expanded[item] = expand(False, item, text_lengths, mixed, gains, *held[2:], deep)
        slope = expanded[item][0]
        deep = dict(enumerate(expanded[item]))
        experts_back.append(
            expand_back(False, item, text_lengths, feeds, mixed, slope, gains, *held[2:])
        )
        middle = experts_back[item][-1]
        wide = {} if item == MB - 1 else {0: experts_back[item][0]}
        heads_back.append(
            attend_back(
                False, item, text_lengths, rows, middle, *attended[item][:2], gains, *held[:2], wide
            )
        )
        earlier = heads_back[item][-1]
        ups.append(passed_along(earlier, -2))
    ends = deep[3]
    left_sent = after(deep[2], earlier)
    lefts = per_item([deep[1], swapped(left_sent, "section", 0)])

    upward = tuple(range(bits))
    back_orders = [upward[1:] + upward[:1], upward]

    def lower_experts_back(item, up):
        mixed, slope = attended[item][2], expanded[item][0]
        grads = heads_back[item][0] if item < MB - 1 else experts_back[item][0]
        results = {0: grads, 1: experts_back[item][1]}
        experts_back[item] = expand_back(
            True, item, text_lengths, up, mixed, slope, gains, *held[2:], results
        )
        return experts_back[item][2]

    def lower_heads_back(item, middle, ends):
        places = dict(enumerate(heads_back[item][:-1]))
        if item < MB - 1:
            places[0] = experts_back[item][0]
        heads_back[item] = attend_back(
            True,
            item,
            text_lengths,
            feeds,
            middle,
            *attended[item][:2],
            gains,
            *held[:2],
            places | {len(places): ends},
        )
        return heads_back[item][-1]

    ups[0] = after(ups[0], earlier)
    ups_other = [swapped(ups[0], "section", 0, (0, 1))]
    middle = lower_experts_back(0, ups[0])
    ends = lower_heads_back(0, middle, ends)
    first_grads = [heads_back[0][0], swapped(heads_back[0][0], "section", 0)]
    ups[1] = after(ups[1], ends)
    ups_other.append(swapped(ups[1], "section", 0, (0, 1)))
    middle = lower_experts_back(1, ups[1])
    inner = experts_back[1][0]
    inners = [first_grads[0], inner, first_grads[1], swapped(inner, "section", 0)]
    ups_other[1] = after(ups_other[1], middle)
    back_pieces = back_grads(text_lengths, lefts, ups + ups_other, feeds_pair, back_orders)
    inners[1] = after(inners[1], back_pieces[0][1], back_pieces[1][1])
    in_pieces = in_grads(text_lengths, lefts, inners)

    sums = Sums()
    for number in (0, 1):
        sums.begin(f"back{number}", back_pieces[number], back_orders[number])
    for number in (0, 1):
        sums.begin(f"in{number}", in_pieces[number], upward)
    middle = after(middle, in_pieces[0][1], in_pieces[1][1])
    ends = lower_heads_back(1, middle, ends)
    outers = [first_grads[0], *heads_back[1][:2], first_grads[1]]
    outers += [swapped(part, "section", 0) for part in heads_back[1][:2]]
    outer_piece = outer_grads(lefts, outers, upward)
    sums.begin("outer", outer_piece, upward)
    sums.last = [outer_piece[1]]
    gain_own, gain_theirs = gain_sums(
        [part[-2] for part in heads_back], [part[1] for part in experts_back]
    )
    gain_own = gain_own + swapped(gain_theirs, "section", 0)
    gain_count = 2 * HALF // n_dp
    gain_stack = gain_own.reshape(2, n_dp, HALF // n_dp).transpose(1, 0, 2)
    gain_stack = gain_stack.reshape(n_dp, 1, gain_count).astype(BF16)
    gain_stack = jnp.pad(gain_stack, ((0, 0), (0, 15), (0, 128 - gain_count)))
    gain_piece = by_lowest_bit(gain_stack)

    sums.begin("gain", gain_piece, upward)
    for name in ("back0", "back1", "back1", "back0", "in0", "back1", "in0", "in1", "in0", "in1"):
        sums.step(name)
    for name in ("back0", "outer", "in1", "outer", "gain", "gain", "outer", "gain"):
        sums.step(name)
    sums.finish(("back0", "back1", "in0", "in1", "outer", "gain"))
    qkv_rows = 3 * D // n_dp
    done = sums.results
    return (
        ends,
        done["gain"][:1, :gain_count].reshape(1, 2, HALF // n_dp),
        done["outer"][:qkv_rows].T[None],
        done["outer"][qkv_rows:].T[None],
        jnp.stack([done["in0"], done["in1"]])[None],
        jnp.stack([done["back0"].T, done["back1"].T])[None],
    )


def solution(mesh):
    return jax.shard_map(
        shards,
        mesh=mesh,
        in_specs=(
            P(("dp", "section"), None),
            P("dp"),
            P("section", None, None),
            P("section", None, None),
            P("section", None, None),
            P("section", None, None, None),
            P("section", None, None, None),
        ),
        out_specs=(
            P(("dp", "section"), None),
            P("section", None, "dp"),
            P("section", None, "dp"),
            P("section", None, "dp"),
            P("section", None, None, "dp"),
            P("section", None, None, "dp"),
        ),
        check_vma=False,
    )
```

```python
import functools

import jax
import jax.numpy as jnp
from jax import lax
from jax.experimental import pallas as pl
from jax.experimental.pallas import tpu as pltpu
from jax.sharding import PartitionSpec as P

D = 768
HALF = D // 2
HEADS = 12
FF = 3072
FF_HALF = FF // 2
HEAD_DIM = 64
IMAGE_ROWS = 197
ROWS = 256
MB = 2
KEPT = FF_HALF + 3 * HALF
TAIL = 192

EPSILON = 1e-05
MASKED = -1e30
F32 = jnp.float32
BF16 = jnp.bfloat16
VMEM_BYTES = 10 * 1024 * 1024
LEFTS = "any"


def cost(size):
    return pl.CostEstimate(flops=size << 20, bytes_accessed=1 << 10, transcendentals=0)


def dot_nn(left, right):
    return lax.dot_general(left, right, (((1,), (0,)), ((), ())), preferred_element_type=F32)


def dot_nt(left, right):
    return lax.dot_general(left, right, (((1,), (1,)), ((), ())), preferred_element_type=F32)


def dot_tn(left, right):
    return lax.dot_general(left, right, (((0,), (0,)), ((), ())), preferred_element_type=F32)


def norm_parts(hidden):
    centred = hidden - jnp.mean(hidden, axis=-1, keepdims=True)
    spread = jnp.mean(centred * centred, axis=-1, keepdims=True)
    inverse = lax.rsqrt(spread + EPSILON)
    return centred * inverse, inverse


def norm_back(grad, hidden, gain_row):
    unit, inverse = norm_parts(hidden)
    gain_grad = jnp.sum(grad * unit, axis=0, keepdims=True)
    scaled = grad * gain_row
    mean_plain = jnp.mean(scaled, axis=-1, keepdims=True)
    mean_unit = jnp.mean(scaled * unit, axis=-1, keepdims=True)
    return inverse * (scaled - mean_plain - unit * mean_unit), gain_grad


def gelu_pair(values):
    size = jnp.abs(values)
    denom = 1.0 + (0.3275911 * 0.7071067811865476) * size
    rough = pl.reciprocal(denom, approx=True)
    t = rough * (2.0 - denom * rough)
    poly = 0.5 * 1.061405429
    for factor in (-1.453152027, 1.421413741, -0.284496736, 0.254829592):
        poly = poly * t + 0.5 * factor
    bell = jnp.exp2(values * values * (-0.5 * 1.4426950408889634))
    upper_tail = poly * t * bell
    cdf = jnp.where(values < 0, upper_tail, 1.0 - upper_tail)
    return values * cdf, cdf + values * bell * 0.3989422804014327


def lane_half(value, which):
    lanes = lax.broadcasted_iota(jnp.int32, value.shape, 1)
    picked = lanes < HEAD_DIM if which == 0 else lanes >= HEAD_DIM
    return jnp.where(picked, value, jnp.zeros_like(value))


def call(kernel, name, ins, outs, scratch, aliases=None, size=1, memory=VMEM_BYTES):
    spaces = {"vmem": pltpu.VMEM, "auto": pltpu.VMEM, "smem": pltpu.SMEM, "any": pl.ANY, "hbm": pltpu.HBM}
    kinds = {"vmem": pltpu.VMEM, "auto": jax.ShapeDtypeStruct, "any": jax.ShapeDtypeStruct, "hbm": pltpu.HBM}
    shapes = [kinds[space](shape, kind) for shape, kind, space in outs]
    return pl.pallas_call(
        kernel,
        out_shape=shapes,
        in_specs=[pl.BlockSpec(memory_space=spaces[space]) for _, space in ins],
        out_specs=[pl.BlockSpec(memory_space=spaces[space]) for _, _, space in outs],
        input_output_aliases=aliases or {},
        scratch_shapes=scratch,
        compiler_params=pltpu.CompilerParams(vmem_limit_bytes=memory),
        cost_estimate=cost(size),
        name=name,
    )(
        *[
            pltpu.with_memory_space_constraint(value, pltpu.HBM) if space == "hbm" else value
            for value, space in ins
        ]
    )


class Place:
    def __init__(self, lengths):
        section = lax.axis_index("section")
        self.lengths = lengths
        self.is_lower = section < 2
        self.pos = section % 2

    def length(self, item, partner=False):
        pos = 1 - self.pos if partner else self.pos
        return self.lengths[pos * MB + item]

    def live(self, item, partner=False):
        return IMAGE_ROWS + self.length(item, partner)

    def experts(self, item, partner=False):
        kind = jnp.where(self.length(item, partner) > 0, 1, 0)
        return jnp.where(self.is_lower, 0, kind), jnp.where(self.is_lower, 1, kind)


def with_earlier(ins, outs, earlier):
    aliases = {}
    for number, value in (earlier or {}).items():
        aliases[len(ins)] = number
        ins = ins + [(value, outs[number][2])]
    return ins, aliases


class Sender:
    def __init__(self, sems):
        self.sems = sems
        self.sent = []
        self.done = 0

    def send(self, source, target):
        copy = pltpu.make_async_copy(source, target, self.sems.at[len(self.sent)])
        copy.start()
        self.sent.append(copy)

    def finish(self, count=None):
        count = len(self.sent) - self.done if count is None else count
        for copy in self.sent[self.done : self.done + count]:
            copy.wait()
        self.done += count


def join_kernel(count, *refs):
    own, other, joined, sems = refs[:count], refs[count : 2 * count], refs[2 * count : -1], refs[-1]
    pos = lax.axis_index("section") % 2
    sender = Sender(sems)
    for mine, theirs, whole in zip(own, other, joined):
        depth = mine.shape[-2]
        for source, at in ((mine, pos), (theirs, 1 - pos)):
            rows = pl.ds(pl.multiple_of(at * depth, depth), depth)
            if len(whole.shape) == 2:
                sender.send(source, whole.at[rows])
            else:
                for expert in range(whole.shape[0]):
                    sender.send(source.at[expert], whole.at[expert, rows])
    sender.finish()


def joined_halves(own, other):
    outs = []
    for part in own:
        shape = part.shape[:-2] + (2 * part.shape[-2], part.shape[-1])
        outs.append((shape, BF16, "vmem"))
    return call(
        functools.partial(join_kernel, len(own)),
        "joined_halves",
        [(value, "hbm") for value in own] + [(value, "any") for value in other],
        outs,
        [pltpu.SemaphoreType.DMA((4 * len(own),))],
    )


def gains_kernel(own, other, gains):
    first = lax.axis_index("section") % 2 == 0
    mine, theirs = own[...].astype(F32), other[...].astype(F32)
    gains[:, pl.ds(0, HALF)] = jnp.where(first, mine, theirs)
    gains[:, pl.ds(HALF, HALF)] = jnp.where(first, theirs, mine)


def joined_gains(own, other):
    return call(
        gains_kernel, "joined_gains", [(own, "vmem"), (other, "vmem")], [((2, D), F32, "vmem")], []
    )[0]


def places(pos, size):
    return (
        pl.ds(pl.multiple_of(pos * size, size), size),
        pl.ds(pl.multiple_of((1 - pos) * size, size), size),
    )


def attend_body(
    sender, place, item, rows_ref, gain_ref, weights, qkv_rows, probs, mixed, lefts, left_rows
):
    qkv_held, proj_held = weights
    own, other = places(place.pos, HALF)

    def send_halves(part):
        to = (pl.ds(item * ROWS, ROWS), pl.ds(FF_HALF + (1 + part) * HALF, HALF))
        for columns, target in zip((own, other), lefts):
            sender.send(left_rows.at[part, :, columns], target.at[to])

    normed = (norm_parts(rows_ref[...].astype(F32))[0] * gain_ref[0:1]).astype(BF16)
    left_rows[0] = normed
    send_halves(0)
    for part in range(3):
        columns = pl.ds(part * D, D)
        qkv_rows[:, columns] = dot_nn(normed, qkv_held[:, columns]).astype(BF16)
    keys_live = lax.broadcasted_iota(jnp.int32, (ROWS, ROWS), 1) < place.live(item)
    for pair in range(HEADS // 2):
        queries = qkv_rows[:, pl.ds(pair * 128, 128)] * jnp.asarray(HEAD_DIM**-0.5, BF16)
        keys = qkv_rows[:, pl.ds(D + pair * 128, 128)]
        values = qkv_rows[:, pl.ds(2 * D + pair * 128, 128)]
        context = None
        for which in (0, 1):
            scores = dot_nt(lane_half(queries, which), keys)
            scores = jnp.where(keys_live, scores, MASKED)
            shifted = jnp.exp(scores - jnp.max(scores, axis=-1, keepdims=True))
            total = jnp.sum(shifted, axis=-1, keepdims=True)
            weight = (shifted * (1.0 / total)).astype(BF16)
            probs[2 * pair + which] = weight
            term = dot_nn(weight, lane_half(values, which))
            context = term if context is None else context + term
        left_rows[1, :, pl.ds(pair * 128, 128)] = context.astype(BF16)
    send_halves(1)
    mixed[...] = rows_ref[...].astype(F32) + dot_nn(left_rows[1], proj_held[...])


def expand_body(
    sender, place, item, lower, mixed, gain_ref, weights, slope, lefts, second_rows, active, high
):
    in_held, back_held = weights
    first, second = place.experts(item)
    halves, deep_halves = places(place.pos, HALF), places(place.pos, FF_HALF)
    rows = pl.ds(item * ROWS, ROWS)

    def send_active():
        for columns, target in zip(deep_halves, lefts):
            sender.send(active.at[:, columns], target.at[rows, pl.ds(0, FF_HALF)])

    normed = (norm_parts(mixed[...])[0] * gain_ref[1:2]).astype(BF16)
    second_rows[...] = normed
    for columns, target in zip(halves, lefts):
        sender.send(second_rows.at[:, columns], target.at[rows, pl.ds(FF_HALF, HALF)])
    for part in range(4):
        columns = pl.ds(part * D, D)
        value, derivative = gelu_pair(dot_nn(normed, in_held[first, :, columns]))
        active[:, columns] = value.astype(BF16)
        slope[:, columns] = derivative.astype(BF16)
    if not lower:
        send_active()
    high[...] = mixed[...] + dot_nn(active[...], back_held[first])
    if not lower:
        return
    tail = pl.ds(TAIL, ROWS - TAIL)
    later = lax.broadcasted_iota(jnp.int32, (ROWS - TAIL, D), 0) >= IMAGE_ROWS - TAIL
    for part in range(4):
        columns = pl.ds(part * D, D)
        value, derivative = gelu_pair(dot_nn(second_rows[tail], in_held[second, :, columns]))
        kept = active[tail, columns].astype(F32)
        active[tail, columns] = jnp.where(later, value, kept).astype(BF16)
        kept = slope[tail, columns].astype(F32)
        slope[tail, columns] = jnp.where(later, derivative, kept).astype(BF16)
    send_active()
    patched = mixed[tail] + dot_nn(active[tail], back_held[second])
    high[tail] = jnp.where(later, patched, high[tail])


def expand_back_body(
    sender, place, item, lower, grad_ref, mixed, slope, gain_ref, weights, target, gain_out, middle, inner
):
    in_held, back_held = weights
    first, second = place.experts(item)
    is_live = lax.broadcasted_iota(jnp.int32, (ROWS, D), 0) < place.live(item)
    grad = jnp.where(is_live, grad_ref[...].astype(F32), 0.0)
    grad_low = grad.astype(BF16)
    for part in range(4):
        columns = pl.ds(part * D, D)
        grad_active = dot_nt(grad_low, back_held[first, columns])
        inner[:, columns] = (grad_active * slope[:, columns].astype(F32)).astype(BF16)
    if not lower:
        sender.send(inner, target)
    middle[...] = dot_nt(inner[...], in_held[first])
    if lower:
        tail = pl.ds(TAIL, ROWS - TAIL)
        later = lax.broadcasted_iota(jnp.int32, (ROWS - TAIL, D), 0) >= IMAGE_ROWS - TAIL
        for part in range(4):
            columns = pl.ds(part * D, D)
            grad_active = dot_nt(grad_low[TAIL:], back_held[second, columns])
            patched = grad_active * slope[tail, columns].astype(F32)
            kept = inner[tail, columns].astype(F32)
            inner[tail, columns] = jnp.where(later, patched, kept).astype(BF16)
        sender.send(inner, target)
        patched = dot_nt(inner[tail], in_held[second])
        middle[tail] = jnp.where(later, patched, middle[tail])
    grad_mixed, gain_out[...] = norm_back(middle[...], mixed[...], gain_ref[1:2])
    middle[...] = grad + grad_mixed


def attend_back_body(
    sender, rows_ref, middle, qkv_rows, probs, gain_ref, weights, targets, gain_out, outer
):
    qkv_held, proj_held = weights
    branch = middle[...].astype(BF16)
    outer[:, pl.ds(3 * D, D)] = branch
    grad_context = dot_nt(branch, proj_held[...]).astype(BF16)
    scale = jnp.asarray(HEAD_DIM**-0.5, BF16)
    for pair in range(HEADS // 2):
        queries = qkv_rows[:, pl.ds(pair * 128, 128)] * scale
        keys = qkv_rows[:, pl.ds(D + pair * 128, 128)] * scale
        values = qkv_rows[:, pl.ds(2 * D + pair * 128, 128)]
        context = grad_context[:, pair * 128 : (pair + 1) * 128]
        grad_q = grad_k = grad_v = None
        for which in (0, 1):
            weight = probs[2 * pair + which]
            context_half = lane_half(context, which)
            grad_probs = dot_nt(context_half, values)
            weight_wide = weight.astype(F32)
            product = weight_wide * grad_probs
            row_total = jnp.sum(product, axis=-1, keepdims=True)
            grad_scores = (product - weight_wide * row_total).astype(BF16)
            term_v = dot_tn(weight, context_half)
            term_q = dot_nn(grad_scores, lane_half(keys, which))
            term_k = dot_tn(grad_scores, lane_half(queries, which))
            grad_q = term_q if grad_q is None else grad_q + term_q
            grad_k = term_k if grad_k is None else grad_k + term_k
            grad_v = term_v if grad_v is None else grad_v + term_v
        outer[:, pl.ds(pair * 128, 128)] = grad_q.astype(BF16)
        outer[:, pl.ds(D + pair * 128, 128)] = grad_k.astype(BF16)
        outer[:, pl.ds(2 * D + pair * 128, 128)] = grad_v.astype(BF16)
    width = 4 * D // len(targets)
    for part, target in enumerate(targets):
        sender.send(outer.at[:, pl.ds(part * width, width)], target)
    grad_normed = dot_nt(outer[:, pl.ds(0, 3 * D)], qkv_held[...])
    grad_hidden, gain_out[...] = norm_back(grad_normed, rows_ref[...].astype(F32), gain_ref[0:1])
    return middle[...] + grad_hidden


def saved_shapes():
    return [((ROWS, 3 * D), BF16), ((HEADS, ROWS, ROWS), BF16), ((ROWS, D), F32)]


def grads_shapes(item):
    if item < MB - 1:
        return [((ROWS, FF + 4 * D), BF16, "any")]
    return [
        ((ROWS, FF), BF16, "any"),
        ((ROWS, 2 * D), BF16, "any"),
        ((ROWS + 16, 2 * D), BF16, "any"),
    ]


def grads_targets(item, refs):
    if item < MB - 1:
        return refs[0].at[:, pl.ds(0, FF)], [refs[0].at[:, pl.ds(FF, 4 * D)]]
    return refs[0], [refs[1], refs[2].at[pl.ds(0, ROWS)]]


def lower_attend_kernel(lengths, feeds, gain_ref, qkv_held, proj_held, *rest):
    saved, lefts, (left_rows, sems) = rest[: 3 * MB], rest[3 * MB : 3 * MB + 2], rest[3 * MB + 2 :]
    place = Place(lengths)

    @pl.when(place.is_lower)
    def _():
        sender = Sender(sems)
        for item in range(MB):
            rows_ref = feeds.at[pl.ds(item * ROWS, ROWS)]
            attend_body(
                sender,
                place,
                item,
                rows_ref,
                gain_ref,
                (qkv_held, proj_held),
                *saved[3 * item : 3 * item + 3],
                lefts,
                left_rows.at[item],
            )
        sender.finish()


def lower_attend(lengths, feeds, gains, qkv_held, proj_held):
    outs = [(*shape, "vmem") for _ in range(MB) for shape in saved_shapes()]
    outs += [((MB * ROWS, KEPT), BF16, LEFTS)] * 2
    ins = [(lengths, "smem")]
    ins += [(value, "vmem") for value in (feeds, gains, qkv_held, proj_held)]
    scratch = [pltpu.VMEM((MB, 2, ROWS, D), BF16), pltpu.SemaphoreType.DMA((4 * MB,))]
    return call(lower_attend_kernel, "lower_attend", ins, outs, scratch)


def lower_expand_kernel(n_alias, item, lengths, mixed, gain_ref, in_held, back_held, *rest):
    slope, keep_out, send_out, low, second_rows, active, high, sems = rest[n_alias:]
    place = Place(lengths)

    @pl.when(place.is_lower)
    def _():
        sender = Sender(sems)
        expand_body(
            sender,
            place,
            item,
            True,
            mixed,
            gain_ref,
            (in_held, back_held),
            slope,
            (keep_out, send_out),
            second_rows,
            active,
            high,
        )
        low[...] = high[...].astype(BF16)
        sender.finish()


def lower_expand(item, lengths, mixed, gains, in_held, back_held, earlier):
    outs = [
        ((ROWS, FF), BF16, "vmem"),
        ((MB * ROWS, KEPT), BF16, LEFTS),
        ((MB * ROWS, KEPT), BF16, LEFTS),
        ((ROWS, D), BF16, "vmem"),
    ]
    ins = [(lengths, "smem")]
    ins += [(value, "vmem") for value in (mixed, gains, in_held, back_held)]
    ins, aliases = with_earlier(ins, outs, earlier)
    scratch = [
        pltpu.VMEM((ROWS, D), BF16),
        pltpu.VMEM((ROWS, FF), BF16),
        pltpu.VMEM((ROWS, D), F32),
        pltpu.SemaphoreType.DMA((4,)),
    ]
    kernel = functools.partial(lower_expand_kernel, len(aliases), item)
    return call(kernel, "lower_expand", ins, outs, scratch, aliases)


def top_attend_kernel(n_alias, item, lengths, rows_ref, gain_ref, qkv_held, proj_held, *rest):
    qkv_rows, probs, mixed, keep_out, send_out, left_rows, sems = rest[n_alias:]
    place = Place(lengths)

    @pl.when(jnp.logical_not(place.is_lower))
    def _():
        sender = Sender(sems)
        attend_body(
            sender,
            place,
            item,
            rows_ref,
            gain_ref,
            (qkv_held, proj_held),
            qkv_rows,
            probs,
            mixed,
            (keep_out, send_out),
            left_rows,
        )
        sender.finish()


def top_attend(item, lengths, rows, gains, qkv_held, proj_held, earlier):
    outs = [(*shape, "vmem") for shape in saved_shapes()]
    outs += [((MB * ROWS, KEPT), BF16, LEFTS)] * 2
    ins = [(lengths, "smem")]
    ins += [(value, "vmem") for value in (rows, gains, qkv_held, proj_held)]
    ins, aliases = with_earlier(ins, outs, earlier)
    scratch = [pltpu.VMEM((2, ROWS, D), BF16), pltpu.SemaphoreType.DMA((4,))]
    kernel = functools.partial(top_attend_kernel, len(aliases), item)
    return call(kernel, "top_attend", ins, outs, scratch, aliases)


def top_expand_kernel(n_alias, item, lengths, mixed, gain_ref, in_held, back_held, *rest):
    slope, keep_out, send_out, high, second_rows, active, sems = rest[n_alias:]
    place = Place(lengths)

    @pl.when(jnp.logical_not(place.is_lower))
    def _():
        sender = Sender(sems)
        expand_body(
            sender,
            place,
            item,
            False,
            mixed,
            gain_ref,
            (in_held, back_held),
            slope,
            (keep_out, send_out),
            second_rows,
            active,
            high,
        )
        sender.finish()


def top_expand(item, lengths, mixed, gains, in_held, back_held, earlier):
    outs = [
        ((ROWS, FF), BF16, "vmem"),
        ((MB * ROWS, KEPT), BF16, LEFTS),
        ((MB * ROWS, KEPT), BF16, LEFTS),
        ((ROWS, D), F32, "vmem"),
    ]
    ins = [(lengths, "smem")]
    ins += [(value, "vmem") for value in (mixed, gains, in_held, back_held)]
    ins, aliases = with_earlier(ins, outs, earlier)
    scratch = [
        pltpu.VMEM((ROWS, D), BF16),
        pltpu.VMEM((ROWS, FF), BF16),
        pltpu.SemaphoreType.DMA((4,)),
    ]
    kernel = functools.partial(top_expand_kernel, len(aliases), item)
    return call(kernel, "top_expand", ins, outs, scratch, aliases)


def top_expand_back_kernel(item, lengths, feeds, mixed, slope, gain_ref, in_held, back_held, *rest):
    target, gain_out, middle, inner, sems = rest
    place = Place(lengths)

    @pl.when(jnp.logical_not(place.is_lower))
    def _():
        sender = Sender(sems)
        expand_back_body(
            sender,
            place,
            item,
            False,
            feeds.at[pl.ds(item * ROWS, ROWS)],
            mixed,
            slope,
            gain_ref,
            (in_held, back_held),
            target.at[:, pl.ds(0, FF)],
            gain_out,
            middle,
            inner,
        )
        sender.finish()


def top_expand_back(item, lengths, feeds, mixed, slope, gains, in_held, back_held):
    outs = [grads_shapes(item)[0], ((1, D), F32, "vmem"), ((ROWS, D), F32, "vmem")]
    ins = [(lengths, "smem")]
    ins += [(value, "vmem") for value in (feeds, mixed, slope, gains, in_held, back_held)]
    scratch = [pltpu.VMEM((ROWS, FF), BF16), pltpu.SemaphoreType.DMA((1,))]
    kernel = functools.partial(top_expand_back_kernel, item)
    return call(kernel, "top_expand_back", ins, outs, scratch)


def top_attend_back_kernel(n_alias, item, lengths, rows_ref, middle, qkv_rows, probs, gain_ref, *rest):
    weights, rest = rest[:2], rest[2 + n_alias :]
    *targets, gain_out, low, outer, sems = rest
    if item < MB - 1:
        targets = [targets[0].at[:, pl.ds(FF, 4 * D)]]
    else:
        targets = [targets[0], targets[1].at[pl.ds(0, ROWS)]]
    place = Place(lengths)

    @pl.when(jnp.logical_not(place.is_lower))
    def _():
        sender = Sender(sems)
        low[...] = attend_back_body(
            sender, rows_ref, middle, qkv_rows, probs, gain_ref, weights, targets, gain_out, outer
        ).astype(BF16)
        sender.finish()


def top_attend_back(item, lengths, rows, middle, saved, gains, weights, earlier):
    shapes = grads_shapes(item)
    outs = [*(shapes[1:] or shapes), ((1, D), F32, "vmem"), ((ROWS, D), BF16, "vmem")]
    ins = [(lengths, "smem")]
    ins += [(value, "vmem") for value in (rows, middle, *saved, gains, *weights)]
    ins, aliases = with_earlier(ins, outs, earlier)
    scratch = [pltpu.VMEM((ROWS, 4 * D), BF16), pltpu.SemaphoreType.DMA((2,))]
    kernel = functools.partial(top_attend_back_kernel, len(aliases), item)
    return call(kernel, "top_attend_back", ins, outs, scratch, aliases)


def lower_expand_back_kernel(
    n_alias, item, lengths, grad_ref, mixed, slope, gain_ref, in_held, back_held, *rest
):
    target, gain_out, middle, inner, sems = rest[n_alias:]
    place = Place(lengths)

    @pl.when(place.is_lower)
    def _():
        sender = Sender(sems)
        expand_back_body(
            sender,
            place,
            item,
            True,
            grad_ref,
            mixed,
            slope,
            gain_ref,
            (in_held, back_held),
            grads_targets(item, [target])[0] if item < MB - 1 else target,
            gain_out,
            middle,
            inner,
        )
        sender.finish()


def lower_expand_back(item, lengths, grad, mixed, slope, gains, in_held, back_held, earlier):
    size = 1 << 13 if item < MB - 1 else 1
    outs = [grads_shapes(item)[0], ((1, D), F32, "vmem"), ((ROWS, D), F32, "vmem")]
    ins = [(lengths, "smem")]
    ins += [(value, "vmem") for value in (grad, mixed, slope, gains, in_held, back_held)]
    ins, aliases = with_earlier(ins, outs, earlier)
    scratch = [pltpu.VMEM((ROWS, FF), BF16), pltpu.SemaphoreType.DMA((1,))]
    kernel = functools.partial(lower_expand_back_kernel, len(aliases), item)
    return call(kernel, "lower_expand_back", ins, outs, scratch, aliases, size)


def lower_attend_back_kernel(n_alias, item, lengths, feeds, middle, qkv_rows, probs, gain_ref, *rest):
    weights, rest = rest[:2], rest[2:]
    top_high, others, rest = rest[0], rest[1:4], rest[4 + n_alias :]
    if item < MB - 1:
        grads, gain_out, ends_out, outer, high, sems = rest
        targets = [grads.at[:, pl.ds(FF, 4 * D)]]
    else:
        first, last, gain_out, ends_out, gain_keep, outer, high, gain_rows, sems = rest
        targets = [first, last.at[pl.ds(0, ROWS)]]
    place = Place(lengths)
    rows = pl.ds(item * ROWS, ROWS)

    @pl.when(place.is_lower)
    def _():
        sender = Sender(sems)
        high[...] = attend_back_body(
            sender,
            feeds.at[rows],
            middle,
            qkv_rows,
            probs,
            gain_ref,
            weights,
            targets,
            gain_out,
            outer,
        )
        sender.send(high, ends_out.at[rows])
        sender.finish()

    @pl.when(jnp.logical_not(place.is_lower))
    def _():
        sender = Sender(sems)
        sender.send(top_high, ends_out.at[rows])
        sender.finish()

    if item == MB - 1:
        sender = Sender(sems)
        own, other = places(place.pos, HALF)
        gain_rows[...] = jnp.zeros_like(gain_rows)
        for row, parts in enumerate(((others[0], gain_out), others[1:])):
            gain_keep[row : row + 1] = parts[0][:, own] + parts[1][:, own]
            gain_rows[row : row + 1, pl.ds(0, HALF)] = parts[0][:, other] + parts[1][:, other]
        outer[pl.ds(0, 16), pl.ds(0, 2 * D)] = gain_rows[...].astype(BF16)
        sender.send(outer.at[pl.ds(0, 16), pl.ds(0, 2 * D)], last.at[pl.ds(ROWS, 16)])
        sender.finish()


def lower_attend_back(item, lengths, feeds, middle, saved, gains, weights, top, others, earlier):
    size = 1 << 13 if item < MB - 1 else 1
    shapes = grads_shapes(item)
    outs = [
        *(shapes[1:] or shapes),
        ((1, D), F32, "vmem"),
        ((MB * ROWS, D), F32, "any"),
    ]
    scratch = [pltpu.VMEM((ROWS, 4 * D), BF16), pltpu.VMEM((ROWS, D), F32)]
    if item == MB - 1:
        outs.append(((2, HALF), F32, "vmem"))
        scratch.append(pltpu.VMEM((16, 2 * D), F32))
    scratch.append(pltpu.SemaphoreType.DMA((3,)))
    ins = [(lengths, "smem")]
    ins += [(value, "vmem") for value in (feeds, middle, *saved, gains, *weights, top, *others)]
    ins, aliases = with_earlier(ins, outs, earlier)
    kernel = functools.partial(lower_attend_back_kernel, len(aliases), item)
    return call(kernel, "lower_attend_back", ins, outs, scratch, aliases, size)


def expert_rows(place, item, partner, expert, live_only=False):
    row = lax.broadcasted_iota(jnp.int32, (1, ROWS), 1)
    first, second = place.experts(item, partner)
    mine = jnp.where(row < IMAGE_ROWS, first, second) == expert
    if live_only:
        mine = mine & (row < place.live(item, partner))
    return mine


def bits_but(*taken):
    count = lax.axis_size("dp").bit_length() - 1
    return [bit for bit in reversed(range(count)) if bit not in taken]


def block_numbers(first_bit):
    here = (lax.axis_index("dp") >> first_bit) & 1
    rest = bits_but(first_bit)
    for number in range(1 << len(rest)):
        where = tuple((number >> (len(rest) - 1 - place)) & 1 for place in range(len(rest)))
        base = sum(value << bit for value, bit in zip(where, rest))
        yield where, base + (here << first_bit), base + ((1 - here) << first_bit)


def write_blocks(total, rows, first_bit, mine, theirs):
    for where, own, other in block_numbers(first_bit):
        own_at = pl.ds(pl.multiple_of(own * rows, rows), rows)
        other_at = pl.ds(pl.multiple_of(other * rows, rows), rows)
        mine[where] = total[own_at].astype(BF16)
        theirs[where] = total[other_at].astype(BF16)


def back_grads_kernel(orders, n_items, lengths, *refs):
    actives, grads, feeds = refs[:n_items], refs[n_items : 2 * n_items], refs[2 * n_items : 2 * n_items + 2]
    outs, (flipped, total) = refs[2 * n_items + 2 : -2], refs[-2:]
    place = Place(lengths)
    tail = ROWS - TAIL
    rows = D // lax.axis_size("dp")

    @pl.when(pl.program_id(0) == 0)
    def _():
        for index in range(n_items):
            item, partner = index % MB, index >= MB
            top = feeds[index // MB][pl.ds(item * ROWS, ROWS)]
            value = jnp.where(place.is_lower, grads[index][...], top).T
            for expert in (0, 1):
                mask = expert_rows(place, item, partner, expert, live_only=True)
                flipped[expert, :, pl.ds(index * ROWS, ROWS)] = jnp.where(mask, value, 0)

    def finished(expert):
        write_blocks(total, rows, orders[expert][0], outs[2 * expert], outs[2 * expert + 1])

    def whole(expert):
        result = None
        for index in range(n_items):
            term = dot_nn(flipped[expert, :, pl.ds(index * ROWS, ROWS)], actives[index][...])
            result = term if result is None else result + term
        total[...] = result

    whole(0)
    finished(0)

    @pl.when(place.is_lower)
    def _():
        left = [
            flipped[1, :, pl.ds(index * ROWS + ROWS // 2, ROWS // 2)] for index in range(n_items)
        ]
        right = [actives[index][pl.ds(ROWS // 2, ROWS // 2)] for index in range(n_items)]
        total[...] = dot_nn(jnp.concatenate(left, axis=1), jnp.concatenate(right, axis=0))

    @pl.when(jnp.logical_not(place.is_lower))
    def _():
        whole(1)

    finished(1)


def halves_shape(block):
    return jax.ShapeDtypeStruct((2,) * len(bits_but(0)) + block, BF16)


def halves_spec(block, place):
    lead = len(bits_but(0))
    return pl.BlockSpec((2,) * lead + block, lambda step: (0,) * lead + place(step))


def by_item(width, count, column, **options):
    return [
        pl.BlockSpec((ROWS, width), lambda step, item=index % MB: (item, column(step)), **options)
        for index in range(count)
    ]


def back_grads(lengths, kept, grads, feeds, orders):
    width = 256
    block = (D // lax.axis_size("dp"), width)
    once = pl.Buffered(1)
    fixed = [pl.BlockSpec((ROWS, D), lambda step: (0, 0), pipeline_mode=once)] * len(kept)
    fixed += [pl.BlockSpec((MB * ROWS, D), lambda step: (0, 0), pipeline_mode=once)] * 2
    results = pl.pallas_call(
        functools.partial(back_grads_kernel, orders, len(kept)),
        grid=(FF_HALF // width,),
        out_shape=[halves_shape((block[0], FF_HALF)) for _ in orders for _ in (0, 1)],
        in_specs=[pl.BlockSpec(memory_space=pltpu.SMEM)]
        + by_item(width, len(kept), lambda step: step)
        + fixed,
        out_specs=[
            halves_spec(block, lambda step: (0, step)) for _ in orders for _ in (0, 1)
        ],
        scratch_shapes=[
            pltpu.VMEM((2, D, len(kept) * ROWS), BF16),
            pltpu.VMEM((D, width), F32),
        ],
        compiler_params=pltpu.CompilerParams(vmem_limit_bytes=VMEM_BYTES),
        cost_estimate=cost(1),
        name="back_grads",
    )(lengths, *kept, *grads, *feeds)
    return [tuple(results[2 * expert : 2 * expert + 2]) for expert in (0, 1)]


def in_grads_kernel(width, n_items, lengths, *refs):
    seconds, inners = refs[:n_items], refs[n_items : 2 * n_items]
    outs, (flipped, total) = refs[2 * n_items : -2], refs[-2:]
    place = Place(lengths)
    half = ROWS // 2
    low_bit = lax.axis_index("dp") % 2

    @pl.when(pl.program_id(0) == 0)
    def _():
        for index in range(n_items):
            item, partner = index % MB, index >= MB
            value = seconds[index][...].T
            for expert in (0, 1):
                mask = expert_rows(place, item, partner, expert)
                flipped[expert, :, pl.ds(index * ROWS, ROWS)] = jnp.where(mask, value, 0)

    def whole(expert):
        result = None
        for index in range(n_items):
            term = dot_nn(flipped[expert, :, pl.ds(index * ROWS, ROWS)], inners[index][...])
            result = term if result is None else result + term
        total[...] = result

    def finished(expert):
        if len(outs) == 2:
            outs[expert][0] = total[...].astype(BF16)
            return
        for out, bit in zip(outs[2 * expert : 2 * expert + 2], (low_bit, 1 - low_bit)):
            out[0] = total[:, pl.ds(pl.multiple_of(bit * width, width), width)].astype(BF16)

    whole(0)
    finished(0)

    @pl.when(place.is_lower)
    def _():
        left = [flipped[1, :, pl.ds(index * ROWS + half, half)] for index in range(n_items)]
        right = [inners[index][pl.ds(half, half)] for index in range(n_items)]
        total[...] = dot_nn(jnp.concatenate(left, axis=1), jnp.concatenate(right, axis=0))

    @pl.when(jnp.logical_not(place.is_lower))
    def _():
        whole(1)

    finished(1)


def in_grads(lengths, kept, inners):
    size = lax.axis_size("dp")
    width = FF // size
    aligned = width % 128 == 0
    columns = 2 * width if aligned else D
    steps = FF // columns
    once = pl.Buffered(1)
    block = (1, HALF, width if aligned else columns)
    count = 4 if aligned else 2
    results = pl.pallas_call(
        functools.partial(in_grads_kernel, width, len(kept)),
        grid=(steps,),
        out_shape=[jax.ShapeDtypeStruct((steps,) + block[1:], BF16)] * count,
        in_specs=[pl.BlockSpec(memory_space=pltpu.SMEM)]
        + by_item(HALF, len(kept), lambda step: FF_HALF // HALF, pipeline_mode=once)
        + [pl.BlockSpec((ROWS, columns), lambda step: (0, step))] * len(inners),
        out_specs=[pl.BlockSpec(block, lambda step: (step, 0, 0))] * count,
        scratch_shapes=[
            pltpu.VMEM((2, HALF, len(kept) * ROWS), BF16),
            pltpu.VMEM((HALF, columns), F32),
        ],
        compiler_params=pltpu.CompilerParams(vmem_limit_bytes=VMEM_BYTES),
        cost_estimate=cost(1),
        name="in_grads",
    )(lengths, *kept, *inners)
    if not aligned:
        whole = [part.transpose(1, 0, 2).reshape(HALF, size, width) for part in results]
        return [by_lowest_bit(part.transpose(1, 0, 2)) for part in whole]
    shape = (2,) * len(bits_but(0)) + block[1:]
    return [tuple(part.reshape(shape) for part in results[2 * e : 2 * e + 2]) for e in (0, 1)]


def outer_grads_kernel(order, *refs):
    lefts, outers, gains, pieces, total = refs[:4], refs[4:10], refs[10:12], refs[12:16], refs[16]
    step = pl.program_id(0)
    result = None
    for index in range(4):
        outer = outers[3 * (index // MB)][...]
        if index % MB == MB - 1:
            first, second = outers[3 * (index // MB) + 1 : 3 * (index // MB) + 3]
            outer = jnp.where(step < 2, first[...], second[...])
        term = dot_tn(outer, lefts[index][...])
        result = term if result is None else result + term
    total[pl.ds(pl.multiple_of(step * D, D), D)] = result

    @pl.when(step == 3)
    def _():
        size = lax.axis_size("dp")
        proj_rows = D // size
        gain_rows = gains[0][...] + gains[1][pl.ds(0, 2), pl.ds(0, HALF)].astype(F32)
        gain_rows = jnp.concatenate([gain_rows, jnp.zeros((14, HALF), F32)], axis=0)
        for where, *numbers in block_numbers(order[0]):
            for target, number in zip((0, 1), numbers):
                at = pl.multiple_of(number * 3 * proj_rows, proj_rows)
                below = pl.multiple_of(3 * D + number * proj_rows, proj_rows)
                first, second = pieces[target], pieces[2 + target]
                first[where] = total[pl.ds(at, 2 * proj_rows)].astype(BF16)
                second[where + (pl.ds(0, proj_rows),)] = total[
                    pl.ds(at + 2 * proj_rows, proj_rows)
                ].astype(BF16)
                second[where + (pl.ds(proj_rows, proj_rows),)] = total[
                    pl.ds(below, proj_rows)
                ].astype(BF16)
                turned = pltpu.roll(gain_rows, HALF - number * (HALF // size), 1)
                second[where + (pl.ds(2 * proj_rows, 16),)] = turned.astype(BF16)


def outer_grads(kept, outers, gains, order):
    block = (2 * D // lax.axis_size("dp"), HALF)
    last = (block[0] + 16, HALF)
    results = pl.pallas_call(
        functools.partial(outer_grads_kernel, order),
        grid=(4,),
        out_shape=[halves_shape(block)] * 2 + [halves_shape(last)] * 2,
        in_specs=by_item(HALF, 4, lambda step: FF_HALF // HALF + 1 + step // 3)
        + [
            pl.BlockSpec((ROWS, D), lambda step: (0, FF // D + step)),
            pl.BlockSpec((ROWS, D), lambda step: (0, jnp.minimum(step, 1))),
            pl.BlockSpec((ROWS, D), lambda step: (0, jnp.maximum(step - 2, 0))),
        ]
        * 2
        + [
            pl.BlockSpec((2, HALF), lambda step: (0, 0)),
            pl.BlockSpec((16, D), lambda step: (ROWS // 16, 0)),
        ],
        out_specs=[halves_spec(block, lambda step: (0, 0))] * 2
        + [halves_spec(last, lambda step: (0, 0))] * 2,
        scratch_shapes=[pltpu.VMEM((4 * D, HALF), F32)],
        compiler_params=pltpu.CompilerParams(vmem_limit_bytes=2 * VMEM_BYTES),
        cost_estimate=cost(1),
        name="outer_grads",
    )(*kept, *outers, *gains)
    return tuple(results[:2]), tuple(results[2:])


def swapped(block, axis, bit, among=None):
    among = range(lax.axis_size(axis)) if among is None else among
    return lax.ppermute(block, axis, [(place, place ^ 1 << bit) for place in among])


def per_item(arrays):
    return [array for array in arrays for _ in range(MB)]


def passed_along(value, steps):
    count = lax.axis_size("section")
    first, last = (max(0, -steps), min(count, count - steps))
    route = [(source, source + steps) for source in range(first, last)]
    return lax.ppermute(value, "section", route)


def split_bit(stacked, bit):
    here = (lax.axis_index("dp") >> bit) & 1
    mine = lax.dynamic_index_in_dim(stacked, here, 0, keepdims=False)
    theirs = lax.dynamic_index_in_dim(stacked, 1 - here, 0, keepdims=False)
    return mine, theirs


def added_kernel(left, right, out):
    out[...] = left[...].astype(F32) + right[...].astype(F32)


def added(left, right):
    ins = [(left, "vmem"), (right, "vmem")]
    return call(added_kernel, "added", ins, [(left.shape, F32, "vmem")], [])[0]


def outer_sums_kernel(first, left, right, qkv_out, proj_out, gain_out):
    rows = proj_out.shape[1]
    second = left[...].astype(F32) + right[...].astype(F32)
    qkv = jnp.concatenate([first[...], second[:rows]], axis=0)
    qkv_out[...] = qkv.T
    proj_out[...] = second[rows : 2 * rows].T
    gain_out[...] = second[2 * rows : 2 * rows + 2]


def outer_sums(first, left, right):
    rows = first.shape[0] // 2
    ins = [(value, "vmem") for value in (first, left, right)]
    shapes = [(HALF, 3 * rows), (HALF, rows), (2, HALF)]
    outs = [(shape, F32, "auto") for shape in shapes]
    return call(outer_sums_kernel, "outer_sums", ins, outs, [])


def added_halves_kernel(axis, bit, left, right, mine, theirs):
    here = (lax.axis_index("dp") >> bit) & 1
    lead = (slice(None),) * axis
    for out, at in ((mine, lead + (here,)), (theirs, lead + (1 - here,))):
        out[...] = (left[at].astype(F32) + right[at].astype(F32)).astype(BF16)


def added_halves(left, right, axis, bit):
    ins = [(left, "vmem"), (right, "vmem")]
    outs = [(left.shape[:axis] + left.shape[axis + 1 :], BF16, "vmem")] * 2
    kernel = functools.partial(added_halves_kernel, axis, bit)
    return call(kernel, "added_halves", ins, outs, [])


def after(value, *earlier):
    return lax.optimization_barrier((value, earlier))[0]


class Sums:
    def __init__(self):
        self.open = {}
        self.results = {}
        self.last = []

    def begin(self, name, piece, order, taken=()):
        mine, theirs = piece
        self.open[name] = (mine, swapped(theirs, "dp", order[0]), order[1:], (*taken, order[0]))

    def step(self, name, hold=False):
        mine, got, rest, taken = self.open.pop(name)
        mine = after(mine, *self.last)
        if len(rest) == 0:
            self.results[name] = added(mine, got)
            self.last = [self.results[name]]
            return
        mine, theirs = added_halves(mine, got, bits_but(*taken).index(rest[0]), rest[0])
        self.last = [theirs]
        if hold:
            return (mine, theirs), rest, taken
        self.begin(name, (mine, theirs), rest, taken)

    def finish(self, but):
        while len(self.open) > 1 or len(self.open[but][2]) > 0:
            for name in list(self.open):
                if name != but or len(self.open[name][2]) > 0:
                    self.step(name)
        mine, got, *_ = self.open.pop(but)
        return after(mine, *self.last), got


def by_lowest_bit(stacked):
    bits = lax.axis_size("dp").bit_length() - 1
    split = jnp.moveaxis(stacked.reshape((2,) * bits + stacked.shape[1:]), bits - 1, 0)
    return split_bit(split, 0)


def shards(feeds, text_lengths, norm_gains, qkv_weight, out_weight, expert_in, expert_out):
    n_dp = lax.axis_size("dp")
    bits = n_dp.bit_length() - 1
    pos = lax.axis_index("section") % 2

    gains_other = swapped(norm_gains[0], "section", 0)
    gains = joined_gains(norm_gains[0], gains_other)
    own = [qkv_weight[0], out_weight[0]]
    other = [swapped(part, "section", 0) for part in own]
    held = joined_halves(own, other)
    in_other = swapped(after(expert_in[0], gains_other, *other), "section", 0)
    back_other = swapped(after(expert_out[0], gains_other, *other), "section", 0)

    *saved, keep, send = lower_attend(text_lengths, feeds, gains, *held)
    saved = [saved[3 * item : 3 * item + 3] for item in range(MB)]
    earlier = saved[-1][2]
    held += joined_halves([expert_in[0]], [after(in_other, earlier)])
    held += joined_halves([expert_out[0]], [after(back_other, earlier)])
    slopes, passed = [], []
    for item in range(MB):
        mixed = after(saved[item][2], earlier)
        slope, keep, send, earlier = lower_expand(
            item, text_lengths, mixed, gains, *held[2:], {1: keep, 2: send}
        )
        slopes.append(slope)
        passed.append(passed_along(earlier, 2))
    grads, gain_grads, ups = [], [], []
    tops = []
    for item in range(MB):
        rows = after(passed[item], earlier)
        places = dict(enumerate(saved[item])) | {3: keep, 4: send}
        *saved[item], keep, send = top_attend(
            item, text_lengths, rows, gains, *held[:2], places
        )
        mixed = saved[item][2]
        places = {0: slopes[item], 1: keep, 2: send}
        slopes[item], keep, send, top = top_expand(
            item, text_lengths, mixed, gains, *held[2:], places
        )
        tops.append(top)
        inner, gain_second, middle = top_expand_back(
            item, text_lengths, feeds, mixed, slopes[item], gains, *held[2:]
        )
        *outer, gain_first, earlier = top_attend_back(
            item,
            text_lengths,
            rows,
            middle,
            saved[item][:2],
            gains,
            held[:2],
            {0: inner} if item < MB - 1 else {},
        )
        grads.append(outer if item < MB - 1 else [inner, *outer])
        gain_grads.append([gain_first, gain_second])
        ups.append(passed_along(earlier, -2))
    feeds_pair = [feeds, swapped(after(feeds, earlier), "section", 0, (2, 3))]
    lefts = per_item([keep, swapped(after(send, earlier), "section", 0)])

    upward = tuple(range(bits))
    back_orders = [upward[1:] + upward[:1], upward]

    def lower_back_experts(item, up):
        results = {0: grads[item][0], 1: gain_grads[item][1]}
        grads[item][0], gain_grads[item][1], middle = lower_expand_back(
            item, text_lengths, up, saved[item][2], slopes[item], gains, *held[2:], results
        )
        return middle

    def lower_back_heads(item, middle, ends, others):
        first = 0 if item < MB - 1 else 1
        parts = [*grads[item][first:], gain_grads[item][0], *ends]
        results = lower_attend_back(
            item,
            text_lengths,
            feeds,
            middle,
            saved[item][:2],
            gains,
            held[:2],
            tops[item],
            others,
            dict(enumerate(parts)),
        )
        count = len(grads[item]) - first
        grads[item][first:], gain_grads[item][0] = results[:count], results[count]
        return results[count + 1 :]

    ups[0] = after(ups[0], earlier)
    ups_other = [swapped(ups[0], "section", 0, (0, 1))]
    middle = lower_back_experts(0, ups[0])
    (ends,) = lower_back_heads(0, middle, [], [gain_grads[0][1]] * 3)
    first_grads = [grads[0][0], swapped(grads[0][0], "section", 0)]
    ups[1] = after(ups[1], ends)
    ups_other.append(swapped(ups[1], "section", 0, (0, 1)))
    middle = lower_back_experts(1, after(ups[1], ups_other[0]))
    inner = grads[1][0]
    inners = [first_grads[0], inner, first_grads[1], swapped(inner, "section", 0)]
    ups_other[1] = after(ups_other[1], middle)
    back_pieces = back_grads(text_lengths, lefts, ups + ups_other, feeds_pair, back_orders)
    inners[1] = after(inners[1], back_pieces[0][1], back_pieces[1][1])
    in_pieces = in_grads(text_lengths, lefts, inners)

    sums = Sums()
    for number in (0, 1):
        sums.begin(f"back{number}", back_pieces[number], back_orders[number])
    sums.begin("in0", in_pieces[0], upward)
    middle = after(middle, in_pieces[0][1], in_pieces[1][1])
    others = [gain_grads[0][0], gain_grads[0][1], gain_grads[1][1]]
    ends, gain_keep = lower_back_heads(1, middle, [ends], others)
    outers = [first_grads[0], *grads[1][1:], first_grads[1]]
    outers += [swapped(part, "section", 0) for part in grads[1][1:]]
    outer_pieces = outer_grads(lefts, outers, (gain_keep, outers[-1]), upward)
    sums.last = [piece[1] for piece in outer_pieces]
    back0, *back0_rest = sums.step("back0", hold=True)
    sums.step("back1")

    def later(piece):
        return piece[0], after(piece[1], *sums.last)

    sums.begin("in1", later(in_pieces[1]), upward)
    sums.begin("outer0", later(outer_pieces[0]), upward)
    sums.step("back1")
    sums.begin("back0", later(back0), *back0_rest)
    sums.step("in0")
    names = "back0 in0 in1 back1".split()
    for name in names:
        sums.step(name)
    sums.begin("outer1", later(outer_pieces[1]), upward)
    names = "outer0 in1 in0 outer1 outer0 in1 outer1 outer0 back0".split()
    for name in names:
        sums.step(name)
    last = sums.finish("outer1")
    qkv_sum, proj_sum, gain_sum = outer_sums(sums.results["outer0"], *last)
    done = sums.results
    return (
        ends,
        gain_sum[None, :, : HALF // n_dp],
        qkv_sum[None],
        proj_sum[None],
        jnp.stack([done["in0"], done["in1"]])[None],
        jnp.stack([done["back0"].T, done["back1"].T])[None],
    )


def solution(mesh):
    return jax.shard_map(
        shards,
        mesh=mesh,
        in_specs=(
            P(("dp", "section"), None),
            P("dp"),
            P("section", None, None),
            P("section", None, None),
            P("section", None, None),
            P("section", None, None, None),
            P("section", None, None, None),
        ),
        out_specs=(
            P(("dp", "section"), None),
            P("section", None, "dp"),
            P("section", None, "dp"),
            P("section", None, "dp"),
            P("section", None, None, "dp"),
            P("section", None, None, "dp"),
        ),
        check_vma=False,
    )
```

```python
import functools

import jax
import jax.numpy as jnp
from jax import lax
from jax.experimental import pallas as pl
from jax.experimental.pallas import tpu as pltpu
from jax.sharding import PartitionSpec as P

D = 768
HALF = D // 2
HEADS = 12
FF = 3072
FF_HALF = FF // 2
HEAD_DIM = 64
IMAGE_ROWS = 197
ROWS = 256
MB = 2
KEPT = FF_HALF + 3 * HALF
TAIL = 192

EPSILON = 1e-05
MASKED = -1e30
F32 = jnp.float32
BF16 = jnp.bfloat16
VMEM_BYTES = 10 * 1024 * 1024
LEFTS = "any"


def cost(size):
    return pl.CostEstimate(flops=size << 20, bytes_accessed=1 << 10, transcendentals=0)


def dot_nn(left, right):
    return lax.dot_general(left, right, (((1,), (0,)), ((), ())), preferred_element_type=F32)


def dot_nt(left, right):
    return lax.dot_general(left, right, (((1,), (1,)), ((), ())), preferred_element_type=F32)


def dot_tn(left, right):
    return lax.dot_general(left, right, (((0,), (0,)), ((), ())), preferred_element_type=F32)


def norm_parts(hidden):
    centred = hidden - jnp.mean(hidden, axis=-1, keepdims=True)
    spread = jnp.mean(centred * centred, axis=-1, keepdims=True)
    inverse = lax.rsqrt(spread + EPSILON)
    return centred * inverse, inverse


def norm_back(grad, hidden, gain_row):
    unit, inverse = norm_parts(hidden)
    gain_grad = jnp.sum(grad * unit, axis=0, keepdims=True)
    scaled = grad * gain_row
    mean_plain = jnp.mean(scaled, axis=-1, keepdims=True)
    mean_unit = jnp.mean(scaled * unit, axis=-1, keepdims=True)
    return inverse * (scaled - mean_plain - unit * mean_unit), gain_grad


def gelu_pair(values):
    size = jnp.abs(values)
    denom = 1.0 + (0.3275911 * 0.7071067811865476) * size
    t = pl.reciprocal(denom, approx=True)
    poly = 0.5 * 1.061405429
    for factor in (-1.453152027, 1.421413741, -0.284496736, 0.254829592):
        poly = poly * t + 0.5 * factor
    bell = jnp.exp2(values * values * (-0.5 * 1.4426950408889634))
    upper_tail = poly * t * bell
    cdf = jnp.where(values < 0, upper_tail, 1.0 - upper_tail)
    return values * cdf, cdf + values * bell * 0.3989422804014327


def lane_half(value, which):
    lanes = lax.broadcasted_iota(jnp.int32, value.shape, 1)
    picked = lanes < HEAD_DIM if which == 0 else lanes >= HEAD_DIM
    return jnp.where(picked, value, jnp.zeros_like(value))


def call(kernel, name, ins, outs, scratch, aliases=None, size=1, memory=VMEM_BYTES):
    spaces = {"vmem": pltpu.VMEM, "auto": pltpu.VMEM, "smem": pltpu.SMEM, "any": pl.ANY, "hbm": pltpu.HBM}
    kinds = {"vmem": pltpu.VMEM, "auto": jax.ShapeDtypeStruct, "any": jax.ShapeDtypeStruct, "hbm": pltpu.HBM}
    shapes = [kinds[space](shape, kind) for shape, kind, space in outs]
    return pl.pallas_call(
        kernel,
        out_shape=shapes,
        in_specs=[pl.BlockSpec(memory_space=spaces[space]) for _, space in ins],
        out_specs=[pl.BlockSpec(memory_space=spaces[space]) for _, _, space in outs],
        input_output_aliases=aliases or {},
        scratch_shapes=scratch,
        compiler_params=pltpu.CompilerParams(vmem_limit_bytes=memory),
        cost_estimate=cost(size),
        name=name,
    )(
        *[
            pltpu.with_memory_space_constraint(value, pltpu.HBM) if space == "hbm" else value
            for value, space in ins
        ]
    )


class Place:
    def __init__(self, lengths):
        section = lax.axis_index("section")
        self.lengths = lengths
        self.is_lower = section < 2
        self.pos = section % 2

    def length(self, item, partner=False):
        pos = 1 - self.pos if partner else self.pos
        return self.lengths[pos * MB + item]

    def live(self, item, partner=False):
        return IMAGE_ROWS + self.length(item, partner)

    def experts(self, item, partner=False):
        kind = jnp.where(self.length(item, partner) > 0, 1, 0)
        return jnp.where(self.is_lower, 0, kind), jnp.where(self.is_lower, 1, kind)


def with_earlier(ins, outs, earlier):
    aliases = {}
    for number, value in (earlier or {}).items():
        aliases[len(ins)] = number
        ins = ins + [(value, outs[number][2])]
    return ins, aliases


class Sender:
    def __init__(self, sems):
        self.sems = sems
        self.sent = []
        self.done = 0

    def send(self, source, target):
        copy = pltpu.make_async_copy(source, target, self.sems.at[len(self.sent)])
        copy.start()
        self.sent.append(copy)

    def finish(self, count=None):
        count = len(self.sent) - self.done if count is None else count
        for copy in self.sent[self.done : self.done + count]:
            copy.wait()
        self.done += count


def join_kernel(count, *refs):
    own, other, joined, sems = refs[:count], refs[count : 2 * count], refs[2 * count : -1], refs[-1]
    pos = lax.axis_index("section") % 2
    sender = Sender(sems)
    for mine, theirs, whole in zip(own, other, joined):
        depth = mine.shape[-2]
        for source, at in ((mine, pos), (theirs, 1 - pos)):
            rows = pl.ds(pl.multiple_of(at * depth, depth), depth)
            if len(whole.shape) == 2:
                sender.send(source, whole.at[rows])
            else:
                for expert in range(whole.shape[0]):
                    sender.send(source.at[expert], whole.at[expert, rows])
    sender.finish()


def joined_halves(own, other):
    outs = []
    for part in own:
        shape = part.shape[:-2] + (2 * part.shape[-2], part.shape[-1])
        outs.append((shape, BF16, "vmem"))
    return call(
        functools.partial(join_kernel, len(own)),
        "joined_halves",
        [(value, "hbm") for value in own] + [(value, "any") for value in other],
        outs,
        [pltpu.SemaphoreType.DMA((4 * len(own),))],
    )


def gains_kernel(own, other, gains):
    first = lax.axis_index("section") % 2 == 0
    mine, theirs = own[...].astype(F32), other[...].astype(F32)
    gains[:, pl.ds(0, HALF)] = jnp.where(first, mine, theirs)
    gains[:, pl.ds(HALF, HALF)] = jnp.where(first, theirs, mine)


def joined_gains(own, other):
    return call(
        gains_kernel, "joined_gains", [(own, "vmem"), (other, "vmem")], [((2, D), F32, "vmem")], []
    )[0]


def places(pos, size):
    return (
        pl.ds(pl.multiple_of(pos * size, size), size),
        pl.ds(pl.multiple_of((1 - pos) * size, size), size),
    )


def attend_body(
    sender, place, item, rows_ref, gain_ref, weights, qkv_rows, probs, mixed, lefts, left_rows
):
    qkv_held, proj_held = weights
    own, other = places(place.pos, HALF)

    def send_halves(part):
        to = (pl.ds(item * ROWS, ROWS), pl.ds(FF_HALF + (1 + part) * HALF, HALF))
        for columns, target in zip((own, other), lefts):
            sender.send(left_rows.at[part, :, columns], target.at[to])

    normed = (norm_parts(rows_ref[...].astype(F32))[0] * gain_ref[0:1]).astype(BF16)
    left_rows[0] = normed
    send_halves(0)
    for part in range(3):
        columns = pl.ds(part * D, D)
        qkv_rows[:, columns] = dot_nn(normed, qkv_held[:, columns]).astype(BF16)
    keys_live = lax.broadcasted_iota(jnp.int32, (ROWS, ROWS), 1) < place.live(item)
    for pair in range(HEADS // 2):
        queries = qkv_rows[:, pl.ds(pair * 128, 128)] * jnp.asarray(HEAD_DIM**-0.5, BF16)
        keys = qkv_rows[:, pl.ds(D + pair * 128, 128)]
        values = qkv_rows[:, pl.ds(2 * D + pair * 128, 128)]
        context = None
        for which in (0, 1):
            scores = dot_nt(lane_half(queries, which), keys)
            scores = jnp.where(keys_live, scores, MASKED)
            shifted = jnp.exp(scores - jnp.max(scores, axis=-1, keepdims=True))
            total = jnp.sum(shifted, axis=-1, keepdims=True)
            weight = (shifted * (1.0 / total)).astype(BF16)
            probs[2 * pair + which] = weight
            term = dot_nn(weight, lane_half(values, which))
            context = term if context is None else context + term
        left_rows[1, :, pl.ds(pair * 128, 128)] = context.astype(BF16)
    send_halves(1)
    mixed[...] = rows_ref[...].astype(F32) + dot_nn(left_rows[1], proj_held[...])


def expand_body(
    sender, place, item, lower, mixed, gain_ref, weights, slope, lefts, second_rows, active, high
):
    in_held, back_held = weights
    first, second = place.experts(item)
    halves, deep_halves = places(place.pos, HALF), places(place.pos, FF_HALF)
    rows = pl.ds(item * ROWS, ROWS)

    def send_active():
        for columns, target in zip(deep_halves, lefts):
            sender.send(active.at[:, columns], target.at[rows, pl.ds(0, FF_HALF)])

    normed = (norm_parts(mixed[...])[0] * gain_ref[1:2]).astype(BF16)
    second_rows[...] = normed
    for columns, target in zip(halves, lefts):
        sender.send(second_rows.at[:, columns], target.at[rows, pl.ds(FF_HALF, HALF)])
    for part in range(4):
        columns = pl.ds(part * D, D)
        value, derivative = gelu_pair(dot_nn(normed, in_held[first, :, columns]))
        active[:, columns] = value.astype(BF16)
        slope[:, columns] = derivative.astype(BF16)
    if not lower:
        send_active()
    high[...] = mixed[...] + dot_nn(active[...], back_held[first])
    if not lower:
        return
    tail = pl.ds(TAIL, ROWS - TAIL)
    later = lax.broadcasted_iota(jnp.int32, (ROWS - TAIL, D), 0) >= IMAGE_ROWS - TAIL
    for part in range(4):
        columns = pl.ds(part * D, D)
        value, derivative = gelu_pair(dot_nn(second_rows[tail], in_held[second, :, columns]))
        kept = active[tail, columns].astype(F32)
        active[tail, columns] = jnp.where(later, value, kept).astype(BF16)
        kept = slope[tail, columns].astype(F32)
        slope[tail, columns] = jnp.where(later, derivative, kept).astype(BF16)
    send_active()
    patched = mixed[tail] + dot_nn(active[tail], back_held[second])
    high[tail] = jnp.where(later, patched, high[tail])


def expand_back_body(
    sender, place, item, lower, grad_ref, mixed, slope, gain_ref, weights, target, gain_out, middle, inner
):
    in_held, back_held = weights
    first, second = place.experts(item)
    is_live = lax.broadcasted_iota(jnp.int32, (ROWS, D), 0) < place.live(item)
    grad = jnp.where(is_live, grad_ref[...].astype(F32), 0.0)
    grad_low = grad.astype(BF16)
    for part in range(4):
        columns = pl.ds(part * D, D)
        grad_active = dot_nt(grad_low, back_held[first, columns])
        inner[:, columns] = (grad_active * slope[:, columns].astype(F32)).astype(BF16)
    if not lower:
        sender.send(inner, target)
    middle[...] = dot_nt(inner[...], in_held[first])
    if lower:
        tail = pl.ds(TAIL, ROWS - TAIL)
        later = lax.broadcasted_iota(jnp.int32, (ROWS - TAIL, D), 0) >= IMAGE_ROWS - TAIL
        for part in range(4):
            columns = pl.ds(part * D, D)
            grad_active = dot_nt(grad_low[TAIL:], back_held[second, columns])
            patched = grad_active * slope[tail, columns].astype(F32)
            kept = inner[tail, columns].astype(F32)
            inner[tail, columns] = jnp.where(later, patched, kept).astype(BF16)
        sender.send(inner, target)
        patched = dot_nt(inner[tail], in_held[second])
        middle[tail] = jnp.where(later, patched, middle[tail])
    grad_mixed, gain_out[...] = norm_back(middle[...], mixed[...], gain_ref[1:2])
    middle[...] = grad + grad_mixed


def attend_back_body(
    sender, rows_ref, middle, qkv_rows, probs, gain_ref, weights, targets, gain_out, outer
):
    qkv_held, proj_held = weights
    branch = middle[...].astype(BF16)
    outer[:, pl.ds(3 * D, D)] = branch
    grad_context = dot_nt(branch, proj_held[...]).astype(BF16)
    scale = jnp.asarray(HEAD_DIM**-0.5, BF16)
    for pair in range(HEADS // 2):
        queries = qkv_rows[:, pl.ds(pair * 128, 128)] * scale
        keys = qkv_rows[:, pl.ds(D + pair * 128, 128)] * scale
        values = qkv_rows[:, pl.ds(2 * D + pair * 128, 128)]
        context = grad_context[:, pair * 128 : (pair + 1) * 128]
        grad_q = grad_k = grad_v = None
        for which in (0, 1):
            weight = probs[2 * pair + which]
            context_half = lane_half(context, which)
            grad_probs = dot_nt(context_half, values)
            weight_wide = weight.astype(F32)
            product = weight_wide * grad_probs
            row_total = jnp.sum(product, axis=-1, keepdims=True)
            grad_scores = (product - weight_wide * row_total).astype(BF16)
            term_v = dot_tn(weight, context_half)
            term_q = dot_nn(grad_scores, lane_half(keys, which))
            term_k = dot_tn(grad_scores, lane_half(queries, which))
            grad_q = term_q if grad_q is None else grad_q + term_q
            grad_k = term_k if grad_k is None else grad_k + term_k
            grad_v = term_v if grad_v is None else grad_v + term_v
        outer[:, pl.ds(pair * 128, 128)] = grad_q.astype(BF16)
        outer[:, pl.ds(D + pair * 128, 128)] = grad_k.astype(BF16)
        outer[:, pl.ds(2 * D + pair * 128, 128)] = grad_v.astype(BF16)
    width = 4 * D // len(targets)
    for part, target in enumerate(targets):
        sender.send(outer.at[:, pl.ds(part * width, width)], target)
    grad_normed = dot_nt(outer[:, pl.ds(0, 3 * D)], qkv_held[...])
    grad_hidden, gain_out[...] = norm_back(grad_normed, rows_ref[...].astype(F32), gain_ref[0:1])
    return middle[...] + grad_hidden


def saved_shapes():
    return [((ROWS, 3 * D), BF16), ((HEADS, ROWS, ROWS), BF16), ((ROWS, D), F32)]


def grads_shapes(item):
    if item < MB - 1:
        return [((ROWS, FF + 4 * D), BF16, "any")]
    return [
        ((ROWS, FF), BF16, "any"),
        ((ROWS, 2 * D), BF16, "any"),
        ((ROWS + 16, 2 * D), BF16, "any"),
    ]


def grads_targets(item, refs):
    if item < MB - 1:
        return refs[0].at[:, pl.ds(0, FF)], [refs[0].at[:, pl.ds(FF, 4 * D)]]
    return refs[0], [refs[1], refs[2].at[pl.ds(0, ROWS)]]


def lower_attend_kernel(lengths, feeds, gain_ref, qkv_held, proj_held, *rest):
    saved, lefts, (left_rows, sems) = rest[: 3 * MB], rest[3 * MB : 3 * MB + 2], rest[3 * MB + 2 :]
    place = Place(lengths)

    @pl.when(place.is_lower)
    def _():
        sender = Sender(sems)
        for item in range(MB):
            rows_ref = feeds.at[pl.ds(item * ROWS, ROWS)]
            attend_body(
                sender,
                place,
                item,
                rows_ref,
                gain_ref,
                (qkv_held, proj_held),
                *saved[3 * item : 3 * item + 3],
                lefts,
                left_rows.at[item],
            )
        sender.finish()


def lower_attend(lengths, feeds, gains, qkv_held, proj_held):
    outs = [(*shape, "vmem") for _ in range(MB) for shape in saved_shapes()]
    outs += [((MB * ROWS, KEPT), BF16, LEFTS)] * 2
    ins = [(lengths, "smem")]
    ins += [(value, "vmem") for value in (feeds, gains, qkv_held, proj_held)]
    scratch = [pltpu.VMEM((MB, 2, ROWS, D), BF16), pltpu.SemaphoreType.DMA((4 * MB,))]
    return call(lower_attend_kernel, "lower_attend", ins, outs, scratch)


def lower_expand_kernel(n_alias, item, lengths, mixed, gain_ref, in_held, back_held, *rest):
    slope, keep_out, send_out, low, second_rows, active, high, sems = rest[n_alias:]
    place = Place(lengths)

    @pl.when(place.is_lower)
    def _():
        sender = Sender(sems)
        expand_body(
            sender,
            place,
            item,
            True,
            mixed,
            gain_ref,
            (in_held, back_held),
            slope,
            (keep_out, send_out),
            second_rows,
            active,
            high,
        )
        low[...] = high[...].astype(BF16)
        sender.finish()


def lower_expand(item, lengths, mixed, gains, in_held, back_held, earlier):
    outs = [
        ((ROWS, FF), BF16, "vmem"),
        ((MB * ROWS, KEPT), BF16, LEFTS),
        ((MB * ROWS, KEPT), BF16, LEFTS),
        ((ROWS, D), BF16, "vmem"),
    ]
    ins = [(lengths, "smem")]
    ins += [(value, "vmem") for value in (mixed, gains, in_held, back_held)]
    ins, aliases = with_earlier(ins, outs, earlier)
    scratch = [
        pltpu.VMEM((ROWS, D), BF16),
        pltpu.VMEM((ROWS, FF), BF16),
        pltpu.VMEM((ROWS, D), F32),
        pltpu.SemaphoreType.DMA((4,)),
    ]
    kernel = functools.partial(lower_expand_kernel, len(aliases), item)
    return call(kernel, "lower_expand", ins, outs, scratch, aliases)


def top_attend_kernel(n_alias, item, lengths, rows_ref, gain_ref, qkv_held, proj_held, *rest):
    qkv_rows, probs, mixed, keep_out, send_out, left_rows, sems = rest[n_alias:]
    place = Place(lengths)

    @pl.when(jnp.logical_not(place.is_lower))
    def _():
        sender = Sender(sems)
        attend_body(
            sender,
            place,
            item,
            rows_ref,
            gain_ref,
            (qkv_held, proj_held),
            qkv_rows,
            probs,
            mixed,
            (keep_out, send_out),
            left_rows,
        )
        sender.finish()


def top_attend(item, lengths, rows, gains, qkv_held, proj_held, earlier):
    outs = [(*shape, "vmem") for shape in saved_shapes()]
    outs += [((MB * ROWS, KEPT), BF16, LEFTS)] * 2
    ins = [(lengths, "smem")]
    ins += [(value, "vmem") for value in (rows, gains, qkv_held, proj_held)]
    ins, aliases = with_earlier(ins, outs, earlier)
    scratch = [pltpu.VMEM((2, ROWS, D), BF16), pltpu.SemaphoreType.DMA((4,))]
    kernel = functools.partial(top_attend_kernel, len(aliases), item)
    return call(kernel, "top_attend", ins, outs, scratch, aliases)


def top_expand_kernel(n_alias, item, lengths, mixed, gain_ref, in_held, back_held, *rest):
    slope, keep_out, send_out, high, second_rows, active, sems = rest[n_alias:]
    place = Place(lengths)

    @pl.when(jnp.logical_not(place.is_lower))
    def _():
        sender = Sender(sems)
        expand_body(
            sender,
            place,
            item,
            False,
            mixed,
            gain_ref,
            (in_held, back_held),
            slope,
            (keep_out, send_out),
            second_rows,
            active,
            high,
        )
        sender.finish()


def top_expand(item, lengths, mixed, gains, in_held, back_held, earlier):
    outs = [
        ((ROWS, FF), BF16, "vmem"),
        ((MB * ROWS, KEPT), BF16, LEFTS),
        ((MB * ROWS, KEPT), BF16, LEFTS),
        ((ROWS, D), F32, "vmem"),
    ]
    ins = [(lengths, "smem")]
    ins += [(value, "vmem") for value in (mixed, gains, in_held, back_held)]
    ins, aliases = with_earlier(ins, outs, earlier)
    scratch = [
        pltpu.VMEM((ROWS, D), BF16),
        pltpu.VMEM((ROWS, FF), BF16),
        pltpu.SemaphoreType.DMA((4,)),
    ]
    kernel = functools.partial(top_expand_kernel, len(aliases), item)
    return call(kernel, "top_expand", ins, outs, scratch, aliases)


def top_expand_back_kernel(item, lengths, feeds, mixed, slope, gain_ref, in_held, back_held, *rest):
    target, gain_out, middle, inner, sems = rest
    place = Place(lengths)

    @pl.when(jnp.logical_not(place.is_lower))
    def _():
        sender = Sender(sems)
        expand_back_body(
            sender,
            place,
            item,
            False,
            feeds.at[pl.ds(item * ROWS, ROWS)],
            mixed,
            slope,
            gain_ref,
            (in_held, back_held),
            target.at[:, pl.ds(0, FF)],
            gain_out,
            middle,
            inner,
        )
        sender.finish()


def top_expand_back(item, lengths, feeds, mixed, slope, gains, in_held, back_held):
    outs = [grads_shapes(item)[0], ((1, D), F32, "vmem"), ((ROWS, D), F32, "vmem")]
    ins = [(lengths, "smem")]
    ins += [(value, "vmem") for value in (feeds, mixed, slope, gains, in_held, back_held)]
    scratch = [pltpu.VMEM((ROWS, FF), BF16), pltpu.SemaphoreType.DMA((1,))]
    kernel = functools.partial(top_expand_back_kernel, item)
    return call(kernel, "top_expand_back", ins, outs, scratch)


def top_attend_back_kernel(n_alias, item, lengths, rows_ref, middle, qkv_rows, probs, gain_ref, *rest):
    weights, rest = rest[:2], rest[2 + n_alias :]
    *targets, gain_out, low, outer, sems = rest
    if item < MB - 1:
        targets = [targets[0].at[:, pl.ds(FF, 4 * D)]]
    else:
        targets = [targets[0], targets[1].at[pl.ds(0, ROWS)]]
    place = Place(lengths)

    @pl.when(jnp.logical_not(place.is_lower))
    def _():
        sender = Sender(sems)
        low[...] = attend_back_body(
            sender, rows_ref, middle, qkv_rows, probs, gain_ref, weights, targets, gain_out, outer
        ).astype(BF16)
        sender.finish()


def top_attend_back(item, lengths, rows, middle, saved, gains, weights, earlier):
    shapes = grads_shapes(item)
    outs = [*(shapes[1:] or shapes), ((1, D), F32, "vmem"), ((ROWS, D), BF16, "vmem")]
    ins = [(lengths, "smem")]
    ins += [(value, "vmem") for value in (rows, middle, *saved, gains, *weights)]
    ins, aliases = with_earlier(ins, outs, earlier)
    scratch = [pltpu.VMEM((ROWS, 4 * D), BF16), pltpu.SemaphoreType.DMA((2,))]
    kernel = functools.partial(top_attend_back_kernel, len(aliases), item)
    return call(kernel, "top_attend_back", ins, outs, scratch, aliases)


def lower_expand_back_kernel(
    n_alias, item, lengths, grad_ref, mixed, slope, gain_ref, in_held, back_held, *rest
):
    target, gain_out, middle, inner, sems = rest[n_alias:]
    place = Place(lengths)

    @pl.when(place.is_lower)
    def _():
        sender = Sender(sems)
        expand_back_body(
            sender,
            place,
            item,
            True,
            grad_ref,
            mixed,
            slope,
            gain_ref,
            (in_held, back_held),
            grads_targets(item, [target])[0] if item < MB - 1 else target,
            gain_out,
            middle,
            inner,
        )
        sender.finish()


def lower_expand_back(item, lengths, grad, mixed, slope, gains, in_held, back_held, earlier):
    size = 1 << 13 if item < MB - 1 else 1
    outs = [grads_shapes(item)[0], ((1, D), F32, "vmem"), ((ROWS, D), F32, "vmem")]
    ins = [(lengths, "smem")]
    ins += [(value, "vmem") for value in (grad, mixed, slope, gains, in_held, back_held)]
    ins, aliases = with_earlier(ins, outs, earlier)
    scratch = [pltpu.VMEM((ROWS, FF), BF16), pltpu.SemaphoreType.DMA((1,))]
    kernel = functools.partial(lower_expand_back_kernel, len(aliases), item)
    return call(kernel, "lower_expand_back", ins, outs, scratch, aliases, size)


def lower_attend_back_kernel(n_alias, item, lengths, feeds, middle, qkv_rows, probs, gain_ref, *rest):
    weights, rest = rest[:2], rest[2:]
    tops, others, rest = rest[:MB], rest[MB : MB + 3], rest[MB + 3 + n_alias :]
    if item < MB - 1:
        grads, gain_out, ends_out, outer, high, sems = rest
        targets = [grads.at[:, pl.ds(FF, 4 * D)]]
    else:
        first, last, gain_out, ends_out, gain_keep, outer, high, gain_rows, sems = rest
        targets = [first, last.at[pl.ds(0, ROWS)]]
    place = Place(lengths)
    rows = pl.ds(item * ROWS, ROWS)

    @pl.when(place.is_lower)
    def _():
        sender = Sender(sems)
        high[...] = attend_back_body(
            sender,
            feeds.at[rows],
            middle,
            qkv_rows,
            probs,
            gain_ref,
            weights,
            targets,
            gain_out,
            outer,
        )
        sender.send(high, ends_out.at[rows])
        sender.finish()

    if item == MB - 1:
        sender = Sender(sems)

        @pl.when(jnp.logical_not(place.is_lower))
        def _():
            top_sender = Sender(sems)
            for top_item, top_high in enumerate(tops):
                top_sender.send(top_high, ends_out.at[pl.ds(top_item * ROWS, ROWS)])
            top_sender.finish()

        own, other = places(place.pos, HALF)
        gain_rows[...] = jnp.zeros_like(gain_rows)
        for row, parts in enumerate(((others[0], gain_out), others[1:])):
            gain_keep[row : row + 1] = parts[0][:, own] + parts[1][:, own]
            gain_rows[row : row + 1, pl.ds(0, HALF)] = parts[0][:, other] + parts[1][:, other]
        outer[pl.ds(0, 16), pl.ds(0, 2 * D)] = gain_rows[...].astype(BF16)
        sender.send(outer.at[pl.ds(0, 16), pl.ds(0, 2 * D)], last.at[pl.ds(ROWS, 16)])
        sender.finish()


def lower_attend_back(item, lengths, feeds, middle, saved, gains, weights, tops, others, earlier):
    size = 1 << 13 if item < MB - 1 else 1
    shapes = grads_shapes(item)
    outs = [
        *(shapes[1:] or shapes),
        ((1, D), F32, "vmem"),
        ((MB * ROWS, D), F32, "any"),
    ]
    scratch = [pltpu.VMEM((ROWS, 4 * D), BF16), pltpu.VMEM((ROWS, D), F32)]
    if item == MB - 1:
        outs.append(((2, HALF), F32, "vmem"))
        scratch.append(pltpu.VMEM((16, 2 * D), F32))
    scratch.append(pltpu.SemaphoreType.DMA((3,)))
    ins = [(lengths, "smem")]
    ins += [(value, "vmem") for value in (feeds, middle, *saved, gains, *weights, *tops, *others)]
    ins, aliases = with_earlier(ins, outs, earlier)
    kernel = functools.partial(lower_attend_back_kernel, len(aliases), item)
    return call(kernel, "lower_attend_back", ins, outs, scratch, aliases, size)


def expert_rows(place, item, partner, expert, live_only=False):
    row = lax.broadcasted_iota(jnp.int32, (1, ROWS), 1)
    first, second = place.experts(item, partner)
    mine = jnp.where(row < IMAGE_ROWS, first, second) == expert
    if live_only:
        mine = mine & (row < place.live(item, partner))
    return mine


def bits_but(*taken):
    count = lax.axis_size("dp").bit_length() - 1
    return [bit for bit in reversed(range(count)) if bit not in taken]


def block_numbers(first_bit):
    here = (lax.axis_index("dp") >> first_bit) & 1
    rest = bits_but(first_bit)
    for number in range(1 << len(rest)):
        where = tuple((number >> (len(rest) - 1 - place)) & 1 for place in range(len(rest)))
        base = sum(value << bit for value, bit in zip(where, rest))
        yield where, base + (here << first_bit), base + ((1 - here) << first_bit)


def write_blocks(total, rows, first_bit, mine, theirs):
    for where, own, other in block_numbers(first_bit):
        own_at = pl.ds(pl.multiple_of(own * rows, rows), rows)
        other_at = pl.ds(pl.multiple_of(other * rows, rows), rows)
        mine[where] = total[own_at].astype(BF16)
        theirs[where] = total[other_at].astype(BF16)


def back_grads_kernel(orders, n_items, lengths, *refs):
    actives, grads, feeds = refs[:n_items], refs[n_items : 2 * n_items], refs[2 * n_items : 2 * n_items + 2]
    outs, (flipped, total) = refs[2 * n_items + 2 : -2], refs[-2:]
    place = Place(lengths)
    tail = ROWS - TAIL
    rows = D // lax.axis_size("dp")

    @pl.when(pl.program_id(0) == 0)
    def _():
        for index in range(n_items):
            item, partner = index % MB, index >= MB
            top = feeds[index // MB][pl.ds(item * ROWS, ROWS)]
            value = jnp.where(place.is_lower, grads[index][...], top).T
            for expert in (0, 1):
                mask = expert_rows(place, item, partner, expert, live_only=True)
                flipped[expert, :, pl.ds(index * ROWS, ROWS)] = jnp.where(mask, value, 0)

    def finished(expert):
        write_blocks(total, rows, orders[expert][0], outs[2 * expert], outs[2 * expert + 1])

    def whole(expert):
        result = None
        for index in range(n_items):
            term = dot_nn(flipped[expert, :, pl.ds(index * ROWS, ROWS)], actives[index][...])
            result = term if result is None else result + term
        total[...] = result

    whole(0)
    finished(0)

    @pl.when(place.is_lower)
    def _():
        left = [
            flipped[1, :, pl.ds(index * ROWS + ROWS // 2, ROWS // 2)] for index in range(n_items)
        ]
        right = [actives[index][pl.ds(ROWS // 2, ROWS // 2)] for index in range(n_items)]
        total[...] = dot_nn(jnp.concatenate(left, axis=1), jnp.concatenate(right, axis=0))

    @pl.when(jnp.logical_not(place.is_lower))
    def _():
        whole(1)

    finished(1)


def halves_shape(block):
    return jax.ShapeDtypeStruct((2,) * len(bits_but(0)) + block, BF16)


def halves_spec(block, place):
    lead = len(bits_but(0))
    return pl.BlockSpec((2,) * lead + block, lambda step: (0,) * lead + place(step))


def by_item(width, count, column, **options):
    return [
        pl.BlockSpec((ROWS, width), lambda step, item=index % MB: (item, column(step)), **options)
        for index in range(count)
    ]


def back_grads(lengths, kept, grads, feeds, orders):
    width = 256
    block = (D // lax.axis_size("dp"), width)
    once = pl.Buffered(1)
    fixed = [pl.BlockSpec((ROWS, D), lambda step: (0, 0), pipeline_mode=once)] * len(kept)
    fixed += [pl.BlockSpec((MB * ROWS, D), lambda step: (0, 0), pipeline_mode=once)] * 2
    results = pl.pallas_call(
        functools.partial(back_grads_kernel, orders, len(kept)),
        grid=(FF_HALF // width,),
        out_shape=[halves_shape((block[0], FF_HALF)) for _ in orders for _ in (0, 1)],
        in_specs=[pl.BlockSpec(memory_space=pltpu.SMEM)]
        + by_item(width, len(kept), lambda step: step)
        + fixed,
        out_specs=[
            halves_spec(block, lambda step: (0, step)) for _ in orders for _ in (0, 1)
        ],
        scratch_shapes=[
            pltpu.VMEM((2, D, len(kept) * ROWS), BF16),
            pltpu.VMEM((D, width), F32),
        ],
        compiler_params=pltpu.CompilerParams(vmem_limit_bytes=VMEM_BYTES),
        cost_estimate=cost(1),
        name="back_grads",
    )(lengths, *kept, *grads, *feeds)
    return [tuple(results[2 * expert : 2 * expert + 2]) for expert in (0, 1)]


def in_grads_kernel(width, n_items, lengths, *refs):
    seconds, inners = refs[:n_items], refs[n_items : 2 * n_items]
    outs, (flipped, total) = refs[2 * n_items : -2], refs[-2:]
    place = Place(lengths)
    half = ROWS // 2
    low_bit = lax.axis_index("dp") % 2

    @pl.when(pl.program_id(0) == 0)
    def _():
        for index in range(n_items):
            item, partner = index % MB, index >= MB
            value = seconds[index][...].T
            for expert in (0, 1):
                mask = expert_rows(place, item, partner, expert)
                flipped[expert, :, pl.ds(index * ROWS, ROWS)] = jnp.where(mask, value, 0)

    def whole(expert):
        result = None
        for index in range(n_items):
            term = dot_nn(flipped[expert, :, pl.ds(index * ROWS, ROWS)], inners[index][...])
            result = term if result is None else result + term
        total[...] = result

    def finished(expert):
        if len(outs) == 2:
            outs[expert][0] = total[...].astype(BF16)
            return
        for out, bit in zip(outs[2 * expert : 2 * expert + 2], (low_bit, 1 - low_bit)):
            out[0] = total[:, pl.ds(pl.multiple_of(bit * width, width), width)].astype(BF16)

    whole(0)
    finished(0)

    @pl.when(place.is_lower)
    def _():
        left = [flipped[1, :, pl.ds(index * ROWS + half, half)] for index in range(n_items)]
        right = [inners[index][pl.ds(half, half)] for index in range(n_items)]
        total[...] = dot_nn(jnp.concatenate(left, axis=1), jnp.concatenate(right, axis=0))

    @pl.when(jnp.logical_not(place.is_lower))
    def _():
        whole(1)

    finished(1)


def in_grads(lengths, kept, inners):
    size = lax.axis_size("dp")
    width = FF // size
    aligned = width % 128 == 0
    columns = 2 * width if aligned else D
    steps = FF // columns
    once = pl.Buffered(1)
    block = (1, HALF, width if aligned else columns)
    count = 4 if aligned else 2
    results = pl.pallas_call(
        functools.partial(in_grads_kernel, width, len(kept)),
        grid=(steps,),
        out_shape=[jax.ShapeDtypeStruct((steps,) + block[1:], BF16)] * count,
        in_specs=[pl.BlockSpec(memory_space=pltpu.SMEM)]
        + by_item(HALF, len(kept), lambda step: FF_HALF // HALF, pipeline_mode=once)
        + [pl.BlockSpec((ROWS, columns), lambda step: (0, step))] * len(inners),
        out_specs=[pl.BlockSpec(block, lambda step: (step, 0, 0))] * count,
        scratch_shapes=[
            pltpu.VMEM((2, HALF, len(kept) * ROWS), BF16),
            pltpu.VMEM((HALF, columns), F32),
        ],
        compiler_params=pltpu.CompilerParams(vmem_limit_bytes=VMEM_BYTES),
        cost_estimate=cost(1),
        name="in_grads",
    )(lengths, *kept, *inners)
    if not aligned:
        whole = [part.transpose(1, 0, 2).reshape(HALF, size, width) for part in results]
        return [by_lowest_bit(part.transpose(1, 0, 2)) for part in whole]
    shape = (2,) * len(bits_but(0)) + block[1:]
    return [tuple(part.reshape(shape) for part in results[2 * e : 2 * e + 2]) for e in (0, 1)]


def outer_grads_kernel(order, *refs):
    lefts, outers, gains, pieces, total = refs[:4], refs[4:10], refs[10:12], refs[12:16], refs[16]
    step = pl.program_id(0)
    result = None
    for index in range(4):
        outer = outers[3 * (index // MB)][...]
        if index % MB == MB - 1:
            first, second = outers[3 * (index // MB) + 1 : 3 * (index // MB) + 3]
            outer = jnp.where(step < 2, first[...], second[...])
        term = dot_tn(outer, lefts[index][...])
        result = term if result is None else result + term
    total[pl.ds(pl.multiple_of(step * D, D), D)] = result

    @pl.when(step == 3)
    def _():
        size = lax.axis_size("dp")
        proj_rows = D // size
        gain_rows = gains[0][...] + gains[1][pl.ds(0, 2), pl.ds(0, HALF)].astype(F32)
        gain_rows = jnp.concatenate([gain_rows, jnp.zeros((14, HALF), F32)], axis=0)
        for where, *numbers in block_numbers(order[0]):
            for target, number in zip((0, 1), numbers):
                at = pl.multiple_of(number * 3 * proj_rows, proj_rows)
                below = pl.multiple_of(3 * D + number * proj_rows, proj_rows)
                first, second = pieces[target], pieces[2 + target]
                first[where] = total[pl.ds(at, 2 * proj_rows)].astype(BF16)
                second[where + (pl.ds(0, proj_rows),)] = total[
                    pl.ds(at + 2 * proj_rows, proj_rows)
                ].astype(BF16)
                second[where + (pl.ds(proj_rows, proj_rows),)] = total[
                    pl.ds(below, proj_rows)
                ].astype(BF16)
                turned = pltpu.roll(gain_rows, HALF - number * (HALF // size), 1)
                second[where + (pl.ds(2 * proj_rows, 16),)] = turned.astype(BF16)


def outer_grads(kept, outers, gains, order):
    block = (2 * D // lax.axis_size("dp"), HALF)
    last = (block[0] + 16, HALF)
    results = pl.pallas_call(
        functools.partial(outer_grads_kernel, order),
        grid=(4,),
        out_shape=[halves_shape(block)] * 2 + [halves_shape(last)] * 2,
        in_specs=by_item(HALF, 4, lambda step: FF_HALF // HALF + 1 + step // 3)
        + [
            pl.BlockSpec((ROWS, D), lambda step: (0, FF // D + step)),
            pl.BlockSpec((ROWS, D), lambda step: (0, jnp.minimum(step, 1))),
            pl.BlockSpec((ROWS, D), lambda step: (0, jnp.maximum(step - 2, 0))),
        ]
        * 2
        + [
            pl.BlockSpec((2, HALF), lambda step: (0, 0)),
            pl.BlockSpec((16, D), lambda step: (ROWS // 16, 0)),
        ],
        out_specs=[halves_spec(block, lambda step: (0, 0))] * 2
        + [halves_spec(last, lambda step: (0, 0))] * 2,
        scratch_shapes=[pltpu.VMEM((4 * D, HALF), F32)],
        compiler_params=pltpu.CompilerParams(vmem_limit_bytes=2 * VMEM_BYTES),
        cost_estimate=cost(1),
        name="outer_grads",
    )(*kept, *outers, *gains)
    return tuple(results[:2]), tuple(results[2:])


def swapped(block, axis, bit, among=None):
    among = range(lax.axis_size(axis)) if among is None else among
    return lax.ppermute(block, axis, [(place, place ^ 1 << bit) for place in among])


def per_item(arrays):
    return [array for array in arrays for _ in range(MB)]


def passed_along(value, steps):
    count = lax.axis_size("section")
    first, last = (max(0, -steps), min(count, count - steps))
    route = [(source, source + steps) for source in range(first, last)]
    return lax.ppermute(value, "section", route)


def split_bit(stacked, bit):
    here = (lax.axis_index("dp") >> bit) & 1
    mine = lax.dynamic_index_in_dim(stacked, here, 0, keepdims=False)
    theirs = lax.dynamic_index_in_dim(stacked, 1 - here, 0, keepdims=False)
    return mine, theirs


def added_kernel(left, right, out):
    out[...] = left[...].astype(F32) + right[...].astype(F32)


def added(left, right):
    ins = [(left, "vmem"), (right, "vmem")]
    return call(added_kernel, "added", ins, [(left.shape, F32, "vmem")], [])[0]


def outer_sums_kernel(first, left, right, qkv_out, proj_out, gain_out):
    rows = proj_out.shape[0]
    second = left[...].astype(F32) + right[...].astype(F32)
    qkv_out[: 2 * rows] = first[...]
    qkv_out[2 * rows :] = second[:rows]
    proj_out[...] = second[rows : 2 * rows]
    gain_out[...] = second[2 * rows : 2 * rows + 2]


def outer_sums(first, left, right):
    rows = first.shape[0] // 2
    ins = [(value, "vmem") for value in (first, left, right)]
    shapes = [(3 * rows, HALF), (rows, HALF), (2, HALF)]
    outs = [(shape, F32, "auto") for shape in shapes]
    return call(outer_sums_kernel, "outer_sums", ins, outs, [])


def added_halves_kernel(axis, bit, left, right, mine, theirs):
    here = (lax.axis_index("dp") >> bit) & 1
    lead = (slice(None),) * axis
    for out, at in ((mine, lead + (here,)), (theirs, lead + (1 - here,))):
        out[...] = (left[at].astype(F32) + right[at].astype(F32)).astype(BF16)


def added_halves(left, right, axis, bit):
    ins = [(left, "vmem"), (right, "vmem")]
    outs = [(left.shape[:axis] + left.shape[axis + 1 :], BF16, "vmem")] * 2
    kernel = functools.partial(added_halves_kernel, axis, bit)
    return call(kernel, "added_halves", ins, outs, [])


def after(value, *earlier):
    return lax.optimization_barrier((value, earlier))[0]


class Sums:
    def __init__(self):
        self.open = {}
        self.results = {}
        self.last = []

    def begin(self, name, piece, order, taken=()):
        mine, theirs = piece
        self.open[name] = (mine, swapped(theirs, "dp", order[0]), order[1:], (*taken, order[0]))

    def step(self, name, hold=False):
        mine, got, rest, taken = self.open.pop(name)
        mine = after(mine, *self.last)
        if len(rest) == 0:
            self.results[name] = added(mine, got)
            self.last = [self.results[name]]
            return
        mine, theirs = added_halves(mine, got, bits_but(*taken).index(rest[0]), rest[0])
        self.last = [theirs]
        if hold:
            return (mine, theirs), rest, taken
        self.begin(name, (mine, theirs), rest, taken)

    def finish(self, but):
        while len(self.open) > 1 or len(self.open[but][2]) > 0:
            for name in list(self.open):
                if name != but or len(self.open[name][2]) > 0:
                    self.step(name)
        mine, got, *_ = self.open.pop(but)
        return after(mine, *self.last), got


def by_lowest_bit(stacked):
    bits = lax.axis_size("dp").bit_length() - 1
    split = jnp.moveaxis(stacked.reshape((2,) * bits + stacked.shape[1:]), bits - 1, 0)
    return split_bit(split, 0)


def shards(feeds, text_lengths, norm_gains, qkv_weight, out_weight, expert_in, expert_out):
    n_dp = lax.axis_size("dp")
    bits = n_dp.bit_length() - 1
    pos = lax.axis_index("section") % 2

    gains_other = swapped(norm_gains[0], "section", 0)
    gains = joined_gains(norm_gains[0], gains_other)
    own = [qkv_weight[0], out_weight[0]]
    other = [swapped(part, "section", 0) for part in own]
    held = joined_halves(own, other)
    in_other = swapped(after(expert_in[0], gains_other, *other), "section", 0)
    back_other = swapped(after(expert_out[0], gains_other, *other), "section", 0)

    *saved, keep, send = lower_attend(text_lengths, feeds, gains, *held)
    saved = [saved[3 * item : 3 * item + 3] for item in range(MB)]
    earlier = saved[-1][2]
    held += joined_halves([expert_in[0]], [after(in_other, earlier)])
    held += joined_halves([expert_out[0]], [after(back_other, earlier)])
    slopes, passed = [], []
    for item in range(MB):
        mixed = after(saved[item][2], earlier)
        slope, keep, send, earlier = lower_expand(
            item, text_lengths, mixed, gains, *held[2:], {1: keep, 2: send}
        )
        slopes.append(slope)
        passed.append(passed_along(earlier, 2))
    grads, gain_grads, ups = [], [], []
    tops = []
    for item in range(MB):
        rows = after(passed[item], earlier)
        places = dict(enumerate(saved[item])) | {3: keep, 4: send}
        *saved[item], keep, send = top_attend(
            item, text_lengths, rows, gains, *held[:2], places
        )
        mixed = saved[item][2]
        places = {0: slopes[item], 1: keep, 2: send}
        slopes[item], keep, send, top = top_expand(
            item, text_lengths, mixed, gains, *held[2:], places
        )
        tops.append(top)
        inner, gain_second, middle = top_expand_back(
            item, text_lengths, feeds, mixed, slopes[item], gains, *held[2:]
        )
        *outer, gain_first, earlier = top_attend_back(
            item,
            text_lengths,
            rows,
            middle,
            saved[item][:2],
            gains,
            held[:2],
            {0: inner} if item < MB - 1 else {},
        )
        grads.append(outer if item < MB - 1 else [inner, *outer])
        gain_grads.append([gain_first, gain_second])
        ups.append(passed_along(earlier, -2))
    feeds_pair = [feeds, swapped(after(feeds, earlier), "section", 0, (2, 3))]
    lefts = per_item([keep, swapped(after(send, earlier), "section", 0)])

    upward = tuple(range(bits))
    back_orders = [upward[1:] + upward[:1], upward]

    def lower_back_experts(item, up):
        results = {0: grads[item][0], 1: gain_grads[item][1]}
        grads[item][0], gain_grads[item][1], middle = lower_expand_back(
            item, text_lengths, up, saved[item][2], slopes[item], gains, *held[2:], results
        )
        return middle

    def lower_back_heads(item, middle, ends, others):
        first = 0 if item < MB - 1 else 1
        parts = [*grads[item][first:], gain_grads[item][0], *ends]
        results = lower_attend_back(
            item,
            text_lengths,
            feeds,
            middle,
            saved[item][:2],
            gains,
            held[:2],
            tops,
            others,
            dict(enumerate(parts)),
        )
        count = len(grads[item]) - first
        grads[item][first:], gain_grads[item][0] = results[:count], results[count]
        return results[count + 1 :]

    ups[0] = after(ups[0], earlier)
    ups_other = [swapped(ups[0], "section", 0, (0, 1))]
    middle = lower_back_experts(0, ups[0])
    (ends,) = lower_back_heads(0, middle, [], [gain_grads[0][1]] * 3)
    first_grads = [grads[0][0], swapped(grads[0][0], "section", 0)]
    ups[1] = after(ups[1], ends)
    ups_other.append(swapped(ups[1], "section", 0, (0, 1)))
    middle = lower_back_experts(1, after(ups[1], ups_other[0]))
    inner = grads[1][0]
    inners = [first_grads[0], inner, first_grads[1], swapped(inner, "section", 0)]
    ups_other[1] = after(ups_other[1], middle)
    back_pieces = back_grads(text_lengths, lefts, ups + ups_other, feeds_pair, back_orders)
    inners[1] = after(inners[1], back_pieces[0][1], back_pieces[1][1])
    in_pieces = in_grads(text_lengths, lefts, inners)

    sums = Sums()
    for number in (0, 1):
        sums.begin(f"back{number}", back_pieces[number], back_orders[number])
    sums.begin("in0", in_pieces[0], upward)
    middle = after(middle, in_pieces[0][1], in_pieces[1][1])
    others = [gain_grads[0][0], gain_grads[0][1], gain_grads[1][1]]
    ends, gain_keep = lower_back_heads(1, middle, [ends], others)
    outers = [first_grads[0], *grads[1][1:], first_grads[1]]
    outers += [swapped(part, "section", 0) for part in grads[1][1:]]
    sums.last = [ends]
    sums.step("back0")
    gain_keep = after(gain_keep, *sums.last)
    outer_pieces = outer_grads(lefts, outers, (gain_keep, outers[-1]), upward)
    sums.last = [piece[1] for piece in outer_pieces]
    sums.step("back1")

    def later(piece):
        return piece[0], after(piece[1], *sums.last)

    sums.begin("in1", later(in_pieces[1]), upward)
    sums.begin("outer0", later(outer_pieces[0]), upward)
    for name in ("back0", "in0", "back1", "in0", "in1", "back1"):
        sums.step(name)
    sums.begin("outer1", later(outer_pieces[1]), upward)
    order = ("outer0", "in1", "in0", "outer1", "outer0", "in1", "outer1", "outer0", "back0")
    for name in order:
        sums.step(name)
    last = sums.finish("outer1")
    qkv_sum, proj_sum, gain_sum = outer_sums(sums.results["outer0"], *last)
    done = sums.results
    return (
        ends,
        gain_sum[None, :, : HALF // n_dp],
        qkv_sum.T[None],
        proj_sum.T[None],
        jnp.stack([done["in0"], done["in1"]])[None],
        jnp.stack([done["back0"].T, done["back1"].T])[None],
    )


def solution(mesh):
    return jax.shard_map(
        shards,
        mesh=mesh,
        in_specs=(
            P(("dp", "section"), None),
            P("dp"),
            P("section", None, None),
            P("section", None, None),
            P("section", None, None),
            P("section", None, None, None),
            P("section", None, None, None),
        ),
        out_specs=(
            P(("dp", "section"), None),
            P("section", None, "dp"),
            P("section", None, "dp"),
            P("section", None, "dp"),
            P("section", None, None, "dp"),
            P("section", None, None, "dp"),
        ),
        check_vma=False,
    )
```

```python
import functools

import jax
import jax.numpy as jnp
from jax import lax
from jax.experimental import pallas as pl
from jax.experimental.pallas import tpu as pltpu
from jax.sharding import PartitionSpec as P

D = 768
HALF = D // 2
HEADS = 12
FF = 3072
FF_HALF = FF // 2
HEAD_DIM = 64
IMAGE_ROWS = 197
ROWS = 256
MB = 2
KEPT = FF_HALF + 3 * HALF
TAIL = 192

EPSILON = 1e-05
MASKED = -1e30
F32 = jnp.float32
BF16 = jnp.bfloat16
VMEM_BYTES = 10 * 1024 * 1024
LEFTS = "any"


def cost(size):
    return pl.CostEstimate(flops=size << 20, bytes_accessed=1 << 10, transcendentals=0)


def dot_nn(left, right):
    return lax.dot_general(left, right, (((1,), (0,)), ((), ())), preferred_element_type=F32)


def dot_nt(left, right):
    return lax.dot_general(left, right, (((1,), (1,)), ((), ())), preferred_element_type=F32)


def dot_tn(left, right):
    return lax.dot_general(left, right, (((0,), (0,)), ((), ())), preferred_element_type=F32)


def norm_parts(hidden):
    centred = hidden - jnp.mean(hidden, axis=-1, keepdims=True)
    spread = jnp.mean(centred * centred, axis=-1, keepdims=True)
    inverse = lax.rsqrt(spread + EPSILON)
    return centred * inverse, inverse


def norm_back(grad, hidden, gain_row):
    unit, inverse = norm_parts(hidden)
    gain_grad = jnp.sum(grad * unit, axis=0, keepdims=True)
    scaled = grad * gain_row
    mean_plain = jnp.mean(scaled, axis=-1, keepdims=True)
    mean_unit = jnp.mean(scaled * unit, axis=-1, keepdims=True)
    return inverse * (scaled - mean_plain - unit * mean_unit), gain_grad


def gelu_pair(values):
    size = jnp.abs(values)
    denom = 1.0 + (0.3275911 * 0.7071067811865476) * size
    t = pl.reciprocal(denom, approx=True)
    poly = 0.5 * 1.061405429
    for factor in (-1.453152027, 1.421413741, -0.284496736, 0.254829592):
        poly = poly * t + 0.5 * factor
    bell = jnp.exp2(values * values * (-0.5 * 1.4426950408889634))
    upper_tail = poly * t * bell
    cdf = jnp.where(values < 0, upper_tail, 1.0 - upper_tail)
    return values * cdf, cdf + values * bell * 0.3989422804014327


def lane_half(value, which):
    lanes = lax.broadcasted_iota(jnp.int32, value.shape, 1)
    picked = lanes < HEAD_DIM if which == 0 else lanes >= HEAD_DIM
    return jnp.where(picked, value, jnp.zeros_like(value))


def call(kernel, name, ins, outs, scratch, aliases=None, size=1, memory=VMEM_BYTES):
    spaces = {"vmem": pltpu.VMEM, "auto": pltpu.VMEM, "smem": pltpu.SMEM, "any": pl.ANY, "hbm": pltpu.HBM}
    kinds = {"vmem": pltpu.VMEM, "auto": jax.ShapeDtypeStruct, "any": jax.ShapeDtypeStruct, "hbm": pltpu.HBM}
    shapes = [kinds[space](shape, kind) for shape, kind, space in outs]
    return pl.pallas_call(
        kernel,
        out_shape=shapes,
        in_specs=[pl.BlockSpec(memory_space=spaces[space]) for _, space in ins],
        out_specs=[pl.BlockSpec(memory_space=spaces[space]) for _, _, space in outs],
        input_output_aliases=aliases or {},
        scratch_shapes=scratch,
        compiler_params=pltpu.CompilerParams(vmem_limit_bytes=memory),
        cost_estimate=cost(size),
        name=name,
    )(
        *[
            pltpu.with_memory_space_constraint(value, pltpu.HBM) if space == "hbm" else value
            for value, space in ins
        ]
    )


class Place:
    def __init__(self, lengths):
        section = lax.axis_index("section")
        self.lengths = lengths
        self.is_lower = section < 2
        self.pos = section % 2

    def length(self, item, partner=False):
        pos = 1 - self.pos if partner else self.pos
        return self.lengths[pos * MB + item]

    def live(self, item, partner=False):
        return IMAGE_ROWS + self.length(item, partner)

    def experts(self, item, partner=False):
        kind = jnp.where(self.length(item, partner) > 0, 1, 0)
        return jnp.where(self.is_lower, 0, kind), jnp.where(self.is_lower, 1, kind)


def with_earlier(ins, outs, earlier):
    aliases = {}
    for number, value in (earlier or {}).items():
        aliases[len(ins)] = number
        ins = ins + [(value, outs[number][2])]
    return ins, aliases


class Sender:
    def __init__(self, sems):
        self.sems = sems
        self.sent = []
        self.done = 0

    def send(self, source, target):
        copy = pltpu.make_async_copy(source, target, self.sems.at[len(self.sent)])
        copy.start()
        self.sent.append(copy)

    def finish(self, count=None):
        count = len(self.sent) - self.done if count is None else count
        for copy in self.sent[self.done : self.done + count]:
            copy.wait()
        self.done += count


def join_kernel(count, *refs):
    own, other, joined, sems = refs[:count], refs[count : 2 * count], refs[2 * count : -1], refs[-1]
    pos = lax.axis_index("section") % 2
    sender = Sender(sems)
    for mine, theirs, whole in zip(own, other, joined):
        depth = mine.shape[-2]
        for source, at in ((mine, pos), (theirs, 1 - pos)):
            rows = pl.ds(pl.multiple_of(at * depth, depth), depth)
            if len(whole.shape) == 2:
                sender.send(source, whole.at[rows])
            else:
                for expert in range(whole.shape[0]):
                    sender.send(source.at[expert], whole.at[expert, rows])
    sender.finish()


def joined_halves(own, other):
    outs = []
    for part in own:
        shape = part.shape[:-2] + (2 * part.shape[-2], part.shape[-1])
        outs.append((shape, BF16, "vmem"))
    return call(
        functools.partial(join_kernel, len(own)),
        "joined_halves",
        [(value, "hbm") for value in own] + [(value, "any") for value in other],
        outs,
        [pltpu.SemaphoreType.DMA((4 * len(own),))],
    )


def gains_kernel(own, other, gains):
    first = lax.axis_index("section") % 2 == 0
    mine, theirs = own[...].astype(F32), other[...].astype(F32)
    gains[:, pl.ds(0, HALF)] = jnp.where(first, mine, theirs)
    gains[:, pl.ds(HALF, HALF)] = jnp.where(first, theirs, mine)


def joined_gains(own, other):
    return call(
        gains_kernel, "joined_gains", [(own, "vmem"), (other, "vmem")], [((2, D), F32, "vmem")], []
    )[0]


def places(pos, size):
    return (
        pl.ds(pl.multiple_of(pos * size, size), size),
        pl.ds(pl.multiple_of((1 - pos) * size, size), size),
    )


def attend_body(
    sender, place, item, rows_ref, gain_ref, weights, qkv_rows, probs, mixed, lefts, left_rows
):
    qkv_held, proj_held = weights
    own, other = places(place.pos, HALF)

    def send_halves(part):
        to = (pl.ds(item * ROWS, ROWS), pl.ds(FF_HALF + (1 + part) * HALF, HALF))
        for columns, target in zip((own, other), lefts):
            sender.send(left_rows.at[part, :, columns], target.at[to])

    normed = (norm_parts(rows_ref[...].astype(F32))[0] * gain_ref[0:1]).astype(BF16)
    left_rows[0] = normed
    send_halves(0)
    for part in range(3):
        columns = pl.ds(part * D, D)
        qkv_rows[:, columns] = dot_nn(normed, qkv_held[:, columns]).astype(BF16)
    keys_live = lax.broadcasted_iota(jnp.int32, (ROWS, ROWS), 1) < place.live(item)
    for pair in range(HEADS // 2):
        queries = qkv_rows[:, pl.ds(pair * 128, 128)] * jnp.asarray(HEAD_DIM**-0.5, BF16)
        keys = qkv_rows[:, pl.ds(D + pair * 128, 128)]
        values = qkv_rows[:, pl.ds(2 * D + pair * 128, 128)]
        context = None
        for which in (0, 1):
            scores = dot_nt(lane_half(queries, which), keys)
            scores = jnp.where(keys_live, scores, MASKED)
            shifted = jnp.exp(scores - jnp.max(scores, axis=-1, keepdims=True))
            total = jnp.sum(shifted, axis=-1, keepdims=True)
            weight = (shifted * pl.reciprocal(total, approx=True)).astype(BF16)
            probs[2 * pair + which] = weight
            term = dot_nn(weight, lane_half(values, which))
            context = term if context is None else context + term
        left_rows[1, :, pl.ds(pair * 128, 128)] = context.astype(BF16)
    send_halves(1)
    mixed[...] = rows_ref[...].astype(F32) + dot_nn(left_rows[1], proj_held[...])


def expand_body(
    sender, place, item, lower, mixed, gain_ref, weights, slope, lefts, second_rows, active, high
):
    in_held, back_held = weights
    first, second = place.experts(item)
    halves, deep_halves = places(place.pos, HALF), places(place.pos, FF_HALF)
    rows = pl.ds(item * ROWS, ROWS)

    def send_active():
        for columns, target in zip(deep_halves, lefts):
            sender.send(active.at[:, columns], target.at[rows, pl.ds(0, FF_HALF)])

    normed = (norm_parts(mixed[...])[0] * gain_ref[1:2]).astype(BF16)
    second_rows[...] = normed
    for columns, target in zip(halves, lefts):
        sender.send(second_rows.at[:, columns], target.at[rows, pl.ds(FF_HALF, HALF)])
    total = mixed[...]
    for part in range(4):
        columns = pl.ds(part * D, D)
        value, derivative = gelu_pair(dot_nn(normed, in_held[first, :, columns]))
        value = value.astype(BF16)
        active[:, columns] = value
        slope[:, columns] = derivative.astype(BF16)
        total = total + dot_nn(value, back_held[first, columns])
    if not lower:
        send_active()
    high[...] = total
    if not lower:
        return
    tail = pl.ds(TAIL, ROWS - TAIL)
    later = lax.broadcasted_iota(jnp.int32, (ROWS - TAIL, D), 0) >= IMAGE_ROWS - TAIL
    total = mixed[tail]
    for part in range(4):
        columns = pl.ds(part * D, D)
        value, derivative = gelu_pair(dot_nn(second_rows[tail], in_held[second, :, columns]))
        kept = active[tail, columns].astype(F32)
        value = jnp.where(later, value, kept).astype(BF16)
        active[tail, columns] = value
        kept = slope[tail, columns].astype(F32)
        slope[tail, columns] = jnp.where(later, derivative, kept).astype(BF16)
        total = total + dot_nn(value, back_held[second, columns])
    send_active()
    high[tail] = jnp.where(later, total, high[tail])


def expand_back_body(
    sender, place, item, lower, grad_ref, mixed, slope, gain_ref, weights, target, gain_out, middle, inner
):
    in_held, back_held = weights
    first, second = place.experts(item)
    is_live = lax.broadcasted_iota(jnp.int32, (ROWS, D), 0) < place.live(item)
    grad = jnp.where(is_live, grad_ref[...].astype(F32), 0.0)
    grad_low = grad.astype(BF16)
    for part in range(4):
        columns = pl.ds(part * D, D)
        grad_active = dot_nt(grad_low, back_held[first, columns])
        inner[:, columns] = (grad_active * slope[:, columns].astype(F32)).astype(BF16)
    if not lower:
        sender.send(inner, target)
    middle[...] = dot_nt(inner[...], in_held[first])
    if lower:
        tail = pl.ds(TAIL, ROWS - TAIL)
        later = lax.broadcasted_iota(jnp.int32, (ROWS - TAIL, D), 0) >= IMAGE_ROWS - TAIL
        for part in range(4):
            columns = pl.ds(part * D, D)
            grad_active = dot_nt(grad_low[TAIL:], back_held[second, columns])
            patched = grad_active * slope[tail, columns].astype(F32)
            kept = inner[tail, columns].astype(F32)
            inner[tail, columns] = jnp.where(later, patched, kept).astype(BF16)
        sender.send(inner, target)
        patched = dot_nt(inner[tail], in_held[second])
        middle[tail] = jnp.where(later, patched, middle[tail])
    grad_mixed, gain_out[...] = norm_back(middle[...], mixed[...], gain_ref[1:2])
    middle[...] = grad + grad_mixed


def attend_back_body(
    sender, rows_ref, middle, qkv_rows, probs, gain_ref, weights, targets, gain_out, outer
):
    qkv_held, proj_held = weights
    branch = middle[...].astype(BF16)
    outer[:, pl.ds(3 * D, D)] = branch
    grad_context = dot_nt(branch, proj_held[...]).astype(BF16)
    scale = jnp.asarray(HEAD_DIM**-0.5, BF16)
    grad_normed = None
    for pair in range(HEADS // 2):
        queries = qkv_rows[:, pl.ds(pair * 128, 128)] * scale
        keys = qkv_rows[:, pl.ds(D + pair * 128, 128)] * scale
        values = qkv_rows[:, pl.ds(2 * D + pair * 128, 128)]
        context = grad_context[:, pair * 128 : (pair + 1) * 128]
        grad_q = grad_k = grad_v = None
        for which in (0, 1):
            weight = probs[2 * pair + which]
            context_half = lane_half(context, which)
            grad_probs = dot_nt(context_half, values)
            weight_wide = weight.astype(F32)
            product = weight_wide * grad_probs
            row_total = jnp.sum(product, axis=-1, keepdims=True)
            grad_scores = (product - weight_wide * row_total).astype(BF16)
            term_v = dot_tn(weight, context_half)
            term_q = dot_nn(grad_scores, lane_half(keys, which))
            term_k = dot_tn(grad_scores, lane_half(queries, which))
            grad_q = term_q if grad_q is None else grad_q + term_q
            grad_k = term_k if grad_k is None else grad_k + term_k
            grad_v = term_v if grad_v is None else grad_v + term_v
        outer[:, pl.ds(pair * 128, 128)] = grad_q.astype(BF16)
        outer[:, pl.ds(D + pair * 128, 128)] = grad_k.astype(BF16)
        outer[:, pl.ds(2 * D + pair * 128, 128)] = grad_v.astype(BF16)
        if pair % 2 == 1:
            for part in range(3):
                columns = pl.ds(part * D + (pair - 1) * 128, 256)
                term = dot_nt(outer[:, columns], qkv_held[:, columns])
                grad_normed = term if grad_normed is None else grad_normed + term
    width = 4 * D // len(targets)
    for part, target in enumerate(targets):
        sender.send(outer.at[:, pl.ds(part * width, width)], target)
    grad_hidden, gain_out[...] = norm_back(grad_normed, rows_ref[...].astype(F32), gain_ref[0:1])
    return middle[...] + grad_hidden


def saved_shapes():
    return [((ROWS, 3 * D), BF16), ((HEADS, ROWS, ROWS), BF16), ((ROWS, D), F32)]


def grads_shapes(item):
    inner = ((ROWS, FF), BF16, "any")
    if item < MB - 1:
        return [inner, ((ROWS, 4 * D), BF16, "any")]
    return [inner, ((ROWS, 2 * D), BF16, "any"), ((ROWS + 16, 2 * D), BF16, "any")]


def lower_attend_kernel(lengths, feeds, gain_ref, qkv_held, proj_held, *rest):
    saved, lefts, (left_rows, sems) = rest[: 3 * MB], rest[3 * MB : 3 * MB + 2], rest[3 * MB + 2 :]
    place = Place(lengths)

    @pl.when(place.is_lower)
    def _():
        sender = Sender(sems)
        for item in range(MB):
            rows_ref = feeds.at[pl.ds(item * ROWS, ROWS)]
            attend_body(
                sender,
                place,
                item,
                rows_ref,
                gain_ref,
                (qkv_held, proj_held),
                *saved[3 * item : 3 * item + 3],
                lefts,
                left_rows.at[item],
            )
        sender.finish()


def lower_attend(lengths, feeds, gains, qkv_held, proj_held):
    outs = [(*shape, "vmem") for _ in range(MB) for shape in saved_shapes()]
    outs += [((MB * ROWS, KEPT), BF16, LEFTS)] * 2
    ins = [(lengths, "smem")]
    ins += [(value, "vmem") for value in (feeds, gains, qkv_held, proj_held)]
    scratch = [pltpu.VMEM((MB, 2, ROWS, D), BF16), pltpu.SemaphoreType.DMA((4 * MB,))]
    return call(lower_attend_kernel, "lower_attend", ins, outs, scratch)


def lower_expand_kernel(n_alias, item, lengths, mixed, gain_ref, in_held, back_held, *rest):
    slope, keep_out, send_out, low, second_rows, active, high, sems = rest[n_alias:]
    place = Place(lengths)

    @pl.when(place.is_lower)
    def _():
        sender = Sender(sems)
        expand_body(
            sender,
            place,
            item,
            True,
            mixed,
            gain_ref,
            (in_held, back_held),
            slope,
            (keep_out, send_out),
            second_rows,
            active,
            high,
        )
        low[...] = high[...].astype(BF16)
        sender.finish()


def lower_expand(item, lengths, mixed, gains, in_held, back_held, earlier):
    outs = [
        ((ROWS, FF), BF16, "vmem"),
        ((MB * ROWS, KEPT), BF16, LEFTS),
        ((MB * ROWS, KEPT), BF16, LEFTS),
        ((ROWS, D), BF16, "vmem"),
    ]
    ins = [(lengths, "smem")]
    ins += [(value, "vmem") for value in (mixed, gains, in_held, back_held)]
    ins, aliases = with_earlier(ins, outs, earlier)
    scratch = [
        pltpu.VMEM((ROWS, D), BF16),
        pltpu.VMEM((ROWS, FF), BF16),
        pltpu.VMEM((ROWS, D), F32),
        pltpu.SemaphoreType.DMA((4,)),
    ]
    kernel = functools.partial(lower_expand_kernel, len(aliases), item)
    return call(kernel, "lower_expand", ins, outs, scratch, aliases)


def top_attend_kernel(n_alias, item, lengths, rows_ref, gain_ref, qkv_held, proj_held, *rest):
    qkv_rows, probs, mixed, keep_out, send_out, left_rows, sems = rest[n_alias:]
    place = Place(lengths)

    @pl.when(jnp.logical_not(place.is_lower))
    def _():
        sender = Sender(sems)
        attend_body(
            sender,
            place,
            item,
            rows_ref,
            gain_ref,
            (qkv_held, proj_held),
            qkv_rows,
            probs,
            mixed,
            (keep_out, send_out),
            left_rows,
        )
        sender.finish()


def top_attend(item, lengths, rows, gains, qkv_held, proj_held, earlier):
    outs = [(*shape, "vmem") for shape in saved_shapes()]
    outs += [((MB * ROWS, KEPT), BF16, LEFTS)] * 2
    ins = [(lengths, "smem")]
    ins += [(value, "vmem") for value in (rows, gains, qkv_held, proj_held)]
    ins, aliases = with_earlier(ins, outs, earlier)
    scratch = [pltpu.VMEM((2, ROWS, D), BF16), pltpu.SemaphoreType.DMA((4,))]
    kernel = functools.partial(top_attend_kernel, len(aliases), item)
    return call(kernel, "top_attend", ins, outs, scratch, aliases)


def top_expand_kernel(n_alias, item, lengths, mixed, gain_ref, in_held, back_held, *rest):
    slope, keep_out, send_out, high, second_rows, active, sems = rest[n_alias:]
    place = Place(lengths)

    @pl.when(jnp.logical_not(place.is_lower))
    def _():
        sender = Sender(sems)
        expand_body(
            sender,
            place,
            item,
            False,
            mixed,
            gain_ref,
            (in_held, back_held),
            slope,
            (keep_out, send_out),
            second_rows,
            active,
            high,
        )
        sender.finish()


def top_expand(item, lengths, mixed, gains, in_held, back_held, earlier):
    outs = [
        ((ROWS, FF), BF16, "vmem"),
        ((MB * ROWS, KEPT), BF16, LEFTS),
        ((MB * ROWS, KEPT), BF16, LEFTS),
        ((ROWS, D), F32, "vmem"),
    ]
    ins = [(lengths, "smem")]
    ins += [(value, "vmem") for value in (mixed, gains, in_held, back_held)]
    ins, aliases = with_earlier(ins, outs, earlier)
    scratch = [
        pltpu.VMEM((ROWS, D), BF16),
        pltpu.VMEM((ROWS, FF), BF16),
        pltpu.SemaphoreType.DMA((4,)),
    ]
    kernel = functools.partial(top_expand_kernel, len(aliases), item)
    return call(kernel, "top_expand", ins, outs, scratch, aliases)


def top_expand_back_kernel(item, lengths, feeds, mixed, slope, gain_ref, in_held, back_held, *rest):
    target, gain_out, middle, inner, sems = rest
    place = Place(lengths)

    @pl.when(jnp.logical_not(place.is_lower))
    def _():
        sender = Sender(sems)
        expand_back_body(
            sender,
            place,
            item,
            False,
            feeds.at[pl.ds(item * ROWS, ROWS)],
            mixed,
            slope,
            gain_ref,
            (in_held, back_held),
            target,
            gain_out,
            middle,
            inner,
        )
        sender.finish()


def top_expand_back(item, lengths, feeds, mixed, slope, gains, in_held, back_held):
    outs = [grads_shapes(item)[0], ((1, D), F32, "vmem"), ((ROWS, D), F32, "vmem")]
    ins = [(lengths, "smem")]
    ins += [(value, "vmem") for value in (feeds, mixed, slope, gains, in_held, back_held)]
    scratch = [pltpu.VMEM((ROWS, FF), BF16), pltpu.SemaphoreType.DMA((1,))]
    kernel = functools.partial(top_expand_back_kernel, item)
    return call(kernel, "top_expand_back", ins, outs, scratch)


def top_attend_back_kernel(lengths, rows_ref, middle, qkv_rows, probs, gain_ref, *rest):
    weights, rest = rest[:2], rest[2:]
    *targets, gain_out, low, outer, sems = rest
    targets[-1] = targets[-1].at[pl.ds(0, ROWS)]
    place = Place(lengths)

    @pl.when(jnp.logical_not(place.is_lower))
    def _():
        sender = Sender(sems)
        low[...] = attend_back_body(
            sender, rows_ref, middle, qkv_rows, probs, gain_ref, weights, targets, gain_out, outer
        ).astype(BF16)
        sender.finish()


def top_attend_back(item, lengths, rows, middle, saved, gains, weights):
    outs = [*grads_shapes(item)[1:], ((1, D), F32, "vmem"), ((ROWS, D), BF16, "vmem")]
    ins = [(lengths, "smem")]
    ins += [(value, "vmem") for value in (rows, middle, *saved, gains, *weights)]
    scratch = [pltpu.VMEM((ROWS, 4 * D), BF16), pltpu.SemaphoreType.DMA((2,))]
    return call(top_attend_back_kernel, "top_attend_back", ins, outs, scratch)


def lower_expand_back_kernel(
    n_alias, item, lengths, grad_ref, mixed, slope, gain_ref, in_held, back_held, *rest
):
    target, gain_out, middle, inner, sems = rest[n_alias:]
    place = Place(lengths)

    @pl.when(place.is_lower)
    def _():
        sender = Sender(sems)
        expand_back_body(
            sender,
            place,
            item,
            True,
            grad_ref,
            mixed,
            slope,
            gain_ref,
            (in_held, back_held),
            target,
            gain_out,
            middle,
            inner,
        )
        sender.finish()


def lower_expand_back(item, lengths, grad, mixed, slope, gains, in_held, back_held, earlier):
    outs = [grads_shapes(item)[0], ((1, D), F32, "vmem"), ((ROWS, D), F32, "vmem")]
    ins = [(lengths, "smem")]
    ins += [(value, "vmem") for value in (grad, mixed, slope, gains, in_held, back_held)]
    ins, aliases = with_earlier(ins, outs, earlier)
    scratch = [pltpu.VMEM((ROWS, FF), BF16), pltpu.SemaphoreType.DMA((1,))]
    kernel = functools.partial(lower_expand_back_kernel, len(aliases), item)
    size = 1 << 16 if item < MB - 1 else 1
    return call(kernel, "lower_expand_back", ins, outs, scratch, aliases, size)


def lower_attend_back_kernel(n_alias, item, lengths, feeds, middle, qkv_rows, probs, gain_ref, *rest):
    weights, rest = rest[:2], rest[2:]
    tops, others, rest = rest[:MB], rest[MB : MB + 3], rest[MB + 3 + n_alias :]
    if item < MB - 1:
        grads, gain_out, ends_out, outer, high, sems = rest
        targets = [grads]
    else:
        first, last, gain_out, ends_out, gain_keep, outer, high, gain_rows, sems = rest
        targets = [first, last.at[pl.ds(0, ROWS)]]
    place = Place(lengths)
    rows = pl.ds(item * ROWS, ROWS)

    @pl.when(place.is_lower)
    def _():
        sender = Sender(sems)
        high[...] = attend_back_body(
            sender,
            feeds.at[rows],
            middle,
            qkv_rows,
            probs,
            gain_ref,
            weights,
            targets,
            gain_out,
            outer,
        )
        sender.send(high, ends_out.at[rows])
        sender.finish()

    if item == MB - 1:
        sender = Sender(sems)

        @pl.when(jnp.logical_not(place.is_lower))
        def _():
            top_sender = Sender(sems)
            for top_item, top_high in enumerate(tops):
                top_sender.send(top_high, ends_out.at[pl.ds(top_item * ROWS, ROWS)])
            top_sender.finish()

        own, other = places(place.pos, HALF)
        gain_rows[...] = jnp.zeros_like(gain_rows)
        for row, parts in enumerate(((others[0], gain_out), others[1:])):
            gain_keep[row : row + 1] = parts[0][:, own] + parts[1][:, own]
            gain_rows[row : row + 1, pl.ds(0, HALF)] = parts[0][:, other] + parts[1][:, other]
        outer[pl.ds(0, 16), pl.ds(0, 2 * D)] = gain_rows[...].astype(BF16)
        sender.send(outer.at[pl.ds(0, 16), pl.ds(0, 2 * D)], last.at[pl.ds(ROWS, 16)])
        sender.finish()


def lower_attend_back(item, lengths, feeds, middle, saved, gains, weights, tops, others, earlier):
    outs = [
        *grads_shapes(item)[1:],
        ((1, D), F32, "vmem"),
        ((MB * ROWS, D), F32, "any"),
    ]
    scratch = [pltpu.VMEM((ROWS, 4 * D), BF16), pltpu.VMEM((ROWS, D), F32)]
    if item == MB - 1:
        outs.append(((2, HALF), F32, "vmem"))
        scratch.append(pltpu.VMEM((16, 2 * D), F32))
    scratch.append(pltpu.SemaphoreType.DMA((3,)))
    ins = [(lengths, "smem")]
    ins += [(value, "vmem") for value in (feeds, middle, *saved, gains, *weights, *tops, *others)]
    ins, aliases = with_earlier(ins, outs, earlier)
    kernel = functools.partial(lower_attend_back_kernel, len(aliases), item)
    return call(kernel, "lower_attend_back", ins, outs, scratch, aliases)


def expert_rows(place, item, partner, expert, live_only=False):
    row = lax.broadcasted_iota(jnp.int32, (1, ROWS), 1)
    first, second = place.experts(item, partner)
    mine = jnp.where(row < IMAGE_ROWS, first, second) == expert
    if live_only:
        mine = mine & (row < place.live(item, partner))
    return mine


def bits_but(*taken):
    count = lax.axis_size("dp").bit_length() - 1
    return [bit for bit in reversed(range(count)) if bit not in taken]


def block_numbers(first_bit):
    here = (lax.axis_index("dp") >> first_bit) & 1
    rest = bits_but(first_bit)
    for number in range(1 << len(rest)):
        where = tuple((number >> (len(rest) - 1 - place)) & 1 for place in range(len(rest)))
        base = sum(value << bit for value, bit in zip(where, rest))
        yield where, base + (here << first_bit), base + ((1 - here) << first_bit)


def write_blocks(total, rows, first_bit, mine, theirs):
    for where, own, other in block_numbers(first_bit):
        own_at = pl.ds(pl.multiple_of(own * rows, rows), rows)
        other_at = pl.ds(pl.multiple_of(other * rows, rows), rows)
        mine[where] = total[own_at].astype(BF16)
        theirs[where] = total[other_at].astype(BF16)


def back_grads_kernel(orders, n_items, lengths, *refs):
    actives, grads, feeds = refs[:n_items], refs[n_items : 2 * n_items], refs[2 * n_items : 2 * n_items + 2]
    outs, (flipped, total) = refs[2 * n_items + 2 : -2], refs[-2:]
    place = Place(lengths)
    tail = ROWS - TAIL
    rows = D // lax.axis_size("dp")

    @pl.when(pl.program_id(0) == 0)
    def _():
        for index in range(n_items):
            item, partner = index % MB, index >= MB
            top = feeds[index // MB][pl.ds(item * ROWS, ROWS)]
            value = jnp.where(place.is_lower, grads[index][...], top).T
            for expert in (0, 1):
                mask = expert_rows(place, item, partner, expert, live_only=True)
                flipped[expert, :, pl.ds(index * ROWS, ROWS)] = jnp.where(mask, value, 0)

    def finished(expert):
        write_blocks(total, rows, orders[expert][0], outs[2 * expert], outs[2 * expert + 1])

    def whole(expert):
        result = None
        for index in range(n_items):
            term = dot_nn(flipped[expert, :, pl.ds(index * ROWS, ROWS)], actives[index][...])
            result = term if result is None else result + term
        total[...] = result

    whole(0)
    finished(0)

    @pl.when(place.is_lower)
    def _():
        left = [
            flipped[1, :, pl.ds(index * ROWS + ROWS // 2, ROWS // 2)] for index in range(n_items)
        ]
        right = [actives[index][pl.ds(ROWS // 2, ROWS // 2)] for index in range(n_items)]
        total[...] = dot_nn(jnp.concatenate(left, axis=1), jnp.concatenate(right, axis=0))

    @pl.when(jnp.logical_not(place.is_lower))
    def _():
        whole(1)

    finished(1)


def halves_shape(block):
    return jax.ShapeDtypeStruct((2,) * len(bits_but(0)) + block, BF16)


def halves_spec(block, place):
    lead = len(bits_but(0))
    return pl.BlockSpec((2,) * lead + block, lambda step: (0,) * lead + place(step))


def by_item(width, count, column, **options):
    return [
        pl.BlockSpec((ROWS, width), lambda step, item=index % MB: (item, column(step)), **options)
        for index in range(count)
    ]


def back_grads(lengths, kept, grads, feeds, orders):
    width = 256
    block = (D // lax.axis_size("dp"), width)
    once = pl.Buffered(1)
    fixed = [pl.BlockSpec((ROWS, D), lambda step: (0, 0), pipeline_mode=once)] * len(kept)
    fixed += [pl.BlockSpec((MB * ROWS, D), lambda step: (0, 0), pipeline_mode=once)] * 2
    results = pl.pallas_call(
        functools.partial(back_grads_kernel, orders, len(kept)),
        grid=(FF_HALF // width,),
        out_shape=[halves_shape((block[0], FF_HALF)) for _ in orders for _ in (0, 1)],
        in_specs=[pl.BlockSpec(memory_space=pltpu.SMEM)]
        + by_item(width, len(kept), lambda step: step)
        + fixed,
        out_specs=[
            halves_spec(block, lambda step: (0, step)) for _ in orders for _ in (0, 1)
        ],
        scratch_shapes=[
            pltpu.VMEM((2, D, len(kept) * ROWS), BF16),
            pltpu.VMEM((D, width), F32),
        ],
        compiler_params=pltpu.CompilerParams(vmem_limit_bytes=VMEM_BYTES),
        cost_estimate=cost(1),
        name="back_grads",
    )(lengths, *kept, *grads, *feeds)
    return [tuple(results[2 * expert : 2 * expert + 2]) for expert in (0, 1)]


def in_grads_kernel(width, n_items, lengths, *refs):
    seconds, inners = refs[:n_items], refs[n_items : 2 * n_items]
    outs, (flipped, total) = refs[2 * n_items : -2], refs[-2:]
    place = Place(lengths)
    half = ROWS // 2
    low_bit = lax.axis_index("dp") % 2

    @pl.when(pl.program_id(0) == 0)
    def _():
        for index in range(n_items):
            item, partner = index % MB, index >= MB
            value = seconds[index][...].T
            for expert in (0, 1):
                mask = expert_rows(place, item, partner, expert)
                flipped[expert, :, pl.ds(index * ROWS, ROWS)] = jnp.where(mask, value, 0)

    def whole(expert):
        result = None
        for index in range(n_items):
            term = dot_nn(flipped[expert, :, pl.ds(index * ROWS, ROWS)], inners[index][...])
            result = term if result is None else result + term
        total[...] = result

    def finished(expert):
        if len(outs) == 2:
            outs[expert][0] = total[...].astype(BF16)
            return
        for out, bit in zip(outs[2 * expert : 2 * expert + 2], (low_bit, 1 - low_bit)):
            out[0] = total[:, pl.ds(pl.multiple_of(bit * width, width), width)].astype(BF16)

    whole(0)
    finished(0)

    @pl.when(place.is_lower)
    def _():
        left = [flipped[1, :, pl.ds(index * ROWS + half, half)] for index in range(n_items)]
        right = [inners[index][pl.ds(half, half)] for index in range(n_items)]
        total[...] = dot_nn(jnp.concatenate(left, axis=1), jnp.concatenate(right, axis=0))

    @pl.when(jnp.logical_not(place.is_lower))
    def _():
        whole(1)

    finished(1)


def in_grads(lengths, kept, inners):
    size = lax.axis_size("dp")
    width = FF // size
    aligned = width % 128 == 0
    columns = 2 * width if aligned else D
    steps = FF // columns
    once = pl.Buffered(1)
    block = (1, HALF, width if aligned else columns)
    count = 4 if aligned else 2
    results = pl.pallas_call(
        functools.partial(in_grads_kernel, width, len(kept)),
        grid=(steps,),
        out_shape=[jax.ShapeDtypeStruct((steps,) + block[1:], BF16)] * count,
        in_specs=[pl.BlockSpec(memory_space=pltpu.SMEM)]
        + by_item(HALF, len(kept), lambda step: FF_HALF // HALF, pipeline_mode=once)
        + [pl.BlockSpec((ROWS, columns), lambda step: (0, step))] * len(inners),
        out_specs=[pl.BlockSpec(block, lambda step: (step, 0, 0))] * count,
        scratch_shapes=[
            pltpu.VMEM((2, HALF, len(kept) * ROWS), BF16),
            pltpu.VMEM((HALF, columns), F32),
        ],
        compiler_params=pltpu.CompilerParams(vmem_limit_bytes=VMEM_BYTES),
        cost_estimate=cost(1),
        name="in_grads",
    )(lengths, *kept, *inners)
    if not aligned:
        whole = [part.transpose(1, 0, 2).reshape(HALF, size, width) for part in results]
        return [by_lowest_bit(part.transpose(1, 0, 2)) for part in whole]
    shape = (2,) * len(bits_but(0)) + block[1:]
    return [tuple(part.reshape(shape) for part in results[2 * e : 2 * e + 2]) for e in (0, 1)]


def outer_grads_kernel(order, *refs):
    lefts, outers, gains, pieces, total = refs[:4], refs[4:10], refs[10:12], refs[12:16], refs[16]
    step = pl.program_id(0)
    result = None
    for index in range(4):
        outer = outers[3 * (index // MB)][...]
        if index % MB == MB - 1:
            first, second = outers[3 * (index // MB) + 1 : 3 * (index // MB) + 3]
            outer = jnp.where(step < 2, first[...], second[...])
        term = dot_tn(outer, lefts[index][...])
        result = term if result is None else result + term
    total[pl.ds(pl.multiple_of(step * D, D), D)] = result

    @pl.when(step == 3)
    def _():
        size = lax.axis_size("dp")
        proj_rows = D // size
        gain_rows = gains[0][...] + gains[1][pl.ds(0, 2), pl.ds(0, HALF)].astype(F32)
        gain_rows = jnp.concatenate([gain_rows, jnp.zeros((14, HALF), F32)], axis=0)
        for where, *numbers in block_numbers(order[0]):
            for target, number in zip((0, 1), numbers):
                at = pl.multiple_of(number * 3 * proj_rows, proj_rows)
                below = pl.multiple_of(3 * D + number * proj_rows, proj_rows)
                first, second = pieces[target], pieces[2 + target]
                first[where] = total[pl.ds(at, 2 * proj_rows)].astype(BF16)
                second[where + (pl.ds(0, proj_rows),)] = total[
                    pl.ds(at + 2 * proj_rows, proj_rows)
                ].astype(BF16)
                second[where + (pl.ds(proj_rows, proj_rows),)] = total[
                    pl.ds(below, proj_rows)
                ].astype(BF16)
                turned = pltpu.roll(gain_rows, HALF - number * (HALF // size), 1)
                second[where + (pl.ds(2 * proj_rows, 16),)] = turned.astype(BF16)


def outer_grads(kept, outers, gains, order):
    block = (2 * D // lax.axis_size("dp"), HALF)
    last = (block[0] + 16, HALF)
    results = pl.pallas_call(
        functools.partial(outer_grads_kernel, order),
        grid=(4,),
        out_shape=[halves_shape(block)] * 2 + [halves_shape(last)] * 2,
        in_specs=by_item(HALF, 4, lambda step: FF_HALF // HALF + 1 + step // 3)
        + [
            pl.BlockSpec((ROWS, D), lambda step: (0, step)),
            pl.BlockSpec((ROWS, D), lambda step: (0, jnp.minimum(step, 1))),
            pl.BlockSpec((ROWS, D), lambda step: (0, jnp.maximum(step - 2, 0))),
        ]
        * 2
        + [
            pl.BlockSpec((2, HALF), lambda step: (0, 0)),
            pl.BlockSpec((16, D), lambda step: (ROWS // 16, 0)),
        ],
        out_specs=[halves_spec(block, lambda step: (0, 0))] * 2
        + [halves_spec(last, lambda step: (0, 0))] * 2,
        scratch_shapes=[pltpu.VMEM((4 * D, HALF), F32)],
        compiler_params=pltpu.CompilerParams(vmem_limit_bytes=2 * VMEM_BYTES),
        cost_estimate=cost(1),
        name="outer_grads",
    )(*kept, *outers, *gains)
    return tuple(results[:2]), tuple(results[2:])


def swapped(block, axis, bit, among=None):
    among = range(lax.axis_size(axis)) if among is None else among
    return lax.ppermute(block, axis, [(place, place ^ 1 << bit) for place in among])


def per_item(arrays):
    return [array for array in arrays for _ in range(MB)]


def passed_along(value, steps):
    count = lax.axis_size("section")
    first, last = (max(0, -steps), min(count, count - steps))
    route = [(source, source + steps) for source in range(first, last)]
    return lax.ppermute(value, "section", route)


def split_bit(stacked, bit):
    here = (lax.axis_index("dp") >> bit) & 1
    mine = lax.dynamic_index_in_dim(stacked, here, 0, keepdims=False)
    theirs = lax.dynamic_index_in_dim(stacked, 1 - here, 0, keepdims=False)
    return mine, theirs


def added_kernel(left, right, out):
    out[...] = left[...].astype(F32) + right[...].astype(F32)


def added(left, right):
    ins = [(left, "vmem"), (right, "vmem")]
    return call(added_kernel, "added", ins, [(left.shape, F32, "vmem")], [])[0]


def outer_sums_kernel(first, left, right, qkv_out, proj_out, gain_out):
    rows = proj_out.shape[0]
    second = left[...].astype(F32) + right[...].astype(F32)
    qkv_out[: 2 * rows] = first[...]
    qkv_out[2 * rows :] = second[:rows]
    proj_out[...] = second[rows : 2 * rows]
    gain_out[...] = second[2 * rows : 2 * rows + 2]


def outer_sums(first, left, right):
    rows = first.shape[0] // 2
    ins = [(value, "vmem") for value in (first, left, right)]
    shapes = [(3 * rows, HALF), (rows, HALF), (2, HALF)]
    outs = [(shape, F32, "auto") for shape in shapes]
    return call(outer_sums_kernel, "outer_sums", ins, outs, [])


def added_halves_kernel(axis, bit, left, right, mine, theirs):
    here = (lax.axis_index("dp") >> bit) & 1
    lead = (slice(None),) * axis
    for out, at in ((mine, lead + (here,)), (theirs, lead + (1 - here,))):
        out[...] = (left[at].astype(F32) + right[at].astype(F32)).astype(BF16)


def added_halves(left, right, axis, bit):
    ins = [(left, "vmem"), (right, "vmem")]
    outs = [(left.shape[:axis] + left.shape[axis + 1 :], BF16, "vmem")] * 2
    kernel = functools.partial(added_halves_kernel, axis, bit)
    return call(kernel, "added_halves", ins, outs, [])


def after(value, *earlier):
    return lax.optimization_barrier((value, earlier))[0]


class Sums:
    def __init__(self):
        self.open = {}
        self.results = {}
        self.last = []

    def begin(self, name, piece, order, taken=()):
        mine, theirs = piece
        self.open[name] = (mine, swapped(theirs, "dp", order[0]), order[1:], (*taken, order[0]))

    def step(self, name, hold=False):
        mine, got, rest, taken = self.open.pop(name)
        mine = after(mine, *self.last)
        if len(rest) == 0:
            self.results[name] = added(mine, got)
            self.last = [self.results[name]]
            return
        mine, theirs = added_halves(mine, got, bits_but(*taken).index(rest[0]), rest[0])
        self.last = [theirs]
        if hold:
            return (mine, theirs), rest, taken
        self.begin(name, (mine, theirs), rest, taken)

    def finish(self, but):
        while len(self.open) > 1 or len(self.open[but][2]) > 0:
            for name in list(self.open):
                if name != but or len(self.open[name][2]) > 0:
                    self.step(name)
        mine, got, *_ = self.open.pop(but)
        return after(mine, *self.last), got


def by_lowest_bit(stacked):
    bits = lax.axis_size("dp").bit_length() - 1
    split = jnp.moveaxis(stacked.reshape((2,) * bits + stacked.shape[1:]), bits - 1, 0)
    return split_bit(split, 0)


def shards(feeds, text_lengths, norm_gains, qkv_weight, out_weight, expert_in, expert_out):
    n_dp = lax.axis_size("dp")
    bits = n_dp.bit_length() - 1
    pos = lax.axis_index("section") % 2

    gains_other = swapped(norm_gains[0], "section", 0)
    gains = joined_gains(norm_gains[0], gains_other)
    own = [qkv_weight[0], out_weight[0]]
    other = [swapped(part, "section", 0) for part in own]
    held = joined_halves(own, other)
    in_other = swapped(after(expert_in[0], gains_other, *other), "section", 0)
    back_other = swapped(after(expert_out[0], gains_other, *other), "section", 0)

    *saved, keep, send = lower_attend(text_lengths, feeds, gains, *held)
    saved = [saved[3 * item : 3 * item + 3] for item in range(MB)]
    earlier = saved[-1][2]
    held += joined_halves([expert_in[0]], [after(in_other, earlier)])
    held += joined_halves([expert_out[0]], [after(back_other, earlier)])
    slopes, passed = [], []
    for item in range(MB):
        mixed = after(saved[item][2], earlier)
        slope, keep, send, earlier = lower_expand(
            item, text_lengths, mixed, gains, *held[2:], {1: keep, 2: send}
        )
        slopes.append(slope)
        passed.append(passed_along(earlier, 2))
    grads, gain_grads, ups = [], [], []
    tops = []
    for item in range(MB):
        rows = after(passed[item], earlier)
        places = dict(enumerate(saved[item])) | {3: keep, 4: send}
        *saved[item], keep, send = top_attend(
            item, text_lengths, rows, gains, *held[:2], places
        )
        mixed = saved[item][2]
        places = {0: slopes[item], 1: keep, 2: send}
        slopes[item], keep, send, top = top_expand(
            item, text_lengths, mixed, gains, *held[2:], places
        )
        tops.append(top)
        inner, gain_second, middle = top_expand_back(
            item, text_lengths, feeds, mixed, slopes[item], gains, *held[2:]
        )
        *outer, gain_first, earlier = top_attend_back(
            item,
            text_lengths,
            rows,
            middle,
            saved[item][:2],
            gains,
            held[:2],
        )
        grads.append([inner, *outer])
        gain_grads.append([gain_first, gain_second])
        ups.append(passed_along(earlier, -2))
    feeds_pair = [feeds, swapped(after(feeds, earlier), "section", 0, (2, 3))]
    lefts = per_item([keep, swapped(after(send, earlier), "section", 0)])

    upward = tuple(range(bits))
    back_orders = [upward[1:] + upward[:1], upward]

    def lower_back_experts(item, up):
        results = {0: grads[item][0], 1: gain_grads[item][1]}
        grads[item][0], gain_grads[item][1], middle = lower_expand_back(
            item, text_lengths, up, saved[item][2], slopes[item], gains, *held[2:], results
        )
        return middle

    def lower_back_heads(item, middle, ends, others):
        parts = [*grads[item][1:], gain_grads[item][0], *ends]
        results = lower_attend_back(
            item,
            text_lengths,
            feeds,
            middle,
            saved[item][:2],
            gains,
            held[:2],
            tops,
            others,
            dict(enumerate(parts)),
        )
        count = len(grads[item]) - 1
        grads[item][1:], gain_grads[item][0] = results[:count], results[count]
        return results[count + 1 :]

    ups[0] = after(ups[0], earlier)
    ups_other = [swapped(ups[0], "section", 0, (0, 1))]
    middle = lower_back_experts(0, ups[0])
    (ends,) = lower_back_heads(0, middle, [], [gain_grads[0][1]] * 3)
    first_grads = [(part, swapped(part, "section", 0)) for part in grads[0]]
    ups[1] = after(ups[1], ends)
    ups_other.append(swapped(ups[1], "section", 0, (0, 1)))
    middle = lower_back_experts(1, after(ups[1], ups_other[0]))
    inner = grads[1][0]
    inners = [first_grads[0][0], inner, first_grads[0][1], swapped(inner, "section", 0)]
    ups_other[1] = after(ups_other[1], middle)
    back_pieces = back_grads(text_lengths, lefts, ups + ups_other, feeds_pair, back_orders)
    inners[1] = after(inners[1], back_pieces[0][1], back_pieces[1][1])
    in_pieces = in_grads(text_lengths, lefts, inners)

    sums = Sums()
    for number in (0, 1):
        sums.begin(f"back{number}", back_pieces[number], back_orders[number])
    sums.begin("in0", in_pieces[0], upward)
    middle = after(middle, in_pieces[0][1], in_pieces[1][1])
    others = [gain_grads[0][0], gain_grads[0][1], gain_grads[1][1]]
    ends, gain_keep = lower_back_heads(1, middle, [ends], others)
    outers = [first_grads[1][0], *grads[1][1:], first_grads[1][1]]
    outers += [swapped(part, "section", 0) for part in grads[1][1:]]
    sums.last = [ends]
    sums.step("back0")
    gain_keep = after(gain_keep, *sums.last)
    outer_pieces = outer_grads(lefts, outers, (gain_keep, outers[-1]), upward)
    sums.last = [piece[1] for piece in outer_pieces]
    sums.step("back1")

    def later(piece):
        return piece[0], after(piece[1], *sums.last)

    sums.begin("in1", later(in_pieces[1]), upward)
    sums.begin("outer0", later(outer_pieces[0]), upward)
    for name in ("back0", "in0", "back1", "in0", "in1", "back1"):
        sums.step(name)
    sums.begin("outer1", later(outer_pieces[1]), upward)
    order = ("outer0", "in1", "in0", "outer1", "outer0", "in1", "outer1", "outer0", "back0")
    for name in order:
        sums.step(name)
    last = sums.finish("outer1")
    qkv_sum, proj_sum, gain_sum = outer_sums(sums.results["outer0"], *last)
    done = sums.results
    return (
        ends,
        gain_sum[None, :, : HALF // n_dp],
        qkv_sum.T[None],
        proj_sum.T[None],
        jnp.stack([done["in0"], done["in1"]])[None],
        jnp.stack([done["back0"].T, done["back1"].T])[None],
    )


def solution(mesh):
    return jax.shard_map(
        shards,
        mesh=mesh,
        in_specs=(
            P(("dp", "section"), None),
            P("dp"),
            P("section", None, None),
            P("section", None, None),
            P("section", None, None),
            P("section", None, None, None),
            P("section", None, None, None),
        ),
        out_specs=(
            P(("dp", "section"), None),
            P("section", None, "dp"),
            P("section", None, "dp"),
            P("section", None, "dp"),
            P("section", None, None, "dp"),
            P("section", None, None, "dp"),
        ),
        check_vma=False,
    )
```

```python
import functools

import jax
import jax.numpy as jnp
from jax import lax
from jax.experimental import pallas as pl
from jax.experimental.pallas import tpu as pltpu
from jax.sharding import PartitionSpec as P

D = 768
HALF = D // 2
HEADS = 12
FF = 3072
FF_HALF = FF // 2
HEAD_DIM = 64
IMAGE_ROWS = 197
ROWS = 256
MB = 2
KEPT = FF_HALF + 3 * HALF
TAIL = 192

EPSILON = 1e-05
MASKED = -1e30
F32 = jnp.float32
BF16 = jnp.bfloat16
VMEM_BYTES = 10 * 1024 * 1024
LEFTS = "any"


def cost(size):
    return pl.CostEstimate(flops=size << 20, bytes_accessed=1 << 10, transcendentals=0)


def dot_nn(left, right):
    return lax.dot_general(left, right, (((1,), (0,)), ((), ())), preferred_element_type=F32)


def dot_nt(left, right):
    return lax.dot_general(left, right, (((1,), (1,)), ((), ())), preferred_element_type=F32)


def dot_tn(left, right):
    return lax.dot_general(left, right, (((0,), (0,)), ((), ())), preferred_element_type=F32)


def norm_parts(hidden):
    centred = hidden - jnp.mean(hidden, axis=-1, keepdims=True)
    spread = jnp.mean(centred * centred, axis=-1, keepdims=True)
    inverse = lax.rsqrt(spread + EPSILON)
    return centred * inverse, inverse


def norm_back(grad, hidden, gain_row):
    unit, inverse = norm_parts(hidden)
    gain_grad = jnp.sum(grad * unit, axis=0, keepdims=True)
    scaled = grad * gain_row
    mean_plain = jnp.mean(scaled, axis=-1, keepdims=True)
    mean_unit = jnp.mean(scaled * unit, axis=-1, keepdims=True)
    return inverse * (scaled - mean_plain - unit * mean_unit), gain_grad


def gelu_pair(values):
    size = jnp.abs(values)
    denom = 1.0 + (0.3275911 * 0.7071067811865476) * size
    t = pl.reciprocal(denom, approx=True)
    poly = 0.5 * 1.061405429
    for factor in (-1.453152027, 1.421413741, -0.284496736, 0.254829592):
        poly = poly * t + 0.5 * factor
    bell = jnp.exp2(values * values * (-0.5 * 1.4426950408889634))
    upper_tail = poly * t * bell
    cdf = jnp.where(values < 0, upper_tail, 1.0 - upper_tail)
    return values * cdf, cdf + values * bell * 0.3989422804014327


def lane_half(value, which):
    lanes = lax.broadcasted_iota(jnp.int32, value.shape, 1)
    picked = lanes < HEAD_DIM if which == 0 else lanes >= HEAD_DIM
    return jnp.where(picked, value, jnp.zeros_like(value))


def call(kernel, name, ins, outs, scratch, aliases=None, size=1, memory=VMEM_BYTES):
    spaces = {"vmem": pltpu.VMEM, "auto": pltpu.VMEM, "smem": pltpu.SMEM, "any": pl.ANY, "hbm": pltpu.HBM}
    kinds = {"vmem": pltpu.VMEM, "auto": jax.ShapeDtypeStruct, "any": jax.ShapeDtypeStruct, "hbm": pltpu.HBM}
    shapes = [kinds[space](shape, kind) for shape, kind, space in outs]
    return pl.pallas_call(
        kernel,
        out_shape=shapes,
        in_specs=[pl.BlockSpec(memory_space=spaces[space]) for _, space in ins],
        out_specs=[pl.BlockSpec(memory_space=spaces[space]) for _, _, space in outs],
        input_output_aliases=aliases or {},
        scratch_shapes=scratch,
        compiler_params=pltpu.CompilerParams(vmem_limit_bytes=memory),
        cost_estimate=cost(size),
        name=name,
    )(
        *[
            pltpu.with_memory_space_constraint(value, pltpu.HBM) if space == "hbm" else value
            for value, space in ins
        ]
    )


class Place:
    def __init__(self, lengths):
        section = lax.axis_index("section")
        self.lengths = lengths
        self.is_lower = section < 2
        self.pos = section % 2

    def length(self, item, partner=False):
        pos = 1 - self.pos if partner else self.pos
        return self.lengths[pos * MB + item]

    def live(self, item, partner=False):
        return IMAGE_ROWS + self.length(item, partner)

    def experts(self, item, partner=False):
        kind = jnp.where(self.length(item, partner) > 0, 1, 0)
        return jnp.where(self.is_lower, 0, kind), jnp.where(self.is_lower, 1, kind)


def with_earlier(ins, outs, earlier):
    aliases = {}
    for number, value in (earlier or {}).items():
        aliases[len(ins)] = number
        ins = ins + [(value, outs[number][2])]
    return ins, aliases


class Sender:
    def __init__(self, sems):
        self.sems = sems
        self.sent = []
        self.done = 0

    def send(self, source, target):
        copy = pltpu.make_async_copy(source, target, self.sems.at[len(self.sent)])
        copy.start()
        self.sent.append(copy)

    def finish(self, count=None):
        count = len(self.sent) - self.done if count is None else count
        for copy in self.sent[self.done : self.done + count]:
            copy.wait()
        self.done += count


def join_kernel(count, *refs):
    own, other, joined, sems = refs[:count], refs[count : 2 * count], refs[2 * count : -1], refs[-1]
    pos = lax.axis_index("section") % 2
    sender = Sender(sems)
    for mine, theirs, whole in zip(own, other, joined):
        depth = mine.shape[-2]
        for source, at in ((mine, pos), (theirs, 1 - pos)):
            rows = pl.ds(pl.multiple_of(at * depth, depth), depth)
            if len(whole.shape) == 2:
                sender.send(source, whole.at[rows])
            else:
                for expert in range(whole.shape[0]):
                    sender.send(source.at[expert], whole.at[expert, rows])
    sender.finish()


def joined_halves(own, other):
    outs = []
    for part in own:
        shape = part.shape[:-2] + (2 * part.shape[-2], part.shape[-1])
        outs.append((shape, BF16, "vmem"))
    return call(
        functools.partial(join_kernel, len(own)),
        "joined_halves",
        [(value, "hbm") for value in own] + [(value, "any") for value in other],
        outs,
        [pltpu.SemaphoreType.DMA((4 * len(own),))],
    )


def gains_kernel(own, other, gains):
    first = lax.axis_index("section") % 2 == 0
    mine, theirs = own[...].astype(F32), other[...].astype(F32)
    gains[:, pl.ds(0, HALF)] = jnp.where(first, mine, theirs)
    gains[:, pl.ds(HALF, HALF)] = jnp.where(first, theirs, mine)


def joined_gains(own, other):
    return call(
        gains_kernel, "joined_gains", [(own, "vmem"), (other, "vmem")], [((2, D), F32, "vmem")], []
    )[0]


def places(pos, size):
    return (
        pl.ds(pl.multiple_of(pos * size, size), size),
        pl.ds(pl.multiple_of((1 - pos) * size, size), size),
    )


def attend_body(
    sender, place, item, rows_ref, gain_ref, weights, qkv_rows, probs, mixed, lefts, left_rows
):
    qkv_held, proj_held = weights
    own, other = places(place.pos, HALF)

    def send_halves(part):
        to = (pl.ds(item * ROWS, ROWS), pl.ds(FF_HALF + (1 + part) * HALF, HALF))
        for columns, target in zip((own, other), lefts):
            sender.send(left_rows.at[part, :, columns], target.at[to])

    normed = (norm_parts(rows_ref[...].astype(F32))[0] * gain_ref[0:1]).astype(BF16)
    left_rows[0] = normed
    send_halves(0)
    for part in range(3):
        columns = pl.ds(part * D, D)
        qkv_rows[:, columns] = dot_nn(normed, qkv_held[:, columns]).astype(BF16)
    keys_live = lax.broadcasted_iota(jnp.int32, (ROWS, ROWS), 1) < place.live(item)
    for pair in range(HEADS // 2):
        queries = qkv_rows[:, pl.ds(pair * 128, 128)] * jnp.asarray(HEAD_DIM**-0.5, BF16)
        keys = qkv_rows[:, pl.ds(D + pair * 128, 128)]
        values = qkv_rows[:, pl.ds(2 * D + pair * 128, 128)]
        context = None
        for which in (0, 1):
            scores = dot_nt(lane_half(queries, which), keys)
            scores = jnp.where(keys_live, scores, MASKED)
            shifted = jnp.exp(scores - jnp.max(scores, axis=-1, keepdims=True))
            total = jnp.sum(shifted, axis=-1, keepdims=True)
            weight = (shifted * pl.reciprocal(total, approx=True)).astype(BF16)
            probs[2 * pair + which] = weight
            term = dot_nn(weight, lane_half(values, which))
            context = term if context is None else context + term
        left_rows[1, :, pl.ds(pair * 128, 128)] = context.astype(BF16)
    send_halves(1)
    mixed[...] = rows_ref[...].astype(F32) + dot_nn(left_rows[1], proj_held[...])


def expand_body(
    sender, place, item, lower, mixed, gain_ref, weights, slope, lefts, second_rows, active, high
):
    in_held, back_held = weights
    first, second = place.experts(item)
    halves, deep_halves = places(place.pos, HALF), places(place.pos, FF_HALF)
    rows = pl.ds(item * ROWS, ROWS)

    def send_active():
        for columns, target in zip(deep_halves, lefts):
            sender.send(active.at[:, columns], target.at[rows, pl.ds(0, FF_HALF)])

    normed = (norm_parts(mixed[...])[0] * gain_ref[1:2]).astype(BF16)
    second_rows[...] = normed
    for columns, target in zip(halves, lefts):
        sender.send(second_rows.at[:, columns], target.at[rows, pl.ds(FF_HALF, HALF)])
    total = mixed[...]
    for part in range(4):
        columns = pl.ds(part * D, D)
        value, derivative = gelu_pair(dot_nn(normed, in_held[first, :, columns]))
        value = value.astype(BF16)
        active[:, columns] = value
        slope[:, columns] = derivative.astype(BF16)
        total = total + dot_nn(value, back_held[first, columns])
    if not lower:
        send_active()
    high[...] = total
    if not lower:
        return
    tail = pl.ds(TAIL, ROWS - TAIL)
    later = lax.broadcasted_iota(jnp.int32, (ROWS - TAIL, D), 0) >= IMAGE_ROWS - TAIL
    total = mixed[tail]
    for part in range(4):
        columns = pl.ds(part * D, D)
        value, derivative = gelu_pair(dot_nn(second_rows[tail], in_held[second, :, columns]))
        kept = active[tail, columns].astype(F32)
        value = jnp.where(later, value, kept).astype(BF16)
        active[tail, columns] = value
        kept = slope[tail, columns].astype(F32)
        slope[tail, columns] = jnp.where(later, derivative, kept).astype(BF16)
        total = total + dot_nn(value, back_held[second, columns])
    send_active()
    high[tail] = jnp.where(later, total, high[tail])


def expand_back_body(
    sender, place, item, lower, grad_ref, mixed, slope, gain_ref, weights, target, gain_out, middle, inner
):
    in_held, back_held = weights
    first, second = place.experts(item)
    is_live = lax.broadcasted_iota(jnp.int32, (ROWS, D), 0) < place.live(item)
    grad = jnp.where(is_live, grad_ref[...].astype(F32), 0.0)
    grad_low = grad.astype(BF16)
    for part in range(4):
        columns = pl.ds(part * D, D)
        grad_active = dot_nt(grad_low, back_held[first, columns])
        inner[:, columns] = (grad_active * slope[:, columns].astype(F32)).astype(BF16)
    if not lower:
        sender.send(inner, target)
    middle[...] = dot_nt(inner[...], in_held[first])
    if lower:
        tail = pl.ds(TAIL, ROWS - TAIL)
        later = lax.broadcasted_iota(jnp.int32, (ROWS - TAIL, D), 0) >= IMAGE_ROWS - TAIL
        for part in range(4):
            columns = pl.ds(part * D, D)
            grad_active = dot_nt(grad_low[TAIL:], back_held[second, columns])
            patched = grad_active * slope[tail, columns].astype(F32)
            kept = inner[tail, columns].astype(F32)
            inner[tail, columns] = jnp.where(later, patched, kept).astype(BF16)
        sender.send(inner, target)
        patched = dot_nt(inner[tail], in_held[second])
        middle[tail] = jnp.where(later, patched, middle[tail])
    grad_mixed, gain_out[...] = norm_back(middle[...], mixed[...], gain_ref[1:2])
    middle[...] = grad + grad_mixed


def attend_back_body(
    sender, rows_ref, middle, qkv_rows, probs, gain_ref, weights, targets, gain_out, outer
):
    qkv_held, proj_held = weights
    branch = middle[...].astype(BF16)
    outer[:, pl.ds(3 * D, D)] = branch
    grad_context = dot_nt(branch, proj_held[...]).astype(BF16)
    scale = jnp.asarray(HEAD_DIM**-0.5, BF16)
    grad_normed = None
    for pair in range(HEADS // 2):
        queries = qkv_rows[:, pl.ds(pair * 128, 128)] * scale
        keys = qkv_rows[:, pl.ds(D + pair * 128, 128)] * scale
        values = qkv_rows[:, pl.ds(2 * D + pair * 128, 128)]
        context = grad_context[:, pair * 128 : (pair + 1) * 128]
        grad_q = grad_k = grad_v = None
        for which in (0, 1):
            weight = probs[2 * pair + which]
            context_half = lane_half(context, which)
            grad_probs = dot_nt(context_half, values)
            weight_wide = weight.astype(F32)
            product = weight_wide * grad_probs
            row_total = jnp.sum(product, axis=-1, keepdims=True)
            grad_scores = (product - weight_wide * row_total).astype(BF16)
            term_v = dot_tn(weight, context_half)
            term_q = dot_nn(grad_scores, lane_half(keys, which))
            term_k = dot_tn(grad_scores, lane_half(queries, which))
            grad_q = term_q if grad_q is None else grad_q + term_q
            grad_k = term_k if grad_k is None else grad_k + term_k
            grad_v = term_v if grad_v is None else grad_v + term_v
        outer[:, pl.ds(pair * 128, 128)] = grad_q.astype(BF16)
        outer[:, pl.ds(D + pair * 128, 128)] = grad_k.astype(BF16)
        outer[:, pl.ds(2 * D + pair * 128, 128)] = grad_v.astype(BF16)
        if pair % 2 == 1:
            for part in range(3):
                columns = pl.ds(part * D + (pair - 1) * 128, 256)
                term = dot_nt(outer[:, columns], qkv_held[:, columns])
                grad_normed = term if grad_normed is None else grad_normed + term
    width = 4 * D // len(targets)
    for part, target in enumerate(targets):
        sender.send(outer.at[:, pl.ds(part * width, width)], target)
    grad_hidden, gain_out[...] = norm_back(grad_normed, rows_ref[...].astype(F32), gain_ref[0:1])
    return middle[...] + grad_hidden


def saved_shapes():
    return [((ROWS, 3 * D), BF16), ((HEADS, ROWS, ROWS), BF16), ((ROWS, D), F32)]


def grads_shapes(item):
    inner = ((ROWS, FF), BF16, "any")
    if item < MB - 1:
        return [inner, ((ROWS, 4 * D), BF16, "any")]
    return [inner, ((ROWS, 2 * D), BF16, "any"), ((ROWS + 16, 2 * D), BF16, "any")]


def lower_attend_kernel(lengths, feeds, gain_ref, qkv_held, proj_held, *rest):
    saved, lefts, (left_rows, sems) = rest[: 3 * MB], rest[3 * MB : 3 * MB + 2], rest[3 * MB + 2 :]
    place = Place(lengths)

    @pl.when(place.is_lower)
    def _():
        sender = Sender(sems)
        for item in range(MB):
            rows_ref = feeds.at[pl.ds(item * ROWS, ROWS)]
            attend_body(
                sender,
                place,
                item,
                rows_ref,
                gain_ref,
                (qkv_held, proj_held),
                *saved[3 * item : 3 * item + 3],
                lefts,
                left_rows.at[item],
            )
        sender.finish()


def lower_attend(lengths, feeds, gains, qkv_held, proj_held):
    outs = [(*shape, "vmem") for _ in range(MB) for shape in saved_shapes()]
    outs += [((MB * ROWS, KEPT), BF16, LEFTS)] * 2
    ins = [(lengths, "smem")]
    ins += [(value, "vmem") for value in (feeds, gains, qkv_held, proj_held)]
    scratch = [pltpu.VMEM((MB, 2, ROWS, D), BF16), pltpu.SemaphoreType.DMA((4 * MB,))]
    return call(lower_attend_kernel, "lower_attend", ins, outs, scratch)


def lower_expand_kernel(n_alias, item, lengths, mixed, gain_ref, in_held, back_held, *rest):
    slope, keep_out, send_out, low, second_rows, active, high, sems = rest[n_alias:]
    place = Place(lengths)

    @pl.when(place.is_lower)
    def _():
        sender = Sender(sems)
        expand_body(
            sender,
            place,
            item,
            True,
            mixed,
            gain_ref,
            (in_held, back_held),
            slope,
            (keep_out, send_out),
            second_rows,
            active,
            high,
        )
        low[...] = high[...].astype(BF16)
        sender.finish()


def lower_expand(item, lengths, mixed, gains, in_held, back_held, earlier):
    outs = [
        ((ROWS, FF), BF16, "vmem"),
        ((MB * ROWS, KEPT), BF16, LEFTS),
        ((MB * ROWS, KEPT), BF16, LEFTS),
        ((ROWS, D), BF16, "vmem"),
    ]
    ins = [(lengths, "smem")]
    ins += [(value, "vmem") for value in (mixed, gains, in_held, back_held)]
    ins, aliases = with_earlier(ins, outs, earlier)
    scratch = [
        pltpu.VMEM((ROWS, D), BF16),
        pltpu.VMEM((ROWS, FF), BF16),
        pltpu.VMEM((ROWS, D), F32),
        pltpu.SemaphoreType.DMA((4,)),
    ]
    kernel = functools.partial(lower_expand_kernel, len(aliases), item)
    return call(kernel, "lower_expand", ins, outs, scratch, aliases)


def top_attend_kernel(n_alias, item, lengths, rows_ref, gain_ref, qkv_held, proj_held, *rest):
    qkv_rows, probs, mixed, keep_out, send_out, left_rows, sems = rest[n_alias:]
    place = Place(lengths)

    @pl.when(jnp.logical_not(place.is_lower))
    def _():
        sender = Sender(sems)
        attend_body(
            sender,
            place,
            item,
            rows_ref,
            gain_ref,
            (qkv_held, proj_held),
            qkv_rows,
            probs,
            mixed,
            (keep_out, send_out),
            left_rows,
        )
        sender.finish()


def top_attend(item, lengths, rows, gains, qkv_held, proj_held, earlier):
    outs = [(*shape, "vmem") for shape in saved_shapes()]
    outs += [((MB * ROWS, KEPT), BF16, LEFTS)] * 2
    ins = [(lengths, "smem")]
    ins += [(value, "vmem") for value in (rows, gains, qkv_held, proj_held)]
    ins, aliases = with_earlier(ins, outs, earlier)
    scratch = [pltpu.VMEM((2, ROWS, D), BF16), pltpu.SemaphoreType.DMA((4,))]
    kernel = functools.partial(top_attend_kernel, len(aliases), item)
    return call(kernel, "top_attend", ins, outs, scratch, aliases)


def top_expand_kernel(n_alias, item, lengths, mixed, gain_ref, in_held, back_held, *rest):
    slope, keep_out, send_out, high, second_rows, active, sems = rest[n_alias:]
    place = Place(lengths)

    @pl.when(jnp.logical_not(place.is_lower))
    def _():
        sender = Sender(sems)
        expand_body(
            sender,
            place,
            item,
            False,
            mixed,
            gain_ref,
            (in_held, back_held),
            slope,
            (keep_out, send_out),
            second_rows,
            active,
            high,
        )
        sender.finish()


def top_expand(item, lengths, mixed, gains, in_held, back_held, earlier):
    outs = [
        ((ROWS, FF), BF16, "vmem"),
        ((MB * ROWS, KEPT), BF16, LEFTS),
        ((MB * ROWS, KEPT), BF16, LEFTS),
        ((ROWS, D), F32, "vmem"),
    ]
    ins = [(lengths, "smem")]
    ins += [(value, "vmem") for value in (mixed, gains, in_held, back_held)]
    ins, aliases = with_earlier(ins, outs, earlier)
    scratch = [
        pltpu.VMEM((ROWS, D), BF16),
        pltpu.VMEM((ROWS, FF), BF16),
        pltpu.SemaphoreType.DMA((4,)),
    ]
    kernel = functools.partial(top_expand_kernel, len(aliases), item)
    return call(kernel, "top_expand", ins, outs, scratch, aliases)


def top_expand_back_kernel(item, lengths, feeds, mixed, slope, gain_ref, in_held, back_held, *rest):
    target, gain_out, middle, inner, sems = rest
    place = Place(lengths)

    @pl.when(jnp.logical_not(place.is_lower))
    def _():
        sender = Sender(sems)
        expand_back_body(
            sender,
            place,
            item,
            False,
            feeds.at[pl.ds(item * ROWS, ROWS)],
            mixed,
            slope,
            gain_ref,
            (in_held, back_held),
            target,
            gain_out,
            middle,
            inner,
        )
        sender.finish()


def top_expand_back(item, lengths, feeds, mixed, slope, gains, in_held, back_held):
    outs = [grads_shapes(item)[0], ((1, D), F32, "vmem"), ((ROWS, D), F32, "vmem")]
    ins = [(lengths, "smem")]
    ins += [(value, "vmem") for value in (feeds, mixed, slope, gains, in_held, back_held)]
    scratch = [pltpu.VMEM((ROWS, FF), BF16), pltpu.SemaphoreType.DMA((1,))]
    kernel = functools.partial(top_expand_back_kernel, item)
    return call(kernel, "top_expand_back", ins, outs, scratch)


def top_attend_back_kernel(lengths, rows_ref, middle, qkv_rows, probs, gain_ref, *rest):
    weights, rest = rest[:2], rest[2:]
    *targets, gain_out, low, outer, sems = rest
    targets[-1] = targets[-1].at[pl.ds(0, ROWS)]
    place = Place(lengths)

    @pl.when(jnp.logical_not(place.is_lower))
    def _():
        sender = Sender(sems)
        low[...] = attend_back_body(
            sender, rows_ref, middle, qkv_rows, probs, gain_ref, weights, targets, gain_out, outer
        ).astype(BF16)
        sender.finish()


def top_attend_back(item, lengths, rows, middle, saved, gains, weights):
    outs = [*grads_shapes(item)[1:], ((1, D), F32, "vmem"), ((ROWS, D), BF16, "vmem")]
    ins = [(lengths, "smem")]
    ins += [(value, "vmem") for value in (rows, middle, *saved, gains, *weights)]
    scratch = [pltpu.VMEM((ROWS, 4 * D), BF16), pltpu.SemaphoreType.DMA((2,))]
    return call(top_attend_back_kernel, "top_attend_back", ins, outs, scratch)


def lower_expand_back_kernel(
    n_alias, item, lengths, grad_ref, mixed, slope, gain_ref, in_held, back_held, *rest
):
    target, gain_out, middle, inner, sems = rest[n_alias:]
    place = Place(lengths)

    @pl.when(place.is_lower)
    def _():
        sender = Sender(sems)
        expand_back_body(
            sender,
            place,
            item,
            True,
            grad_ref,
            mixed,
            slope,
            gain_ref,
            (in_held, back_held),
            target,
            gain_out,
            middle,
            inner,
        )
        sender.finish()


def lower_expand_back(item, lengths, grad, mixed, slope, gains, in_held, back_held, earlier):
    outs = [grads_shapes(item)[0], ((1, D), F32, "vmem"), ((ROWS, D), F32, "vmem")]
    ins = [(lengths, "smem")]
    ins += [(value, "vmem") for value in (grad, mixed, slope, gains, in_held, back_held)]
    ins, aliases = with_earlier(ins, outs, earlier)
    scratch = [pltpu.VMEM((ROWS, FF), BF16), pltpu.SemaphoreType.DMA((1,))]
    kernel = functools.partial(lower_expand_back_kernel, len(aliases), item)
    size = 1 << 16 if item < MB - 1 else 1
    return call(kernel, "lower_expand_back", ins, outs, scratch, aliases, size)


def lower_attend_back_kernel(n_alias, item, lengths, feeds, middle, qkv_rows, probs, gain_ref, *rest):
    weights, rest = rest[:2], rest[2:]
    tops, others, rest = rest[:MB], rest[MB : MB + 3], rest[MB + 3 + n_alias :]
    if item < MB - 1:
        grads, gain_out, ends_out, outer, high, sems = rest
        targets = [grads]
    else:
        first, last, gain_out, ends_out, gain_keep, outer, high, gain_rows, sems = rest
        targets = [first, last.at[pl.ds(0, ROWS)]]
    place = Place(lengths)
    rows = pl.ds(item * ROWS, ROWS)

    @pl.when(place.is_lower)
    def _():
        sender = Sender(sems)
        high[...] = attend_back_body(
            sender,
            feeds.at[rows],
            middle,
            qkv_rows,
            probs,
            gain_ref,
            weights,
            targets,
            gain_out,
            outer,
        )
        sender.send(high, ends_out.at[rows])
        sender.finish()

    if item == MB - 1:
        sender = Sender(sems)

        @pl.when(jnp.logical_not(place.is_lower))
        def _():
            top_sender = Sender(sems)
            for top_item, top_high in enumerate(tops):
                top_sender.send(top_high, ends_out.at[pl.ds(top_item * ROWS, ROWS)])
            top_sender.finish()

        own, other = places(place.pos, HALF)
        gain_rows[...] = jnp.zeros_like(gain_rows)
        for row, parts in enumerate(((others[0], gain_out), others[1:])):
            gain_keep[row : row + 1] = parts[0][:, own] + parts[1][:, own]
            gain_rows[row : row + 1, pl.ds(0, HALF)] = parts[0][:, other] + parts[1][:, other]
        outer[pl.ds(0, 16), pl.ds(0, 2 * D)] = gain_rows[...].astype(BF16)
        sender.send(outer.at[pl.ds(0, 16), pl.ds(0, 2 * D)], last.at[pl.ds(ROWS, 16)])
        sender.finish()


def lower_attend_back(item, lengths, feeds, middle, saved, gains, weights, tops, others, earlier):
    outs = [
        *grads_shapes(item)[1:],
        ((1, D), F32, "vmem"),
        ((MB * ROWS, D), F32, "any"),
    ]
    scratch = [pltpu.VMEM((ROWS, 4 * D), BF16), pltpu.VMEM((ROWS, D), F32)]
    if item == MB - 1:
        outs.append(((2, HALF), F32, "vmem"))
        scratch.append(pltpu.VMEM((16, 2 * D), F32))
    scratch.append(pltpu.SemaphoreType.DMA((3,)))
    ins = [(lengths, "smem")]
    ins += [(value, "vmem") for value in (feeds, middle, *saved, gains, *weights, *tops, *others)]
    ins, aliases = with_earlier(ins, outs, earlier)
    kernel = functools.partial(lower_attend_back_kernel, len(aliases), item)
    return call(kernel, "lower_attend_back", ins, outs, scratch, aliases)


def expert_rows(place, item, partner, expert, live_only=False):
    row = lax.broadcasted_iota(jnp.int32, (1, ROWS), 1)
    first, second = place.experts(item, partner)
    mine = jnp.where(row < IMAGE_ROWS, first, second) == expert
    if live_only:
        mine = mine & (row < place.live(item, partner))
    return mine


def bits_but(*taken):
    count = lax.axis_size("dp").bit_length() - 1
    return [bit for bit in reversed(range(count)) if bit not in taken]


def block_numbers(first_bit):
    here = (lax.axis_index("dp") >> first_bit) & 1
    rest = bits_but(first_bit)
    for number in range(1 << len(rest)):
        where = tuple((number >> (len(rest) - 1 - place)) & 1 for place in range(len(rest)))
        base = sum(value << bit for value, bit in zip(where, rest))
        yield where, base + (here << first_bit), base + ((1 - here) << first_bit)


def write_blocks(total, rows, first_bit, mine, theirs):
    for where, own, other in block_numbers(first_bit):
        own_at = pl.ds(pl.multiple_of(own * rows, rows), rows)
        other_at = pl.ds(pl.multiple_of(other * rows, rows), rows)
        mine[where] = total[own_at].astype(BF16)
        theirs[where] = total[other_at].astype(BF16)


def back_grads_kernel(orders, n_items, lengths, *refs):
    actives, grads, feeds = refs[:n_items], refs[n_items : 2 * n_items], refs[2 * n_items : 2 * n_items + 2]
    outs, (flipped, total) = refs[2 * n_items + 2 : -2], refs[-2:]
    place = Place(lengths)
    tail = ROWS - TAIL
    rows = D // lax.axis_size("dp")

    @pl.when(pl.program_id(0) == 0)
    def _():
        for index in range(n_items):
            item, partner = index % MB, index >= MB
            top = feeds[index // MB][pl.ds(item * ROWS, ROWS)]
            value = jnp.where(place.is_lower, grads[index][...], top).T
            for expert in (0, 1):
                mask = expert_rows(place, item, partner, expert, live_only=True)
                flipped[expert, :, pl.ds(index * ROWS, ROWS)] = jnp.where(mask, value, 0)

    def finished(expert):
        write_blocks(total, rows, orders[expert][0], outs[2 * expert], outs[2 * expert + 1])

    def whole(expert):
        result = None
        for index in range(n_items):
            term = dot_nn(flipped[expert, :, pl.ds(index * ROWS, ROWS)], actives[index][...])
            result = term if result is None else result + term
        total[...] = result

    whole(0)
    finished(0)

    @pl.when(place.is_lower)
    def _():
        left = [
            flipped[1, :, pl.ds(index * ROWS + ROWS // 2, ROWS // 2)] for index in range(n_items)
        ]
        right = [actives[index][pl.ds(ROWS // 2, ROWS // 2)] for index in range(n_items)]
        total[...] = dot_nn(jnp.concatenate(left, axis=1), jnp.concatenate(right, axis=0))

    @pl.when(jnp.logical_not(place.is_lower))
    def _():
        whole(1)

    finished(1)


def halves_shape(block):
    return jax.ShapeDtypeStruct((2,) * len(bits_but(0)) + block, BF16)


def halves_spec(block, place):
    lead = len(bits_but(0))
    return pl.BlockSpec((2,) * lead + block, lambda step: (0,) * lead + place(step))


def by_item(width, count, column, **options):
    return [
        pl.BlockSpec((ROWS, width), lambda step, item=index % MB: (item, column(step)), **options)
        for index in range(count)
    ]


def back_grads(lengths, kept, grads, feeds, orders):
    width = 256
    block = (D // lax.axis_size("dp"), width)
    once = pl.Buffered(1)
    fixed = [pl.BlockSpec((ROWS, D), lambda step: (0, 0), pipeline_mode=once)] * len(kept)
    fixed += [pl.BlockSpec((MB * ROWS, D), lambda step: (0, 0), pipeline_mode=once)] * 2
    results = pl.pallas_call(
        functools.partial(back_grads_kernel, orders, len(kept)),
        grid=(FF_HALF // width,),
        out_shape=[halves_shape((block[0], FF_HALF)) for _ in orders for _ in (0, 1)],
        in_specs=[pl.BlockSpec(memory_space=pltpu.SMEM)]
        + by_item(width, len(kept), lambda step: step)
        + fixed,
        out_specs=[
            halves_spec(block, lambda step: (0, step)) for _ in orders for _ in (0, 1)
        ],
        scratch_shapes=[
            pltpu.VMEM((2, D, len(kept) * ROWS), BF16),
            pltpu.VMEM((D, width), F32),
        ],
        compiler_params=pltpu.CompilerParams(vmem_limit_bytes=VMEM_BYTES),
        cost_estimate=cost(1),
        name="back_grads",
    )(lengths, *kept, *grads, *feeds)
    return [tuple(results[2 * expert : 2 * expert + 2]) for expert in (0, 1)]


def in_grads_kernel(width, n_items, lengths, *refs):
    seconds, inners = refs[:n_items], refs[n_items : 2 * n_items]
    outs, (flipped, total) = refs[2 * n_items : -2], refs[-2:]
    place = Place(lengths)
    half = ROWS // 2
    low_bit = lax.axis_index("dp") % 2

    @pl.when(pl.program_id(0) == 0)
    def _():
        for index in range(n_items):
            item, partner = index % MB, index >= MB
            value = seconds[index][...].T
            for expert in (0, 1):
                mask = expert_rows(place, item, partner, expert)
                flipped[expert, :, pl.ds(index * ROWS, ROWS)] = jnp.where(mask, value, 0)

    def whole(expert):
        result = None
        for index in range(n_items):
            term = dot_nn(flipped[expert, :, pl.ds(index * ROWS, ROWS)], inners[index][...])
            result = term if result is None else result + term
        total[...] = result

    def finished(expert):
        if len(outs) == 2:
            outs[expert][0] = total[...].astype(BF16)
            return
        for out, bit in zip(outs[2 * expert : 2 * expert + 2], (low_bit, 1 - low_bit)):
            out[0] = total[:, pl.ds(pl.multiple_of(bit * width, width), width)].astype(BF16)

    whole(0)
    finished(0)

    @pl.when(place.is_lower)
    def _():
        left = [flipped[1, :, pl.ds(index * ROWS + half, half)] for index in range(n_items)]
        right = [inners[index][pl.ds(half, half)] for index in range(n_items)]
        total[...] = dot_nn(jnp.concatenate(left, axis=1), jnp.concatenate(right, axis=0))

    @pl.when(jnp.logical_not(place.is_lower))
    def _():
        whole(1)

    finished(1)


def in_grads(lengths, kept, inners):
    size = lax.axis_size("dp")
    width = FF // size
    aligned = width % 128 == 0
    columns = 2 * width if aligned else D
    steps = FF // columns
    once = pl.Buffered(1)
    block = (1, HALF, width if aligned else columns)
    count = 4 if aligned else 2
    results = pl.pallas_call(
        functools.partial(in_grads_kernel, width, len(kept)),
        grid=(steps,),
        out_shape=[jax.ShapeDtypeStruct((steps,) + block[1:], BF16)] * count,
        in_specs=[pl.BlockSpec(memory_space=pltpu.SMEM)]
        + by_item(HALF, len(kept), lambda step: FF_HALF // HALF, pipeline_mode=once)
        + [pl.BlockSpec((ROWS, columns), lambda step: (0, step))] * len(inners),
        out_specs=[pl.BlockSpec(block, lambda step: (step, 0, 0))] * count,
        scratch_shapes=[
            pltpu.VMEM((2, HALF, len(kept) * ROWS), BF16),
            pltpu.VMEM((HALF, columns), F32),
        ],
        compiler_params=pltpu.CompilerParams(vmem_limit_bytes=VMEM_BYTES),
        cost_estimate=cost(1),
        name="in_grads",
    )(lengths, *kept, *inners)
    if not aligned:
        whole = [part.transpose(1, 0, 2).reshape(HALF, size, width) for part in results]
        return [by_lowest_bit(part.transpose(1, 0, 2)) for part in whole]
    shape = (2,) * len(bits_but(0)) + block[1:]
    return [tuple(part.reshape(shape) for part in results[2 * e : 2 * e + 2]) for e in (0, 1)]


def outer_grads_kernel(order, *refs):
    lefts, outers, gains, pieces, total = refs[:4], refs[4:10], refs[10:12], refs[12:16], refs[16]
    step = pl.program_id(0)
    result = None
    for index in range(4):
        outer = outers[3 * (index // MB)][...]
        if index % MB == MB - 1:
            first, second = outers[3 * (index // MB) + 1 : 3 * (index // MB) + 3]
            outer = jnp.where(step < 2, first[...], second[...])
        term = dot_tn(outer, lefts[index][...])
        result = term if result is None else result + term
    total[pl.ds(pl.multiple_of(step * D, D), D)] = result

    @pl.when(step == 3)
    def _():
        size = lax.axis_size("dp")
        proj_rows = D // size
        gain_rows = gains[0][...] + gains[1][pl.ds(0, 2), pl.ds(0, HALF)].astype(F32)
        gain_rows = jnp.concatenate([gain_rows, jnp.zeros((14, HALF), F32)], axis=0)
        for where, *numbers in block_numbers(order[0]):
            for target, number in zip((0, 1), numbers):
                at = pl.multiple_of(number * 3 * proj_rows, proj_rows)
                below = pl.multiple_of(3 * D + number * proj_rows, proj_rows)
                first, second = pieces[target], pieces[2 + target]
                first[where] = total[pl.ds(at, 2 * proj_rows)].astype(BF16)
                second[where + (pl.ds(0, proj_rows),)] = total[
                    pl.ds(at + 2 * proj_rows, proj_rows)
                ].astype(BF16)
                second[where + (pl.ds(proj_rows, proj_rows),)] = total[
                    pl.ds(below, proj_rows)
                ].astype(BF16)
                turned = pltpu.roll(gain_rows, HALF - number * (HALF // size), 1)
                second[where + (pl.ds(2 * proj_rows, 16),)] = turned.astype(BF16)


def outer_grads(kept, outers, gains, order):
    block = (2 * D // lax.axis_size("dp"), HALF)
    last = (block[0] + 16, HALF)
    results = pl.pallas_call(
        functools.partial(outer_grads_kernel, order),
        grid=(4,),
        out_shape=[halves_shape(block)] * 2 + [halves_shape(last)] * 2,
        in_specs=by_item(HALF, 4, lambda step: FF_HALF // HALF + 1 + step // 3)
        + [
            pl.BlockSpec((ROWS, D), lambda step: (0, step)),
            pl.BlockSpec((ROWS, D), lambda step: (0, jnp.minimum(step, 1))),
            pl.BlockSpec((ROWS, D), lambda step: (0, jnp.maximum(step - 2, 0))),
        ]
        * 2
        + [
            pl.BlockSpec((2, HALF), lambda step: (0, 0)),
            pl.BlockSpec((16, D), lambda step: (ROWS // 16, 0)),
        ],
        out_specs=[halves_spec(block, lambda step: (0, 0))] * 2
        + [halves_spec(last, lambda step: (0, 0))] * 2,
        scratch_shapes=[pltpu.VMEM((4 * D, HALF), F32)],
        compiler_params=pltpu.CompilerParams(vmem_limit_bytes=2 * VMEM_BYTES),
        cost_estimate=cost(1),
        name="outer_grads",
    )(*kept, *outers, *gains)
    return tuple(results[:2]), tuple(results[2:])


def swapped(block, axis, bit, among=None):
    among = range(lax.axis_size(axis)) if among is None else among
    return lax.ppermute(block, axis, [(place, place ^ 1 << bit) for place in among])


def per_item(arrays):
    return [array for array in arrays for _ in range(MB)]


def passed_along(value, steps):
    count = lax.axis_size("section")
    first, last = (max(0, -steps), min(count, count - steps))
    route = [(source, source + steps) for source in range(first, last)]
    return lax.ppermute(value, "section", route)


def split_bit(stacked, bit):
    here = (lax.axis_index("dp") >> bit) & 1
    mine = lax.dynamic_index_in_dim(stacked, here, 0, keepdims=False)
    theirs = lax.dynamic_index_in_dim(stacked, 1 - here, 0, keepdims=False)
    return mine, theirs


def added_kernel(left, right, out):
    out[...] = left[...].astype(F32) + right[...].astype(F32)


def added(left, right):
    ins = [(left, "vmem"), (right, "vmem")]
    return call(added_kernel, "added", ins, [(left.shape, F32, "vmem")], [])[0]


def outer_sums_kernel(first, left, right, qkv_out, proj_out, gain_out):
    rows = proj_out.shape[0]
    second = left[...].astype(F32) + right[...].astype(F32)
    qkv_out[: 2 * rows] = first[...]
    qkv_out[2 * rows :] = second[:rows]
    proj_out[...] = second[rows : 2 * rows]
    gain_out[...] = second[2 * rows : 2 * rows + 2]


def outer_sums(first, left, right):
    rows = first.shape[0] // 2
    ins = [(value, "vmem") for value in (first, left, right)]
    shapes = [(3 * rows, HALF), (rows, HALF), (2, HALF)]
    outs = [(shape, F32, "auto") for shape in shapes]
    return call(outer_sums_kernel, "outer_sums", ins, outs, [])


def added_halves_kernel(axis, bit, left, right, mine, theirs):
    here = (lax.axis_index("dp") >> bit) & 1
    lead = (slice(None),) * axis
    for out, at in ((mine, lead + (here,)), (theirs, lead + (1 - here,))):
        out[...] = (left[at].astype(F32) + right[at].astype(F32)).astype(BF16)


def added_halves(left, right, axis, bit):
    ins = [(left, "vmem"), (right, "vmem")]
    outs = [(left.shape[:axis] + left.shape[axis + 1 :], BF16, "vmem")] * 2
    kernel = functools.partial(added_halves_kernel, axis, bit)
    return call(kernel, "added_halves", ins, outs, [])


def after(value, *earlier):
    return lax.optimization_barrier((value, earlier))[0]


class Sums:
    def __init__(self):
        self.open = {}
        self.results = {}
        self.last = []

    def begin(self, name, piece, order, taken=()):
        mine, theirs = piece
        self.open[name] = (mine, swapped(theirs, "dp", order[0]), order[1:], (*taken, order[0]))

    def step(self, name, hold=False):
        mine, got, rest, taken = self.open.pop(name)
        mine = after(mine, *self.last)
        if len(rest) == 0:
            self.results[name] = added(mine, got)
            self.last = [self.results[name]]
            return
        mine, theirs = added_halves(mine, got, bits_but(*taken).index(rest[0]), rest[0])
        self.last = [theirs]
        if hold:
            return (mine, theirs), rest, taken
        self.begin(name, (mine, theirs), rest, taken)

    def finish(self, but):
        while len(self.open) > 1 or len(self.open[but][2]) > 0:
            for name in list(self.open):
                if name != but or len(self.open[name][2]) > 0:
                    self.step(name)
        mine, got, *_ = self.open.pop(but)
        return after(mine, *self.last), got


def by_lowest_bit(stacked):
    bits = lax.axis_size("dp").bit_length() - 1
    split = jnp.moveaxis(stacked.reshape((2,) * bits + stacked.shape[1:]), bits - 1, 0)
    return split_bit(split, 0)


def shards(feeds, text_lengths, norm_gains, qkv_weight, out_weight, expert_in, expert_out):
    n_dp = lax.axis_size("dp")
    bits = n_dp.bit_length() - 1
    pos = lax.axis_index("section") % 2

    gains_other = swapped(norm_gains[0], "section", 0)
    gains = joined_gains(norm_gains[0], gains_other)
    own = [qkv_weight[0], out_weight[0]]
    other = [swapped(part, "section", 0) for part in own]
    held = joined_halves(own, other)
    in_other = swapped(after(expert_in[0], gains_other, *other), "section", 0)
    back_other = swapped(after(expert_out[0], gains_other, *other), "section", 0)

    *saved, keep, send = lower_attend(text_lengths, feeds, gains, *held)
    saved = [saved[3 * item : 3 * item + 3] for item in range(MB)]
    earlier = saved[-1][2]
    held += joined_halves([expert_in[0]], [after(in_other, earlier)])
    held += joined_halves([expert_out[0]], [after(back_other, earlier)])
    slopes, passed = [], []
    for item in range(MB):
        mixed = after(saved[item][2], earlier)
        slope, keep, send, earlier = lower_expand(
            item, text_lengths, mixed, gains, *held[2:], {1: keep, 2: send}
        )
        slopes.append(slope)
        passed.append(passed_along(earlier, 2))
    grads, gain_grads, ups = [], [], []
    tops = []
    for item in range(MB):
        rows = after(passed[item], earlier)
        places = dict(enumerate(saved[item])) | {3: keep, 4: send}
        *saved[item], keep, send = top_attend(
            item, text_lengths, rows, gains, *held[:2], places
        )
        mixed = saved[item][2]
        places = {0: slopes[item], 1: keep, 2: send}
        slopes[item], keep, send, top = top_expand(
            item, text_lengths, mixed, gains, *held[2:], places
        )
        tops.append(top)
        inner, gain_second, middle = top_expand_back(
            item, text_lengths, feeds, mixed, slopes[item], gains, *held[2:]
        )
        *outer, gain_first, earlier = top_attend_back(
            item,
            text_lengths,
            rows,
            middle,
            saved[item][:2],
            gains,
            held[:2],
        )
        grads.append([inner, *outer])
        gain_grads.append([gain_first, gain_second])
        ups.append(passed_along(earlier, -2))
    feeds_pair = [feeds, swapped(after(feeds, earlier), "section", 0, (2, 3))]
    lefts = per_item([keep, swapped(after(send, earlier), "section", 0)])

    upward = tuple(range(bits))
    back_orders = [upward[1:] + upward[:1], upward]

    def lower_back_experts(item, up):
        results = {0: grads[item][0], 1: gain_grads[item][1]}
        grads[item][0], gain_grads[item][1], middle = lower_expand_back(
            item, text_lengths, up, saved[item][2], slopes[item], gains, *held[2:], results
        )
        return middle

    def lower_back_heads(item, middle, ends, others):
        parts = [*grads[item][1:], gain_grads[item][0], *ends]
        results = lower_attend_back(
            item,
            text_lengths,
            feeds,
            middle,
            saved[item][:2],
            gains,
            held[:2],
            tops,
            others,
            dict(enumerate(parts)),
        )
        count = len(grads[item]) - 1
        grads[item][1:], gain_grads[item][0] = results[:count], results[count]
        return results[count + 1 :]

    ups[0] = after(ups[0], earlier)
    ups_other = [swapped(ups[0], "section", 0, (0, 1))]
    middle = lower_back_experts(0, ups[0])
    (ends,) = lower_back_heads(0, middle, [], [gain_grads[0][1]] * 3)
    first_grads = [(part, swapped(part, "section", 0)) for part in grads[0]]
    ups[1] = after(ups[1], ends)
    ups_other.append(swapped(ups[1], "section", 0, (0, 1)))
    middle = lower_back_experts(1, after(ups[1], ups_other[0]))
    inner = grads[1][0]
    inners = [first_grads[0][0], inner, first_grads[0][1], swapped(inner, "section", 0)]
    ups_other[1] = after(ups_other[1], middle)
    back_pieces = back_grads(text_lengths, lefts, ups + ups_other, feeds_pair, back_orders)
    inners[1] = after(inners[1], back_pieces[0][1], back_pieces[1][1])
    in_pieces = in_grads(text_lengths, lefts, inners)

    sums = Sums()
    for number in (0, 1):
        sums.begin(f"back{number}", back_pieces[number], back_orders[number])
    sums.begin("in0", in_pieces[0], upward)
    middle = after(middle, in_pieces[0][1], in_pieces[1][1])
    others = [gain_grads[0][0], gain_grads[0][1], gain_grads[1][1]]
    ends, gain_keep = lower_back_heads(1, middle, [ends], others)
    outers = [first_grads[1][0], *grads[1][1:], first_grads[1][1]]
    outers += [swapped(part, "section", 0) for part in grads[1][1:]]
    sums.last = [ends]
    sums.step("back0")
    sums.step("back1")
    gain_keep = after(gain_keep, *sums.last)
    outer_pieces = outer_grads(lefts, outers, (gain_keep, outers[-1]), upward)
    sums.last = [piece[1] for piece in outer_pieces]

    def later(piece):
        return piece[0], after(piece[1], *sums.last)

    sums.begin("in1", later(in_pieces[1]), upward)
    sums.begin("outer0", later(outer_pieces[0]), upward)
    for name in ("back1", "back0", "in0", "in0", "in1", "back1"):
        sums.step(name)
    sums.begin("outer1", later(outer_pieces[1]), upward)
    order = ("outer0", "in1", "in0", "outer1", "outer0", "in1", "outer1", "outer0", "back0")
    for name in order:
        sums.step(name)
    last = sums.finish("outer1")
    qkv_sum, proj_sum, gain_sum = outer_sums(sums.results["outer0"], *last)
    done = sums.results
    return (
        ends,
        gain_sum[None, :, : HALF // n_dp],
        qkv_sum.T[None],
        proj_sum.T[None],
        jnp.stack([done["in0"], done["in1"]])[None],
        jnp.stack([done["back0"].T, done["back1"].T])[None],
    )


def solution(mesh):
    return jax.shard_map(
        shards,
        mesh=mesh,
        in_specs=(
            P(("dp", "section"), None),
            P("dp"),
            P("section", None, None),
            P("section", None, None),
            P("section", None, None),
            P("section", None, None, None),
            P("section", None, None, None),
        ),
        out_specs=(
            P(("dp", "section"), None),
            P("section", None, "dp"),
            P("section", None, "dp"),
            P("section", None, "dp"),
            P("section", None, None, "dp"),
            P("section", None, None, "dp"),
        ),
        check_vma=False,
    )
```

```python
import functools

import jax
import jax.numpy as jnp
from jax import lax
from jax.experimental import pallas as pl
from jax.experimental.pallas import tpu as pltpu
from jax.sharding import PartitionSpec as P

D = 768
HALF = D // 2
HEADS = 12
FF = 3072
FF_HALF = FF // 2
HEAD_DIM = 64
IMAGE_ROWS = 197
ROWS = 256
MB = 2
KEPT = FF_HALF + 3 * HALF
TAIL = 192

EPSILON = 1e-05
MASKED = -1e30
F32 = jnp.float32
BF16 = jnp.bfloat16
VMEM_BYTES = 10 * 1024 * 1024
LEFTS = "any"


def cost(size):
    return pl.CostEstimate(flops=size << 20, bytes_accessed=1 << 10, transcendentals=0)


def dot_nn(left, right):
    return lax.dot_general(left, right, (((1,), (0,)), ((), ())), preferred_element_type=F32)


def dot_nt(left, right):
    return lax.dot_general(left, right, (((1,), (1,)), ((), ())), preferred_element_type=F32)


def dot_tn(left, right):
    return lax.dot_general(left, right, (((0,), (0,)), ((), ())), preferred_element_type=F32)


def norm_parts(hidden):
    centred = hidden - jnp.mean(hidden, axis=-1, keepdims=True)
    spread = jnp.mean(centred * centred, axis=-1, keepdims=True)
    inverse = lax.rsqrt(spread + EPSILON)
    return centred * inverse, inverse


def norm_back(grad, hidden, gain_row):
    unit, inverse = norm_parts(hidden)
    gain_grad = jnp.sum(grad * unit, axis=0, keepdims=True)
    scaled = grad * gain_row
    mean_plain = jnp.mean(scaled, axis=-1, keepdims=True)
    mean_unit = jnp.mean(scaled * unit, axis=-1, keepdims=True)
    return inverse * (scaled - mean_plain - unit * mean_unit), gain_grad


def gelu_pair(values):
    size = jnp.abs(values)
    denom = 1.0 + (0.3275911 * 0.7071067811865476) * size
    t = pl.reciprocal(denom, approx=True)
    poly = 0.5 * 1.061405429
    for factor in (-1.453152027, 1.421413741, -0.284496736, 0.254829592):
        poly = poly * t + 0.5 * factor
    bell = jnp.exp2(values * values * (-0.5 * 1.4426950408889634))
    upper_tail = poly * t * bell
    cdf = jnp.where(values < 0, upper_tail, 1.0 - upper_tail)
    return values * cdf, cdf + values * bell * 0.3989422804014327


def lane_half(value, which):
    lanes = lax.broadcasted_iota(jnp.int32, value.shape, 1)
    picked = lanes < HEAD_DIM if which == 0 else lanes >= HEAD_DIM
    return jnp.where(picked, value, jnp.zeros_like(value))


def call(kernel, name, ins, outs, scratch, aliases=None, size=1, memory=VMEM_BYTES):
    spaces = {"vmem": pltpu.VMEM, "auto": pltpu.VMEM, "smem": pltpu.SMEM, "any": pl.ANY, "hbm": pltpu.HBM}
    kinds = {"vmem": pltpu.VMEM, "auto": jax.ShapeDtypeStruct, "any": jax.ShapeDtypeStruct, "hbm": pltpu.HBM}
    shapes = [kinds[space](shape, kind) for shape, kind, space in outs]
    return pl.pallas_call(
        kernel,
        out_shape=shapes,
        in_specs=[pl.BlockSpec(memory_space=spaces[space]) for _, space in ins],
        out_specs=[pl.BlockSpec(memory_space=spaces[space]) for _, _, space in outs],
        input_output_aliases=aliases or {},
        scratch_shapes=scratch,
        compiler_params=pltpu.CompilerParams(vmem_limit_bytes=memory),
        cost_estimate=cost(size),
        name=name,
    )(
        *[
            pltpu.with_memory_space_constraint(value, pltpu.HBM) if space == "hbm" else value
            for value, space in ins
        ]
    )


class Place:
    def __init__(self, lengths):
        section = lax.axis_index("section")
        self.lengths = lengths
        self.is_lower = section < 2
        self.pos = section % 2

    def length(self, item, partner=False):
        pos = 1 - self.pos if partner else self.pos
        return self.lengths[pos * MB + item]

    def live(self, item, partner=False):
        return IMAGE_ROWS + self.length(item, partner)

    def experts(self, item, partner=False):
        kind = jnp.where(self.length(item, partner) > 0, 1, 0)
        return jnp.where(self.is_lower, 0, kind), jnp.where(self.is_lower, 1, kind)


def with_earlier(ins, outs, earlier):
    aliases = {}
    for number, value in (earlier or {}).items():
        aliases[len(ins)] = number
        ins = ins + [(value, outs[number][2])]
    return ins, aliases


class Sender:
    def __init__(self, sems):
        self.sems = sems
        self.sent = []
        self.done = 0

    def send(self, source, target):
        copy = pltpu.make_async_copy(source, target, self.sems.at[len(self.sent)])
        copy.start()
        self.sent.append(copy)

    def finish(self, count=None):
        count = len(self.sent) - self.done if count is None else count
        for copy in self.sent[self.done : self.done + count]:
            copy.wait()
        self.done += count


def join_kernel(count, *refs):
    own, other, joined, sems = refs[:count], refs[count : 2 * count], refs[2 * count : -1], refs[-1]
    pos = lax.axis_index("section") % 2
    sender = Sender(sems)
    for mine, theirs, whole in zip(own, other, joined):
        depth = mine.shape[-2]
        for source, at in ((mine, pos), (theirs, 1 - pos)):
            rows = pl.ds(pl.multiple_of(at * depth, depth), depth)
            if len(whole.shape) == 2:
                sender.send(source, whole.at[rows])
            else:
                for expert in range(whole.shape[0]):
                    sender.send(source.at[expert], whole.at[expert, rows])
    sender.finish()


def joined_halves(own, other):
    outs = []
    for part in own:
        shape = part.shape[:-2] + (2 * part.shape[-2], part.shape[-1])
        outs.append((shape, BF16, "vmem"))
    return call(
        functools.partial(join_kernel, len(own)),
        "joined_halves",
        [(value, "hbm") for value in own] + [(value, "any") for value in other],
        outs,
        [pltpu.SemaphoreType.DMA((4 * len(own),))],
    )


def gains_kernel(own, other, gains):
    first = lax.axis_index("section") % 2 == 0
    mine, theirs = own[...].astype(F32), other[...].astype(F32)
    gains[:, pl.ds(0, HALF)] = jnp.where(first, mine, theirs)
    gains[:, pl.ds(HALF, HALF)] = jnp.where(first, theirs, mine)


def joined_gains(own, other):
    return call(
        gains_kernel, "joined_gains", [(own, "vmem"), (other, "vmem")], [((2, D), F32, "vmem")], []
    )[0]


def places(pos, size):
    return (
        pl.ds(pl.multiple_of(pos * size, size), size),
        pl.ds(pl.multiple_of((1 - pos) * size, size), size),
    )


def attend_body(
    sender, place, item, rows_ref, gain_ref, weights, qkv_rows, probs, mixed, lefts, left_rows
):
    qkv_held, proj_held = weights
    own, other = places(place.pos, HALF)

    def send_halves(part):
        to = (pl.ds(item * ROWS, ROWS), pl.ds(FF_HALF + (1 + part) * HALF, HALF))
        for columns, target in zip((own, other), lefts):
            sender.send(left_rows.at[part, :, columns], target.at[to])

    normed = (norm_parts(rows_ref[...].astype(F32))[0] * gain_ref[0:1]).astype(BF16)
    left_rows[0] = normed
    send_halves(0)
    for part in range(3):
        columns = pl.ds(part * D, D)
        qkv_rows[:, columns] = dot_nn(normed, qkv_held[:, columns]).astype(BF16)
    keys_live = lax.broadcasted_iota(jnp.int32, (ROWS, ROWS), 1) < place.live(item)
    for pair in range(HEADS // 2):
        queries = qkv_rows[:, pl.ds(pair * 128, 128)] * jnp.asarray(HEAD_DIM**-0.5, BF16)
        keys = qkv_rows[:, pl.ds(D + pair * 128, 128)]
        values = qkv_rows[:, pl.ds(2 * D + pair * 128, 128)]
        context = None
        for which in (0, 1):
            scores = dot_nt(lane_half(queries, which), keys)
            scores = jnp.where(keys_live, scores, MASKED)
            shifted = jnp.exp(scores - jnp.max(scores, axis=-1, keepdims=True))
            total = jnp.sum(shifted, axis=-1, keepdims=True)
            weight = (shifted * pl.reciprocal(total, approx=True)).astype(BF16)
            probs[2 * pair + which] = weight
            term = dot_nn(weight, lane_half(values, which))
            context = term if context is None else context + term
        left_rows[1, :, pl.ds(pair * 128, 128)] = context.astype(BF16)
    send_halves(1)
    mixed[...] = rows_ref[...].astype(F32) + dot_nn(left_rows[1], proj_held[...])


def expand_body(
    sender, place, item, lower, mixed, gain_ref, weights, slope, lefts, second_rows, active, high
):
    in_held, back_held = weights
    first, second = place.experts(item)
    halves, deep_halves = places(place.pos, HALF), places(place.pos, FF_HALF)
    rows = pl.ds(item * ROWS, ROWS)

    def send_active():
        for columns, target in zip(deep_halves, lefts):
            sender.send(active.at[:, columns], target.at[rows, pl.ds(0, FF_HALF)])

    normed = (norm_parts(mixed[...])[0] * gain_ref[1:2]).astype(BF16)
    second_rows[...] = normed
    for columns, target in zip(halves, lefts):
        sender.send(second_rows.at[:, columns], target.at[rows, pl.ds(FF_HALF, HALF)])
    total = mixed[...]
    for part in range(4):
        columns = pl.ds(part * D, D)
        value, derivative = gelu_pair(dot_nn(normed, in_held[first, :, columns]))
        value = value.astype(BF16)
        active[:, columns] = value
        slope[:, columns] = derivative.astype(BF16)
        total = total + dot_nn(value, back_held[first, columns])
    if not lower:
        send_active()
    high[...] = total
    if not lower:
        return
    tail = pl.ds(TAIL, ROWS - TAIL)
    later = lax.broadcasted_iota(jnp.int32, (ROWS - TAIL, D), 0) >= IMAGE_ROWS - TAIL
    total = mixed[tail]
    for part in range(4):
        columns = pl.ds(part * D, D)
        value, derivative = gelu_pair(dot_nn(second_rows[tail], in_held[second, :, columns]))
        kept = active[tail, columns].astype(F32)
        value = jnp.where(later, value, kept).astype(BF16)
        active[tail, columns] = value
        kept = slope[tail, columns].astype(F32)
        slope[tail, columns] = jnp.where(later, derivative, kept).astype(BF16)
        total = total + dot_nn(value, back_held[second, columns])
    send_active()
    high[tail] = jnp.where(later, total, high[tail])


def expand_back_body(
    sender, place, item, lower, grad_ref, mixed, slope, gain_ref, weights, target, gain_out, middle, inner
):
    in_held, back_held = weights
    first, second = place.experts(item)
    is_live = lax.broadcasted_iota(jnp.int32, (ROWS, D), 0) < place.live(item)
    grad = jnp.where(is_live, grad_ref[...].astype(F32), 0.0)
    grad_low = grad.astype(BF16)
    for part in range(4):
        columns = pl.ds(part * D, D)
        grad_active = dot_nt(grad_low, back_held[first, columns])
        inner[:, columns] = (grad_active * slope[:, columns].astype(F32)).astype(BF16)
    if not lower:
        sender.send(inner, target)
    middle[...] = dot_nt(inner[...], in_held[first])
    if lower:
        tail = pl.ds(TAIL, ROWS - TAIL)
        later = lax.broadcasted_iota(jnp.int32, (ROWS - TAIL, D), 0) >= IMAGE_ROWS - TAIL
        for part in range(4):
            columns = pl.ds(part * D, D)
            grad_active = dot_nt(grad_low[TAIL:], back_held[second, columns])
            patched = grad_active * slope[tail, columns].astype(F32)
            kept = inner[tail, columns].astype(F32)
            inner[tail, columns] = jnp.where(later, patched, kept).astype(BF16)
        sender.send(inner, target)
        patched = dot_nt(inner[tail], in_held[second])
        middle[tail] = jnp.where(later, patched, middle[tail])
    grad_mixed, gain_out[...] = norm_back(middle[...], mixed[...], gain_ref[1:2])
    middle[...] = grad + grad_mixed


def attend_back_body(
    sender, rows_ref, middle, qkv_rows, probs, gain_ref, weights, targets, gain_out, outer
):
    qkv_held, proj_held = weights
    branch = middle[...].astype(BF16)
    outer[:, pl.ds(3 * D, D)] = branch
    grad_context = dot_nt(branch, proj_held[...]).astype(BF16)
    scale = jnp.asarray(HEAD_DIM**-0.5, BF16)
    grad_normed = None
    for pair in range(HEADS // 2):
        queries = qkv_rows[:, pl.ds(pair * 128, 128)] * scale
        keys = qkv_rows[:, pl.ds(D + pair * 128, 128)] * scale
        values = qkv_rows[:, pl.ds(2 * D + pair * 128, 128)]
        context = grad_context[:, pair * 128 : (pair + 1) * 128]
        grad_q = grad_k = grad_v = None
        for which in (0, 1):
            weight = probs[2 * pair + which]
            context_half = lane_half(context, which)
            grad_probs = dot_nt(context_half, values)
            weight_wide = weight.astype(F32)
            product = weight_wide * grad_probs
            row_total = jnp.sum(product, axis=-1, keepdims=True)
            grad_scores = (product - weight_wide * row_total).astype(BF16)
            term_v = dot_tn(weight, context_half)
            term_q = dot_nn(grad_scores, lane_half(keys, which))
            term_k = dot_tn(grad_scores, lane_half(queries, which))
            grad_q = term_q if grad_q is None else grad_q + term_q
            grad_k = term_k if grad_k is None else grad_k + term_k
            grad_v = term_v if grad_v is None else grad_v + term_v
        outer[:, pl.ds(pair * 128, 128)] = grad_q.astype(BF16)
        outer[:, pl.ds(D + pair * 128, 128)] = grad_k.astype(BF16)
        outer[:, pl.ds(2 * D + pair * 128, 128)] = grad_v.astype(BF16)
        if pair % 2 == 1:
            for part in range(3):
                columns = pl.ds(part * D + (pair - 1) * 128, 256)
                term = dot_nt(outer[:, columns], qkv_held[:, columns])
                grad_normed = term if grad_normed is None else grad_normed + term
    width = 4 * D // len(targets)
    for part, target in enumerate(targets):
        sender.send(outer.at[:, pl.ds(part * width, width)], target)
    grad_hidden, gain_out[...] = norm_back(grad_normed, rows_ref[...].astype(F32), gain_ref[0:1])
    return middle[...] + grad_hidden


def saved_shapes():
    return [((ROWS, 3 * D), BF16), ((HEADS, ROWS, ROWS), BF16), ((ROWS, D), F32)]


def grads_shapes(item):
    inner = ((ROWS, FF), BF16, "any")
    if item < MB - 1:
        return [inner, ((ROWS, 4 * D), BF16, "any")]
    return [inner, ((ROWS, 2 * D), BF16, "any"), ((ROWS + 16, 2 * D), BF16, "any")]


def lower_attend_kernel(lengths, feeds, gain_ref, qkv_held, proj_held, *rest):
    saved, lefts, (left_rows, sems) = rest[: 3 * MB], rest[3 * MB : 3 * MB + 2], rest[3 * MB + 2 :]
    place = Place(lengths)

    @pl.when(place.is_lower)
    def _():
        sender = Sender(sems)
        for item in range(MB):
            rows_ref = feeds.at[pl.ds(item * ROWS, ROWS)]
            attend_body(
                sender,
                place,
                item,
                rows_ref,
                gain_ref,
                (qkv_held, proj_held),
                *saved[3 * item : 3 * item + 3],
                lefts,
                left_rows.at[item],
            )
        sender.finish()


def lower_attend(lengths, feeds, gains, qkv_held, proj_held):
    outs = [(*shape, "vmem") for _ in range(MB) for shape in saved_shapes()]
    outs += [((MB * ROWS, KEPT), BF16, LEFTS)] * 2
    ins = [(lengths, "smem")]
    ins += [(value, "vmem") for value in (feeds, gains, qkv_held, proj_held)]
    scratch = [pltpu.VMEM((MB, 2, ROWS, D), BF16), pltpu.SemaphoreType.DMA((4 * MB,))]
    return call(lower_attend_kernel, "lower_attend", ins, outs, scratch)


def lower_expand_kernel(n_alias, item, lengths, mixed, gain_ref, in_held, back_held, *rest):
    slope, keep_out, send_out, low, second_rows, active, high, sems = rest[n_alias:]
    place = Place(lengths)

    @pl.when(place.is_lower)
    def _():
        sender = Sender(sems)
        expand_body(
            sender,
            place,
            item,
            True,
            mixed,
            gain_ref,
            (in_held, back_held),
            slope,
            (keep_out, send_out),
            second_rows,
            active,
            high,
        )
        low[...] = high[...].astype(BF16)
        sender.finish()


def lower_expand(item, lengths, mixed, gains, in_held, back_held, earlier):
    outs = [
        ((ROWS, FF), BF16, "vmem"),
        ((MB * ROWS, KEPT), BF16, LEFTS),
        ((MB * ROWS, KEPT), BF16, LEFTS),
        ((ROWS, D), BF16, "vmem"),
    ]
    ins = [(lengths, "smem")]
    ins += [(value, "vmem") for value in (mixed, gains, in_held, back_held)]
    ins, aliases = with_earlier(ins, outs, earlier)
    scratch = [
        pltpu.VMEM((ROWS, D), BF16),
        pltpu.VMEM((ROWS, FF), BF16),
        pltpu.VMEM((ROWS, D), F32),
        pltpu.SemaphoreType.DMA((4,)),
    ]
    kernel = functools.partial(lower_expand_kernel, len(aliases), item)
    return call(kernel, "lower_expand", ins, outs, scratch, aliases)


def top_attend_kernel(n_alias, item, lengths, rows_ref, gain_ref, qkv_held, proj_held, *rest):
    qkv_rows, probs, mixed, keep_out, send_out, left_rows, sems = rest[n_alias:]
    place = Place(lengths)

    @pl.when(jnp.logical_not(place.is_lower))
    def _():
        sender = Sender(sems)
        attend_body(
            sender,
            place,
            item,
            rows_ref,
            gain_ref,
            (qkv_held, proj_held),
            qkv_rows,
            probs,
            mixed,
            (keep_out, send_out),
            left_rows,
        )
        sender.finish()


def top_attend(item, lengths, rows, gains, qkv_held, proj_held, earlier):
    outs = [(*shape, "vmem") for shape in saved_shapes()]
    outs += [((MB * ROWS, KEPT), BF16, LEFTS)] * 2
    ins = [(lengths, "smem")]
    ins += [(value, "vmem") for value in (rows, gains, qkv_held, proj_held)]
    ins, aliases = with_earlier(ins, outs, earlier)
    scratch = [pltpu.VMEM((2, ROWS, D), BF16), pltpu.SemaphoreType.DMA((4,))]
    kernel = functools.partial(top_attend_kernel, len(aliases), item)
    return call(kernel, "top_attend", ins, outs, scratch, aliases)


def top_expand_kernel(n_alias, item, lengths, mixed, gain_ref, in_held, back_held, *rest):
    slope, keep_out, send_out, high, second_rows, active, sems = rest[n_alias:]
    place = Place(lengths)

    @pl.when(jnp.logical_not(place.is_lower))
    def _():
        sender = Sender(sems)
        expand_body(
            sender,
            place,
            item,
            False,
            mixed,
            gain_ref,
            (in_held, back_held),
            slope,
            (keep_out, send_out),
            second_rows,
            active,
            high,
        )
        sender.finish()


def top_expand(item, lengths, mixed, gains, in_held, back_held, earlier):
    outs = [
        ((ROWS, FF), BF16, "vmem"),
        ((MB * ROWS, KEPT), BF16, LEFTS),
        ((MB * ROWS, KEPT), BF16, LEFTS),
        ((ROWS, D), F32, "vmem"),
    ]
    ins = [(lengths, "smem")]
    ins += [(value, "vmem") for value in (mixed, gains, in_held, back_held)]
    ins, aliases = with_earlier(ins, outs, earlier)
    scratch = [
        pltpu.VMEM((ROWS, D), BF16),
        pltpu.VMEM((ROWS, FF), BF16),
        pltpu.SemaphoreType.DMA((4,)),
    ]
    kernel = functools.partial(top_expand_kernel, len(aliases), item)
    return call(kernel, "top_expand", ins, outs, scratch, aliases)


def top_expand_back_kernel(item, lengths, feeds, mixed, slope, gain_ref, in_held, back_held, *rest):
    target, gain_out, middle, inner, sems = rest
    place = Place(lengths)

    @pl.when(jnp.logical_not(place.is_lower))
    def _():
        sender = Sender(sems)
        expand_back_body(
            sender,
            place,
            item,
            False,
            feeds.at[pl.ds(item * ROWS, ROWS)],
            mixed,
            slope,
            gain_ref,
            (in_held, back_held),
            target,
            gain_out,
            middle,
            inner,
        )
        sender.finish()


def top_expand_back(item, lengths, feeds, mixed, slope, gains, in_held, back_held):
    outs = [grads_shapes(item)[0], ((1, D), F32, "vmem"), ((ROWS, D), F32, "vmem")]
    ins = [(lengths, "smem")]
    ins += [(value, "vmem") for value in (feeds, mixed, slope, gains, in_held, back_held)]
    scratch = [pltpu.VMEM((ROWS, FF), BF16), pltpu.SemaphoreType.DMA((1,))]
    kernel = functools.partial(top_expand_back_kernel, item)
    return call(kernel, "top_expand_back", ins, outs, scratch)


def top_attend_back_kernel(lengths, rows_ref, middle, qkv_rows, probs, gain_ref, *rest):
    weights, rest = rest[:2], rest[2:]
    *targets, gain_out, low, outer, sems = rest
    targets[-1] = targets[-1].at[pl.ds(0, ROWS)]
    place = Place(lengths)

    @pl.when(jnp.logical_not(place.is_lower))
    def _():
        sender = Sender(sems)
        low[...] = attend_back_body(
            sender, rows_ref, middle, qkv_rows, probs, gain_ref, weights, targets, gain_out, outer
        ).astype(BF16)
        sender.finish()


def top_attend_back(item, lengths, rows, middle, saved, gains, weights):
    outs = [*grads_shapes(item)[1:], ((1, D), F32, "vmem"), ((ROWS, D), BF16, "vmem")]
    ins = [(lengths, "smem")]
    ins += [(value, "vmem") for value in (rows, middle, *saved, gains, *weights)]
    scratch = [pltpu.VMEM((ROWS, 4 * D), BF16), pltpu.SemaphoreType.DMA((2,))]
    return call(top_attend_back_kernel, "top_attend_back", ins, outs, scratch)


def lower_expand_back_kernel(
    n_alias, item, lengths, grad_ref, mixed, slope, gain_ref, in_held, back_held, *rest
):
    target, gain_out, middle, inner, sems = rest[n_alias:]
    place = Place(lengths)

    @pl.when(place.is_lower)
    def _():
        sender = Sender(sems)
        expand_back_body(
            sender,
            place,
            item,
            True,
            grad_ref,
            mixed,
            slope,
            gain_ref,
            (in_held, back_held),
            target,
            gain_out,
            middle,
            inner,
        )
        sender.finish()


def lower_expand_back(item, lengths, grad, mixed, slope, gains, in_held, back_held, earlier):
    outs = [grads_shapes(item)[0], ((1, D), F32, "vmem"), ((ROWS, D), F32, "vmem")]
    ins = [(lengths, "smem")]
    ins += [(value, "vmem") for value in (grad, mixed, slope, gains, in_held, back_held)]
    ins, aliases = with_earlier(ins, outs, earlier)
    scratch = [pltpu.VMEM((ROWS, FF), BF16), pltpu.SemaphoreType.DMA((1,))]
    kernel = functools.partial(lower_expand_back_kernel, len(aliases), item)
    size = 1 << 16 if item < MB - 1 else 1
    return call(kernel, "lower_expand_back", ins, outs, scratch, aliases, size)


def lower_attend_back_kernel(n_alias, item, lengths, feeds, middle, qkv_rows, probs, gain_ref, *rest):
    weights, rest = rest[:2], rest[2:]
    tops, others, rest = rest[:MB], rest[MB : MB + 3], rest[MB + 3 + n_alias :]
    if item < MB - 1:
        grads, gain_out, ends_out, outer, high, sems = rest
        targets = [grads]
    else:
        first, last, gain_out, ends_out, gain_keep, outer, high, gain_rows, sems = rest
        targets = [first, last.at[pl.ds(0, ROWS)]]
    place = Place(lengths)
    rows = pl.ds(item * ROWS, ROWS)

    @pl.when(place.is_lower)
    def _():
        sender = Sender(sems)
        high[...] = attend_back_body(
            sender,
            feeds.at[rows],
            middle,
            qkv_rows,
            probs,
            gain_ref,
            weights,
            targets,
            gain_out,
            outer,
        )
        sender.send(high, ends_out.at[rows])
        sender.finish()

    if item == MB - 1:
        sender = Sender(sems)

        @pl.when(jnp.logical_not(place.is_lower))
        def _():
            top_sender = Sender(sems)
            for top_item, top_high in enumerate(tops):
                top_sender.send(top_high, ends_out.at[pl.ds(top_item * ROWS, ROWS)])
            top_sender.finish()

        own, other = places(place.pos, HALF)
        gain_rows[...] = jnp.zeros_like(gain_rows)
        for row, parts in enumerate(((others[0], gain_out), others[1:])):
            gain_keep[row : row + 1] = parts[0][:, own] + parts[1][:, own]
            gain_rows[row : row + 1, pl.ds(0, HALF)] = parts[0][:, other] + parts[1][:, other]
        outer[pl.ds(0, 16), pl.ds(0, 2 * D)] = gain_rows[...].astype(BF16)
        sender.send(outer.at[pl.ds(0, 16), pl.ds(0, 2 * D)], last.at[pl.ds(ROWS, 16)])
        sender.finish()


def lower_attend_back(item, lengths, feeds, middle, saved, gains, weights, tops, others, earlier):
    outs = [
        *grads_shapes(item)[1:],
        ((1, D), F32, "vmem"),
        ((MB * ROWS, D), F32, "any"),
    ]
    scratch = [pltpu.VMEM((ROWS, 4 * D), BF16), pltpu.VMEM((ROWS, D), F32)]
    if item == MB - 1:
        outs.append(((2, HALF), F32, "vmem"))
        scratch.append(pltpu.VMEM((16, 2 * D), F32))
    scratch.append(pltpu.SemaphoreType.DMA((3,)))
    ins = [(lengths, "smem")]
    ins += [(value, "vmem") for value in (feeds, middle, *saved, gains, *weights, *tops, *others)]
    ins, aliases = with_earlier(ins, outs, earlier)
    kernel = functools.partial(lower_attend_back_kernel, len(aliases), item)
    return call(kernel, "lower_attend_back", ins, outs, scratch, aliases)


def expert_rows(place, item, partner, expert, live_only=False):
    row = lax.broadcasted_iota(jnp.int32, (1, ROWS), 1)
    first, second = place.experts(item, partner)
    mine = jnp.where(row < IMAGE_ROWS, first, second) == expert
    if live_only:
        mine = mine & (row < place.live(item, partner))
    return mine


def bits_but(*taken):
    count = lax.axis_size("dp").bit_length() - 1
    return [bit for bit in reversed(range(count)) if bit not in taken]


def block_numbers(first_bit):
    here = (lax.axis_index("dp") >> first_bit) & 1
    rest = bits_but(first_bit)
    for number in range(1 << len(rest)):
        where = tuple((number >> (len(rest) - 1 - place)) & 1 for place in range(len(rest)))
        base = sum(value << bit for value, bit in zip(where, rest))
        yield where, base + (here << first_bit), base + ((1 - here) << first_bit)


def write_blocks(total, rows, first_bit, mine, theirs):
    for where, own, other in block_numbers(first_bit):
        own_at = pl.ds(pl.multiple_of(own * rows, rows), rows)
        other_at = pl.ds(pl.multiple_of(other * rows, rows), rows)
        mine[where] = total[own_at].astype(BF16)
        theirs[where] = total[other_at].astype(BF16)


def back_grads_kernel(orders, n_items, lengths, *refs):
    actives, grads, feeds = refs[:n_items], refs[n_items : 2 * n_items], refs[2 * n_items : 2 * n_items + 2]
    outs, (flipped, total) = refs[2 * n_items + 2 : -2], refs[-2:]
    place = Place(lengths)
    tail = ROWS - TAIL
    rows = D // lax.axis_size("dp")

    @pl.when(pl.program_id(0) == 0)
    def _():
        for index in range(n_items):
            item, partner = index % MB, index >= MB
            top = feeds[index // MB][pl.ds(item * ROWS, ROWS)]
            value = jnp.where(place.is_lower, grads[index][...], top).T
            for expert in (0, 1):
                mask = expert_rows(place, item, partner, expert, live_only=True)
                flipped[expert, :, pl.ds(index * ROWS, ROWS)] = jnp.where(mask, value, 0)

    def finished(expert):
        write_blocks(total, rows, orders[expert][0], outs[2 * expert], outs[2 * expert + 1])

    def whole(expert):
        result = None
        for index in range(n_items):
            term = dot_nn(flipped[expert, :, pl.ds(index * ROWS, ROWS)], actives[index][...])
            result = term if result is None else result + term
        total[...] = result

    whole(0)
    finished(0)

    @pl.when(place.is_lower)
    def _():
        left = [
            flipped[1, :, pl.ds(index * ROWS + ROWS // 2, ROWS // 2)] for index in range(n_items)
        ]
        right = [actives[index][pl.ds(ROWS // 2, ROWS // 2)] for index in range(n_items)]
        total[...] = dot_nn(jnp.concatenate(left, axis=1), jnp.concatenate(right, axis=0))

    @pl.when(jnp.logical_not(place.is_lower))
    def _():
        whole(1)

    finished(1)


def halves_shape(block):
    return jax.ShapeDtypeStruct((2,) * len(bits_but(0)) + block, BF16)


def halves_spec(block, place):
    lead = len(bits_but(0))
    return pl.BlockSpec((2,) * lead + block, lambda step: (0,) * lead + place(step))


def by_item(width, count, column, **options):
    return [
        pl.BlockSpec((ROWS, width), lambda step, item=index % MB: (item, column(step)), **options)
        for index in range(count)
    ]


def back_grads(lengths, kept, grads, feeds, orders):
    width = 256
    block = (D // lax.axis_size("dp"), width)
    once = pl.Buffered(1)
    fixed = [pl.BlockSpec((ROWS, D), lambda step: (0, 0), pipeline_mode=once)] * len(kept)
    fixed += [pl.BlockSpec((MB * ROWS, D), lambda step: (0, 0), pipeline_mode=once)] * 2
    results = pl.pallas_call(
        functools.partial(back_grads_kernel, orders, len(kept)),
        grid=(FF_HALF // width,),
        out_shape=[halves_shape((block[0], FF_HALF)) for _ in orders for _ in (0, 1)],
        in_specs=[pl.BlockSpec(memory_space=pltpu.SMEM)]
        + by_item(width, len(kept), lambda step: step)
        + fixed,
        out_specs=[
            halves_spec(block, lambda step: (0, step)) for _ in orders for _ in (0, 1)
        ],
        scratch_shapes=[
            pltpu.VMEM((2, D, len(kept) * ROWS), BF16),
            pltpu.VMEM((D, width), F32),
        ],
        compiler_params=pltpu.CompilerParams(vmem_limit_bytes=VMEM_BYTES),
        cost_estimate=cost(1),
        name="back_grads",
    )(lengths, *kept, *grads, *feeds)
    return [tuple(results[2 * expert : 2 * expert + 2]) for expert in (0, 1)]


def in_grads_kernel(width, n_items, lengths, *refs):
    seconds, inners = refs[:n_items], refs[n_items : 2 * n_items]
    outs, (flipped, total) = refs[2 * n_items : -2], refs[-2:]
    place = Place(lengths)
    half = ROWS // 2
    low_bit = lax.axis_index("dp") % 2

    @pl.when(pl.program_id(0) == 0)
    def _():
        for index in range(n_items):
            item, partner = index % MB, index >= MB
            value = seconds[index][...].T
            for expert in (0, 1):
                mask = expert_rows(place, item, partner, expert)
                flipped[expert, :, pl.ds(index * ROWS, ROWS)] = jnp.where(mask, value, 0)

    def whole(expert):
        result = None
        for index in range(n_items):
            term = dot_nn(flipped[expert, :, pl.ds(index * ROWS, ROWS)], inners[index][...])
            result = term if result is None else result + term
        total[...] = result

    def finished(expert):
        if len(outs) == 2:
            outs[expert][0] = total[...].astype(BF16)
            return
        for out, bit in zip(outs[2 * expert : 2 * expert + 2], (low_bit, 1 - low_bit)):
            out[0] = total[:, pl.ds(pl.multiple_of(bit * width, width), width)].astype(BF16)

    whole(0)
    finished(0)

    @pl.when(place.is_lower)
    def _():
        left = [flipped[1, :, pl.ds(index * ROWS + half, half)] for index in range(n_items)]
        right = [inners[index][pl.ds(half, half)] for index in range(n_items)]
        total[...] = dot_nn(jnp.concatenate(left, axis=1), jnp.concatenate(right, axis=0))

    @pl.when(jnp.logical_not(place.is_lower))
    def _():
        whole(1)

    finished(1)


def in_grads(lengths, kept, inners):
    size = lax.axis_size("dp")
    width = FF // size
    aligned = width % 128 == 0
    columns = 2 * width if aligned else D
    steps = FF // columns
    once = pl.Buffered(1)
    block = (1, HALF, width if aligned else columns)
    count = 4 if aligned else 2
    results = pl.pallas_call(
        functools.partial(in_grads_kernel, width, len(kept)),
        grid=(steps,),
        out_shape=[jax.ShapeDtypeStruct((steps,) + block[1:], BF16)] * count,
        in_specs=[pl.BlockSpec(memory_space=pltpu.SMEM)]
        + by_item(HALF, len(kept), lambda step: FF_HALF // HALF, pipeline_mode=once)
        + [pl.BlockSpec((ROWS, columns), lambda step: (0, step))] * len(inners),
        out_specs=[pl.BlockSpec(block, lambda step: (step, 0, 0))] * count,
        scratch_shapes=[
            pltpu.VMEM((2, HALF, len(kept) * ROWS), BF16),
            pltpu.VMEM((HALF, columns), F32),
        ],
        compiler_params=pltpu.CompilerParams(vmem_limit_bytes=VMEM_BYTES),
        cost_estimate=cost(1),
        name="in_grads",
    )(lengths, *kept, *inners)
    if not aligned:
        whole = [part.transpose(1, 0, 2).reshape(HALF, size, width) for part in results]
        return [by_lowest_bit(part.transpose(1, 0, 2)) for part in whole]
    shape = (2,) * len(bits_but(0)) + block[1:]
    return [tuple(part.reshape(shape) for part in results[2 * e : 2 * e + 2]) for e in (0, 1)]


def outer_grads_kernel(order, *refs):
    lefts, outers, gains, pieces, total = refs[:4], refs[4:10], refs[10:12], refs[12:16], refs[16]
    step = pl.program_id(0)
    result = None
    for index in range(4):
        outer = outers[3 * (index // MB)][...]
        if index % MB == MB - 1:
            first, second = outers[3 * (index // MB) + 1 : 3 * (index // MB) + 3]
            outer = jnp.where(step < 2, first[...], second[...])
        term = dot_tn(outer, lefts[index][...])
        result = term if result is None else result + term
    total[pl.ds(pl.multiple_of(step * D, D), D)] = result

    @pl.when(step == 3)
    def _():
        size = lax.axis_size("dp")
        proj_rows = D // size
        gain_rows = gains[0][...] + gains[1][pl.ds(0, 2), pl.ds(0, HALF)].astype(F32)
        gain_rows = jnp.concatenate([gain_rows, jnp.zeros((14, HALF), F32)], axis=0)
        for where, *numbers in block_numbers(order[0]):
            for target, number in zip((0, 1), numbers):
                at = pl.multiple_of(number * 3 * proj_rows, proj_rows)
                below = pl.multiple_of(3 * D + number * proj_rows, proj_rows)
                first, second = pieces[target], pieces[2 + target]
                first[where] = total[pl.ds(at, 2 * proj_rows)].astype(BF16)
                second[where + (pl.ds(0, proj_rows),)] = total[
                    pl.ds(at + 2 * proj_rows, proj_rows)
                ].astype(BF16)
                second[where + (pl.ds(proj_rows, proj_rows),)] = total[
                    pl.ds(below, proj_rows)
                ].astype(BF16)
                turned = pltpu.roll(gain_rows, HALF - number * (HALF // size), 1)
                second[where + (pl.ds(2 * proj_rows, 16),)] = turned.astype(BF16)


def outer_grads(kept, outers, gains, order):
    block = (2 * D // lax.axis_size("dp"), HALF)
    last = (block[0] + 16, HALF)
    results = pl.pallas_call(
        functools.partial(outer_grads_kernel, order),
        grid=(4,),
        out_shape=[halves_shape(block)] * 2 + [halves_shape(last)] * 2,
        in_specs=by_item(HALF, 4, lambda step: FF_HALF // HALF + 1 + step // 3)
        + [
            pl.BlockSpec((ROWS, D), lambda step: (0, step)),
            pl.BlockSpec((ROWS, D), lambda step: (0, jnp.minimum(step, 1))),
            pl.BlockSpec((ROWS, D), lambda step: (0, jnp.maximum(step - 2, 0))),
        ]
        * 2
        + [
            pl.BlockSpec((2, HALF), lambda step: (0, 0)),
            pl.BlockSpec((16, D), lambda step: (ROWS // 16, 0)),
        ],
        out_specs=[halves_spec(block, lambda step: (0, 0))] * 2
        + [halves_spec(last, lambda step: (0, 0))] * 2,
        scratch_shapes=[pltpu.VMEM((4 * D, HALF), F32)],
        compiler_params=pltpu.CompilerParams(vmem_limit_bytes=2 * VMEM_BYTES),
        cost_estimate=cost(1),
        name="outer_grads",
    )(*kept, *outers, *gains)
    return tuple(results[:2]), tuple(results[2:])


def swapped(block, axis, bit, among=None):
    among = range(lax.axis_size(axis)) if among is None else among
    return lax.ppermute(block, axis, [(place, place ^ 1 << bit) for place in among])


def per_item(arrays):
    return [array for array in arrays for _ in range(MB)]


def passed_along(value, steps):
    count = lax.axis_size("section")
    first, last = (max(0, -steps), min(count, count - steps))
    route = [(source, source + steps) for source in range(first, last)]
    return lax.ppermute(value, "section", route)


def split_bit(stacked, bit):
    here = (lax.axis_index("dp") >> bit) & 1
    mine = lax.dynamic_index_in_dim(stacked, here, 0, keepdims=False)
    theirs = lax.dynamic_index_in_dim(stacked, 1 - here, 0, keepdims=False)
    return mine, theirs


def added_kernel(left, right, out):
    out[...] = left[...].astype(F32) + right[...].astype(F32)


def added(left, right):
    ins = [(left, "vmem"), (right, "vmem")]
    return call(added_kernel, "added", ins, [(left.shape, F32, "vmem")], [])[0]


def outer_sums_kernel(first, left, right, qkv_out, proj_out, gain_out):
    rows = proj_out.shape[0]
    second = left[...].astype(F32) + right[...].astype(F32)
    qkv_out[: 2 * rows] = first[...]
    qkv_out[2 * rows :] = second[:rows]
    proj_out[...] = second[rows : 2 * rows]
    gain_out[...] = second[2 * rows : 2 * rows + 2, : gain_out.shape[1]]


def outer_sums(first, left, right):
    rows = first.shape[0] // 2
    ins = [(value, "vmem") for value in (first, left, right)]
    shapes = [(3 * rows, HALF), (rows, HALF), (2, rows // 2)]
    outs = [(shape, F32, "auto") for shape in shapes]
    return call(outer_sums_kernel, "outer_sums", ins, outs, [])


def added_halves_kernel(axis, bit, left, right, mine, theirs):
    here = (lax.axis_index("dp") >> bit) & 1
    lead = (slice(None),) * axis
    for out, at in ((mine, lead + (here,)), (theirs, lead + (1 - here,))):
        out[...] = (left[at].astype(F32) + right[at].astype(F32)).astype(BF16)


def added_halves(left, right, axis, bit):
    ins = [(left, "vmem"), (right, "vmem")]
    outs = [(left.shape[:axis] + left.shape[axis + 1 :], BF16, "vmem")] * 2
    kernel = functools.partial(added_halves_kernel, axis, bit)
    return call(kernel, "added_halves", ins, outs, [])


def after(value, *earlier):
    return lax.optimization_barrier((value, earlier))[0]


class Sums:
    def __init__(self):
        self.open = {}
        self.results = {}
        self.last = []

    def begin(self, name, piece, order, taken=()):
        mine, theirs = piece
        self.open[name] = (mine, swapped(theirs, "dp", order[0]), order[1:], (*taken, order[0]))

    def step(self, name, hold=False):
        mine, got, rest, taken = self.open.pop(name)
        mine = after(mine, *self.last)
        if len(rest) == 0:
            self.results[name] = added(mine, got)
            self.last = [self.results[name]]
            return
        mine, theirs = added_halves(mine, got, bits_but(*taken).index(rest[0]), rest[0])
        self.last = [theirs]
        if hold:
            return (mine, theirs), rest, taken
        self.begin(name, (mine, theirs), rest, taken)

    def finish(self, but):
        while len(self.open) > 1 or len(self.open[but][2]) > 0:
            for name in list(self.open):
                if name != but or len(self.open[name][2]) > 0:
                    self.step(name)
        mine, got, *_ = self.open.pop(but)
        return after(mine, *self.last), got


def by_lowest_bit(stacked):
    bits = lax.axis_size("dp").bit_length() - 1
    split = jnp.moveaxis(stacked.reshape((2,) * bits + stacked.shape[1:]), bits - 1, 0)
    return split_bit(split, 0)


def shards(feeds, text_lengths, norm_gains, qkv_weight, out_weight, expert_in, expert_out):
    n_dp = lax.axis_size("dp")
    bits = n_dp.bit_length() - 1
    pos = lax.axis_index("section") % 2

    gains_other = swapped(norm_gains[0], "section", 0)
    gains = joined_gains(norm_gains[0], gains_other)
    own = [qkv_weight[0], out_weight[0]]
    other = [swapped(part, "section", 0) for part in own]
    held = joined_halves(own, other)
    in_other = swapped(after(expert_in[0], gains_other, *other), "section", 0)
    back_other = swapped(after(expert_out[0], gains_other, *other), "section", 0)

    *saved, keep, send = lower_attend(text_lengths, feeds, gains, *held)
    saved = [saved[3 * item : 3 * item + 3] for item in range(MB)]
    earlier = saved[-1][2]
    held += joined_halves([expert_in[0]], [after(in_other, earlier)])
    held += joined_halves([expert_out[0]], [after(back_other, earlier)])
    slopes, passed = [], []
    for item in range(MB):
        mixed = after(saved[item][2], earlier)
        slope, keep, send, earlier = lower_expand(
            item, text_lengths, mixed, gains, *held[2:], {1: keep, 2: send}
        )
        slopes.append(slope)
        passed.append(passed_along(earlier, 2))
    grads, gain_grads, ups = [], [], []
    tops = []
    for item in range(MB):
        rows = after(passed[item], earlier)
        places = dict(enumerate(saved[item])) | {3: keep, 4: send}
        *saved[item], keep, send = top_attend(
            item, text_lengths, rows, gains, *held[:2], places
        )
        mixed = saved[item][2]
        places = {0: slopes[item], 1: keep, 2: send}
        slopes[item], keep, send, top = top_expand(
            item, text_lengths, mixed, gains, *held[2:], places
        )
        tops.append(top)
        inner, gain_second, middle = top_expand_back(
            item, text_lengths, feeds, mixed, slopes[item], gains, *held[2:]
        )
        *outer, gain_first, earlier = top_attend_back(
            item,
            text_lengths,
            rows,
            middle,
            saved[item][:2],
            gains,
            held[:2],
        )
        grads.append([inner, *outer])
        gain_grads.append([gain_first, gain_second])
        ups.append(passed_along(earlier, -2))
    feeds_pair = [feeds, swapped(after(feeds, earlier), "section", 0, (2, 3))]
    lefts = per_item([keep, swapped(after(send, earlier), "section", 0)])

    upward = tuple(range(bits))
    back_orders = [upward[1:] + upward[:1], upward]

    def lower_back_experts(item, up):
        results = {0: grads[item][0], 1: gain_grads[item][1]}
        grads[item][0], gain_grads[item][1], middle = lower_expand_back(
            item, text_lengths, up, saved[item][2], slopes[item], gains, *held[2:], results
        )
        return middle

    def lower_back_heads(item, middle, ends, others):
        parts = [*grads[item][1:], gain_grads[item][0], *ends]
        results = lower_attend_back(
            item,
            text_lengths,
            feeds,
            middle,
            saved[item][:2],
            gains,
            held[:2],
            tops,
            others,
            dict(enumerate(parts)),
        )
        count = len(grads[item]) - 1
        grads[item][1:], gain_grads[item][0] = results[:count], results[count]
        return results[count + 1 :]

    ups[0] = after(ups[0], earlier)
    ups_other = [swapped(ups[0], "section", 0, (0, 1))]
    middle = lower_back_experts(0, ups[0])
    (ends,) = lower_back_heads(0, middle, [], [gain_grads[0][1]] * 3)
    first_grads = [(part, swapped(part, "section", 0)) for part in grads[0]]
    ups[1] = after(ups[1], ends)
    ups_other.append(swapped(ups[1], "section", 0, (0, 1)))
    middle = lower_back_experts(1, after(ups[1], ups_other[0]))
    inner = grads[1][0]
    inners = [first_grads[0][0], inner, first_grads[0][1], swapped(inner, "section", 0)]
    ups_other[1] = after(ups_other[1], middle)
    back_pieces = back_grads(text_lengths, lefts, ups + ups_other, feeds_pair, back_orders)
    inners[1] = after(inners[1], back_pieces[0][1], back_pieces[1][1])
    in_pieces = in_grads(text_lengths, lefts, inners)

    sums = Sums()
    for number in (0, 1):
        sums.begin(f"back{number}", back_pieces[number], back_orders[number])
    sums.begin("in0", in_pieces[0], upward)
    middle = after(middle, in_pieces[0][1], in_pieces[1][1])
    others = [gain_grads[0][0], gain_grads[0][1], gain_grads[1][1]]
    ends, gain_keep = lower_back_heads(1, middle, [ends], others)
    outers = [first_grads[1][0], *grads[1][1:], first_grads[1][1]]
    outers += [swapped(part, "section", 0) for part in grads[1][1:]]
    sums.last = [ends]
    sums.step("back0")
    sums.step("back1")
    gain_keep = after(gain_keep, *sums.last)
    outer_pieces = outer_grads(lefts, outers, (gain_keep, outers[-1]), upward)
    sums.last = [piece[1] for piece in outer_pieces]

    def later(piece):
        return piece[0], after(piece[1], *sums.last)

    sums.begin("in1", later(in_pieces[1]), upward)
    sums.begin("outer0", later(outer_pieces[0]), upward)
    for name in ("back1", "back0", "in0", "in0", "in1", "back1"):
        sums.step(name)
    sums.begin("outer1", later(outer_pieces[1]), upward)
    order = ("outer0", "in1", "in0", "outer1", "outer0", "in1", "outer1", "outer0", "back0")
    for name in order:
        sums.step(name)
    last = sums.finish("outer1")
    qkv_sum, proj_sum, gain_sum = outer_sums(sums.results["outer0"], *last)
    done = sums.results
    return (
        ends,
        gain_sum[None],
        qkv_sum.T[None],
        proj_sum.T[None],
        jnp.stack([done["in0"], done["in1"]])[None],
        jnp.stack([done["back0"].T, done["back1"].T])[None],
    )


def solution(mesh):
    return jax.shard_map(
        shards,
        mesh=mesh,
        in_specs=(
            P(("dp", "section"), None),
            P("dp"),
            P("section", None, None),
            P("section", None, None),
            P("section", None, None),
            P("section", None, None, None),
            P("section", None, None, None),
        ),
        out_specs=(
            P(("dp", "section"), None),
            P("section", None, "dp"),
            P("section", None, "dp"),
            P("section", None, "dp"),
            P("section", None, None, "dp"),
            P("section", None, None, "dp"),
        ),
        check_vma=False,
    )
```
